256 devices in a mesh: ctx: 16 (over z, core), exp: 16 (over y, x).
Axes of the slice: x: 4, y: 4, z: 8, core: 2. Of those that a mesh axis runs over, the one named last changes fastest.
Arguments:
- cache: bfloat16 [96, 6144, 576], P('exp', 'ctx'), may hold values from -6 to 6
- idx_keys: bfloat16 [96, 6144, 128], P('exp', 'ctx'), may hold values from -6 to 6
- lat_query: bfloat16 [96, 128, 576], P('exp'), may hold values from -240 to 240
- idx_query: bfloat16 [96, 64, 128], P('exp'), may hold values from -6 to 6
- idx_weight: float32 [96, 64], P('exp'), may hold values from -6 to 6
- chosen_blocks: int32 [96, 32], P('exp'), may hold values from 0 to 95, as said below
- w_uv: bfloat16 [128, 512, 128], P('ctx'), may hold values from -2.390625 to 2.390625
- w_o: bfloat16 [16384, 7168], P('ctx', 'exp'), may hold values from -0.046875 to 0.046875
- hidden_in: bfloat16 [96, 7168], P(None, 'exp'), may hold values from -6 to 6
- norm_gain: float32 [7168], P('exp'), may hold values from 0.5 to 1.5
- route: int32 [96, 4], replicated, may hold values from 0 to 15, all different within a row; in each aligned block of 96 rows (0 to 95, 96 to 191, ...) at most 48 rows name the same one
- route_weight: float32 [96, 4], replicated, may hold values from 0.2 to 1
- w_in: bfloat16 [16, 7168, 4096], P('ctx', 'exp'), may hold values from -0.0625 to 0.0625
- w_down: bfloat16 [16, 2048, 7168], P('ctx', None, 'exp'), may hold values from -0.125 to 0.125
Outputs:
- index_scores: float32 [96, 6144], P('exp', 'ctx')
- layer_out: bfloat16 [96, 7168], P('ctx', 'exp')
The draws below stay inside these ranges and needn't reach their ends.
Inputs may be any that keep to these rules, and one draw needn't show every extreme that they name: `chosen_blocks`: each row names 32 different blocks. `route`: each row names 4 different experts; no expert is named by more than 48 rows, a bound that some block reaches.
All inputs are finite; a program needn't handle non-finite values.
Results may differ from the reference program's by a relative error of at most 0.029.
Values may be sent and summed in bfloat16 or wider, within the bound.
No kernel may reach another device: no remote copies, remote signals or barrier semaphores. Data moves between devices by JAX's collectives and lax.ppermute only.
A program may use at most 128 MiB of HBM per device.

```python
import math
import jax
import jax.numpy as jnp
import numpy as np
from jax import lax

D = 7168
D_LAT = 512
D_ROPE = 64
V_HEAD = 128
HEADS = 128
IDX_HEADS = 64
IDX_DIM = 128
FF = 2048
BLOCK = 64
SEL = 32
TOP = 4
SHARD_TOK = 384
ROWS = 96
SEQ = 6144
BLOCKS = 96
EXPERTS = 16
CAP = 48
N_CTX = 16


def planted(key):
    key = jax.random.fold_in(key, 101)
    sel_key = jax.random.fold_in(key, 0)
    block_iota = jnp.arange(BLOCKS, dtype=jnp.int32)
    ranking = jax.random.randint(sel_key, (ROWS, BLOCKS), 0, 1 << 16, jnp.int32) * BLOCKS + block_iota[None, :]
    row_iota = jnp.arange(ROWS, dtype=jnp.int32)
    forced = (row_iota[:, None] == 0) & ((block_iota[None, :] == 0) | (block_iota[None, :] == BLOCKS - 1))
    ranking = ranking + jnp.where(forced, 1 << 26, 0).astype(jnp.int32)
    chosen = lax.top_k(ranking, SEL)[1].astype(jnp.int32)
    return chosen


def draw_chosen_blocks(key, part):
    chosen = planted(key)
    return chosen


def draw_cache(key, part):
    key = jax.random.fold_in(key, 7)
    base = jax.random.normal(key, (ROWS, SEQ, D_LAT + D_ROPE), jnp.float32)
    base = jnp.clip(base, -6.0, 6.0)
    return base.astype(jnp.bfloat16)


def draw_lat_query(key, part):
    key = jax.random.fold_in(key, 11)
    base_key = jax.random.fold_in(key, 0)
    base = jax.random.normal(base_key, (ROWS, HEADS, D_LAT + D_ROPE), jnp.float32)
    base = jnp.clip(base, -6.0, 6.0)
    return base.astype(jnp.bfloat16)


def level_of(own_key, shape, pieces, low, largest):
    loudness = 1.0
    for dim, parts in pieces:
        draws = jax.random.uniform(jax.random.fold_in(jax.random.fold_in(own_key, 6), dim), (parts,), jnp.float32, low / len(pieces), largest / len(pieces))
        loudness = loudness * jnp.repeat(jnp.exp(draws), shape[dim] // parts).reshape((-1,) + (1,) * (len(shape) - 1 - dim))
    return loudness


def routed_block(stream_key, own, number, rows, amount, top, most, lean):
    sequence = jax.random.permutation(stream_key, amount)
    heavy_load, usual = load_shares(amount, rows * top, most, lean, True), load_shares(amount, rows * top, most, lean, False)
    places = jnp.arange(amount)

    def named(sizes, turn):
        used = int((sizes > 0).sum())
        fixed = max(1, used // 4)
        moved = fixed + (places - fixed + turn * (used - fixed)) % max(1, amount - fixed)
        return jnp.zeros((amount,), jnp.int32).at[sequence[jnp.where(places < fixed, places, moved)]].set(jnp.asarray(sizes, jnp.int32))

    sizes = jnp.where(number % 4 == 0, named(heavy_load, number // 4), named(usual, number - number // 4 - 1))
    mixed = jax.random.permutation(jax.random.fold_in(own, 3), amount)
    source_of, receiver = mixed[0:amount // 2 * 2:2], mixed[1:amount // 2 * 2:2]
    slack = jnp.minimum(sizes[source_of] - 1, most - sizes[receiver]) // 2
    slack = jnp.where((source_of == sequence[0]) | (receiver == sequence[0]) | (sizes[receiver] == 0), 0, jnp.maximum(slack, 0))
    moved = jax.random.randint(jax.random.fold_in(own, 4), (amount // 2,), 0, 1 << 20) % (slack + 1)
    sizes = sizes.at[source_of].add(-moved).at[receiver].add(moved)
    members = jnp.searchsorted(jnp.cumsum(sizes), jnp.arange(rows * top), side="right").astype(jnp.int32)
    listing = members.reshape(top, rows).T
    listing = listing[jax.random.permutation(jax.random.fold_in(own, 1), rows)]
    turn = jax.random.randint(jax.random.fold_in(own, 2), (rows, 1), 0, top)
    return jnp.take_along_axis(listing, (jnp.arange(top)[None, :] + turn) % top, axis=1)


def load_shares(amount, total, reach, skew, full):
    loads = [(1 << 20) // math.isqrt(grade ** skew) + 1 for grade in range(1, amount + 1)]
    largest = reach if full else min(reach, max(-(-total // amount), total * loads[0] // sum(loads)))
    least = 1 if total - largest >= amount - 1 else 0
    holding, spare = [largest] + [least] * (amount - 1), total - largest - least * (amount - 1)
    while spare > 0:
        free = [i for i in range(1, amount) if holding[i] < largest] or [i for i in range(1, amount) if holding[i] < reach]
        pool, remaining = sum([loads[i] for i in free]), spare
        for i in free:
            addition = min(reach - holding[i], max(1, remaining * loads[i] // pool), spare)
            holding[i] = holding[i] + addition
            spare = spare - addition
    return np.array(holding)


def bell_draw(key, shape, scale, limit, cuts=(), kind=jnp.bfloat16):
    array = scale * jax.random.normal(key, shape, jnp.float32)
    if cuts:
        array = array * level_of(key, shape, cuts, -0.22, 0.18)
    return jnp.clip(array, -limit, limit).astype(kind)


def setup_inputs(seed: int = 0) -> dict:
    streams_of = jax.random.split(jax.random.key(seed), 15)
    cache = draw_cache(jax.random.fold_in(streams_of[14], 71), 0)
    idx_keys = bell_draw(streams_of[1], (ROWS, SEQ, IDX_DIM), 1.0, 6.0, ((0, 16), (1, 16)))
    lat_query = draw_lat_query(jax.random.fold_in(streams_of[14], 71), 0)
    idx_query = bell_draw(streams_of[3], (ROWS, IDX_HEADS, IDX_DIM), 1.0, 6.0, ((0, 16),))
    idx_weight = bell_draw(streams_of[4], (ROWS, IDX_HEADS), 1.0, 6.0, ((0, 16),), jnp.float32)
    chosen_blocks = draw_chosen_blocks(jax.random.fold_in(streams_of[14], 71), 0)
    w_uv = bell_draw(streams_of[6], (HEADS, D_LAT, V_HEAD), 0.4, 2.390625, ((0, 16),))
    w_o = bell_draw(streams_of[7], (HEADS * V_HEAD, D), (HEADS * V_HEAD) ** -0.5, 0.046875, ((0, 16), (1, 16)))
    hidden_in = bell_draw(streams_of[8], (ROWS, D), 1.0, 6.0, ((1, 16),))
    norm_gain = jnp.clip(1.0 + 0.1 * jax.random.normal(streams_of[9], (D,), jnp.float32), 0.5, 1.5)
    route_keys = jax.random.split(jax.random.fold_in(streams_of[10], 1), ROWS // ROWS)
    route_turns = jax.random.permutation(jax.random.fold_in(streams_of[10], 3), ROWS // ROWS)
    route = jax.vmap(lambda own, number: routed_block(jax.random.fold_in(streams_of[10], 2), own, number, ROWS, EXPERTS, TOP, CAP, 2))(route_keys, route_turns).reshape((ROWS, TOP))
    route_weight = jnp.clip(jax.random.uniform(streams_of[11], (ROWS, TOP), jnp.float32, 0.2, 1.0), 0.2, 1.0)
    w_in = bell_draw(streams_of[12], (EXPERTS, D, 2 * FF), D ** -0.5, 0.0625, ((0, 16), (1, 16)))
    w_down = bell_draw(streams_of[13], (EXPERTS, FF, D), FF ** -0.5, 0.125, ((0, 16), (2, 16)))
    return {"cache": cache, "idx_keys": idx_keys, "lat_query": lat_query, "idx_query": idx_query, "idx_weight": idx_weight, "chosen_blocks": chosen_blocks, "w_uv": w_uv, "w_o": w_o, "hidden_in": hidden_in, "norm_gain": norm_gain, "route": route, "route_weight": route_weight, "w_in": w_in, "w_down": w_down}


neg_big = -1e+30
score_scale = 192.0 ** (-0.5)
eps = 1e-06

def reference(cache, idx_keys, lat_query, idx_query, idx_weight, chosen_blocks, w_uv, w_o, hidden_in, norm_gain, route, route_weight, w_in, w_down):
    rows_all = cache.shape[0]
    block_ids = jnp.arange(SEQ, dtype=jnp.int32) // BLOCK

    def one_row(items):
        row_cache, row_keys, row_query, row_iq, row_iw, row_sel = items
        raw = jnp.dot(row_iq, row_keys.T, preferred_element_type=jnp.float32) * IDX_DIM ** (-0.5)
        index_row = jnp.dot(row_iw, jnp.maximum(raw, 0.0), precision=lax.Precision.HIGHEST)
        chosen = jnp.any(block_ids[:, None] == row_sel[None, :], axis=-1)
        scores = jnp.dot(row_query, row_cache.T, preferred_element_type=jnp.float32) * score_scale
        chosen_seg = chosen.reshape(N_CTX, SHARD_TOK)[None]
        masked = jnp.where(chosen[None, :], scores, neg_big).reshape(HEADS, N_CTX, SHARD_TOK)
        peak_seg = lax.optimization_barrier(jnp.max(masked, axis=-1))
        expo = jnp.where(chosen_seg, jnp.exp(masked - peak_seg[..., None]), 0.0)
        total_seg = lax.optimization_barrier(jnp.sum(expo, axis=-1))
        latent = row_cache[:, :D_LAT].reshape(N_CTX, SHARD_TOK, D_LAT).astype(jnp.float32)
        weighted = jnp.einsum('hnt,ntd->hnd', expo.astype(jnp.bfloat16).astype(jnp.float32), latent, precision=lax.Precision.HIGHEST)
        peak = lax.optimization_barrier(jnp.max(peak_seg, axis=1))
        factor = jnp.exp(peak_seg - peak[:, None])
        summed = lax.optimization_barrier(jnp.sum(weighted * factor[..., None], axis=1))
        total = lax.optimization_barrier(jnp.sum(total_seg * factor, axis=1))
        return (index_row, (summed / total[:, None]).astype(jnp.bfloat16))
    index_scores, attn_lat = lax.map(one_row, (cache, idx_keys, lat_query, idx_query, idx_weight, chosen_blocks))
    values = jnp.einsum('rhd,hdv->rhv', attn_lat.astype(jnp.float32), w_uv.astype(jnp.float32), precision=lax.Precision.HIGHEST)
    values = values.astype(jnp.bfloat16).reshape(rows_all, HEADS * V_HEAD)
    attn_out = jnp.dot(values, w_o, preferred_element_type=jnp.float32)
    resid = (hidden_in.astype(jnp.float32) + attn_out).astype(jnp.bfloat16)
    resid32 = lax.optimization_barrier(resid).astype(jnp.float32)
    scaled = (resid32 * norm_gain[None, :]).astype(jnp.bfloat16)
    inv_rms = lax.rsqrt(lax.optimization_barrier(jnp.sum(resid32 * resid32, axis=1)) / D + eps)

    def one_expert(carry, expert):
        gate_up = jnp.dot(scaled, w_in[expert], preferred_element_type=jnp.float32) * inv_rms[:, None]
        act = (jax.nn.silu(gate_up[:, :FF]) * gate_up[:, FF:]).astype(jnp.bfloat16)
        out_rows = jnp.dot(act, w_down[expert], preferred_element_type=jnp.float32)
        weight = lax.optimization_barrier(jnp.sum(jnp.where(route == expert, route_weight, 0.0), axis=1))
        return (carry + weight[:, None] * out_rows, None)
    moe, _ = lax.scan(one_expert, jnp.zeros((rows_all, D), jnp.float32), jnp.arange(EXPERTS, dtype=jnp.int32))
    layer_out = (resid32 + moe).astype(jnp.bfloat16)
    return (index_scores, layer_out)
```

```python
import functools

import jax
import jax.numpy as jnp
from jax import lax
from jax.experimental import pallas as pl
from jax.experimental.pallas import tpu as pltpu
from jax.sharding import PartitionSpec as P

f32 = jnp.float32
bf16 = jnp.bfloat16
D = 7168
BLOCK = 64
LAT = 512
WIDE = 640
CAP = 48
NEG = -1e30
SCORE_SCALE = 192.0 ** (-0.5)
EPS = 1e-06
HIGH = lax.Precision.HIGHEST
MB = 1 << 20

VMEM = pl.BlockSpec(memory_space=pltpu.VMEM)
SMEM = pl.BlockSpec(memory_space=pltpu.SMEM)


def params(mb=32):
    return pltpu.CompilerParams(vmem_limit_bytes=mb * MB)


def iota(shape, dim):
    return lax.broadcasted_iota(jnp.int32, shape, dim)


def dot(a, b, dims=((1,), (0,)), precision=None):
    return lax.dot_general(a, b, (dims, ((), ())), precision=precision, preferred_element_type=f32)


def split3(x):
    hi = x.astype(bf16).astype(f32)
    mid = (x - hi).astype(bf16).astype(f32)
    low = (x - hi - mid).astype(bf16).astype(f32)
    return hi, mid, low


def stats_tile(peak, total):
    lane = iota(peak.shape[:-1] + (128,), len(peak.shape) - 1)
    tile = jnp.zeros(peak.shape[:-1] + (128,), f32)
    for place, part in enumerate(split3(peak) + split3(total)):
        tile = jnp.where(lane == place, part, tile)
    return tile


def read_stats(x):
    tile = x[..., LAT:WIDE]
    lane = iota(tile.shape, len(tile.shape) - 1)
    peak = jnp.sum(jnp.where(lane < 3, tile, 0.0), axis=-1, keepdims=True)
    total = jnp.sum(jnp.where((lane >= 3) & (lane < 6), tile, 0.0), axis=-1, keepdims=True)
    return peak, total


def attention_kernel(ctx_ref, blocks_ref, query_ref, cache_ref, mine_ref, other_ref, mask_ref):
    step = pl.program_id(0)
    ctx = ctx_ref[0]
    core = lax.rem(ctx, 2)
    tokens = cache_ref.shape[1]
    per = tokens // BLOCK

    @pl.when(step == 0)
    def _():
        rows = blocks_ref.shape[0]
        block_of = iota((rows, tokens), 1) // BLOCK
        mask = jnp.zeros((rows, tokens), f32)
        picked = blocks_ref[...]
        for b in range(per):
            hit = jnp.max(jnp.where(picked == ctx * per + b, 1.0, 0.0), axis=1, keepdims=True)
            mask = jnp.where(block_of == b, hit, mask)
        mask_ref[...] = mask

    mine, other = [], []
    for i in range(2):
        chosen = mask_ref[pl.ds(step * 2 + i, 1), :] > 0.0
        keys = cache_ref[i]
        scores = dot(query_ref[i], keys, ((1,), (1,))) * SCORE_SCALE
        masked = jnp.where(chosen, scores, NEG)
        peak = jnp.max(masked, axis=1, keepdims=True)
        expo = jnp.where(chosen, jnp.exp(masked - peak), 0.0)
        total = jnp.sum(expo, axis=1, keepdims=True)
        weighted = dot(expo.astype(bf16), keys[:, :LAT])
        wide = jnp.concatenate([weighted, stats_tile(peak, total)], axis=1)
        wide = wide.reshape(8, 2, 8, WIDE)
        mine.append(jnp.where(core == 0, wide[:, 0], wide[:, 1]))
        other.append(jnp.where(core == 0, wide[:, 1], wide[:, 0]))
    mine_ref[...] = jnp.concatenate(mine, axis=1)
    other_ref[...] = jnp.concatenate(other, axis=1).astype(bf16)


def attention(ctx, blocks, query, cache):
    rows, heads, width = query.shape
    tokens = cache.shape[1]
    return pl.pallas_call(
        attention_kernel,
        grid=(rows // 2,),
        in_specs=[
            SMEM,
            pl.BlockSpec((rows, blocks.shape[1]), lambda i: (0, 0)),
            pl.BlockSpec((2, heads, width), lambda i: (i, 0, 0)),
            pl.BlockSpec((2, tokens, width), lambda i: (i, 0, 0)),
        ],
        out_specs=[pl.BlockSpec((8, 16, WIDE), lambda i: (0, i, 0))] * 2,
        out_shape=[
            jax.ShapeDtypeStruct((8, rows * 8, WIDE), f32),
            jax.ShapeDtypeStruct((8, rows * 8, WIDE), bf16),
        ],
        scratch_shapes=[pltpu.VMEM((rows, tokens), f32)],
        compiler_params=params(),
        name="attention",
    )(ctx, blocks, query, cache)


def side_kernel(ctx_ref, route_ref, gate_ref, iq_ref, iw_ref, keys_ref, score_ref, pick_ref, back_ref, slot_ref):
    rows = iq_ref.shape[0]
    for r in range(rows):
        raw = dot(iq_ref[r], keys_ref[r], ((1,), (1,))) * (iq_ref.shape[2] ** (-0.5))
        score_ref[r : r + 1, :] = dot(iw_ref[r : r + 1, :], jnp.maximum(raw, 0.0), precision=HIGH)
    n = route_ref.shape[1]
    is_mine = route_ref[...] == ctx_ref[0]
    hit = jnp.max(jnp.where(is_mine, 1.0, 0.0), axis=0, keepdims=True)
    gate = jnp.sum(jnp.where(is_mine, gate_ref[...], 0.0), axis=0, keepdims=True)
    upto = jnp.where(iota((n, n), 0) <= iota((n, n), 1), 1.0, 0.0).astype(bf16)
    slot = dot(jnp.broadcast_to(hit, (8, n)).astype(bf16), upto)[0:1].astype(jnp.int32) - 1
    pick = jnp.where((iota((CAP, n), 0) == slot) & (hit > 0.0), 1.0, 0.0)
    pick_ref[...] = pick.astype(bf16)
    row, col = iota((128, n), 0), iota((128, n), 1)
    spread = (row // 8 * 6 + row % 8 == col) & (row % 8 < 6)
    spread = jnp.where(spread, 1.0, 0.0).astype(bf16)
    back_ref[...] = dot(spread, pick.astype(bf16), ((1,), (1,))).astype(bf16)
    slot_ref[...] = jnp.broadcast_to(jnp.sum(pick * gate, axis=1, keepdims=True), (CAP, 128))


def side(ctx, route, gate, iq, iw, keys):
    return pl.pallas_call(
        side_kernel,
        in_specs=[SMEM] + [VMEM] * 5,
        out_specs=[VMEM] * 4,
        out_shape=[
            jax.ShapeDtypeStruct((iq.shape[0], keys.shape[1]), f32),
            jax.ShapeDtypeStruct((CAP, route.shape[1]), bf16),
            jax.ShapeDtypeStruct((128, CAP), bf16),
            jax.ShapeDtypeStruct((CAP, 128), f32),
        ],
        compiler_params=params(),
        name="side",
    )(ctx, route, gate, iq, iw, keys)


def pair_kernel(mine_ref, other_ref, out_ref):
    one = mine_ref[...]
    two = other_ref[...].astype(f32)
    peak_one, total_one = read_stats(one)
    peak_two, total_two = read_stats(two)
    peak = jnp.maximum(peak_one, peak_two)
    f_one, f_two = jnp.exp(peak_one - peak), jnp.exp(peak_two - peak)
    out_ref[..., :LAT] = (one[..., :LAT] * f_one + two[..., :LAT] * f_two).astype(bf16)
    out_ref[..., LAT:] = stats_tile(peak, total_one * f_one + total_two * f_two).astype(bf16)


def pair(mine, other):
    spec = pl.BlockSpec((2,) + mine.shape[1:], lambda i: (i, 0, 0))
    return pl.pallas_call(
        pair_kernel,
        grid=(mine.shape[0] // 2,),
        in_specs=[spec, spec],
        out_specs=spec,
        out_shape=jax.ShapeDtypeStruct(mine.shape, bf16),
        compiler_params=params(),
        name="pair",
    )(mine, other)


def values_kernel(parts_ref, w_ref, out_ref):
    n, rows, _ = parts_ref.shape
    peaks, totals = [], []
    for i in range(n):
        p, t = read_stats(parts_ref[i].astype(f32))
        peaks.append(p)
        totals.append(t)
    peak = functools.reduce(jnp.maximum, peaks)
    summed = jnp.zeros((rows, LAT), f32)
    total = jnp.zeros((rows, 1), f32)
    for i in range(n):
        factor = jnp.exp(peaks[i] - peak)
        summed = summed + parts_ref[i, :, :LAT].astype(f32) * factor
        total = total + totals[i] * factor
    lat = (summed / total).astype(bf16)
    row, col = iota((64, rows), 0), iota((64, rows), 1)
    by_head = jnp.where((row % 8) * 8 + row // 8 == col, 1.0, 0.0).astype(bf16)
    lat = dot(by_head, lat)
    out = [dot(lat[8 * h : 8 * h + 8].astype(bf16), w_ref[h]) for h in range(8)]
    half = jnp.concatenate([jnp.concatenate(out[:4], axis=1), jnp.concatenate(out[4:], axis=1)], axis=0)
    half = half.astype(bf16)
    for e in range(out_ref.shape[0]):
        out_ref[e] = half


def values(parts, w_uv, n_exp):
    return pl.pallas_call(
        values_kernel,
        in_specs=[VMEM] * 2,
        out_specs=VMEM,
        out_shape=jax.ShapeDtypeStruct((n_exp, 16, 512), bf16),
        compiler_params=params(),
        name="values",
    )(parts, w_uv)


def project_kernel(values_ref, w_ref, out_ref, acc_ref):
    x = values_ref[...].astype(f32)
    n = x.shape[0]
    low = x[:, :8].reshape(n * 8, 512).astype(bf16)
    high = x[:, 8:].reshape(n * 8, 512).astype(bf16)
    acc = dot(low, w_ref[:512, :]) + dot(high, w_ref[512:, :])
    for e in range(n):
        acc_ref[6 * e : 6 * e + 6, :] = acc[8 * e : 8 * e + 6, :]
    out_ref[...] = acc_ref[...].astype(bf16)


def project(vals, w_o):
    shape = (vals.shape[0] * 6, w_o.shape[1])
    return pl.pallas_call(
        project_kernel,
        in_specs=[VMEM] * 2,
        out_specs=VMEM,
        out_shape=jax.ShapeDtypeStruct(shape, bf16),
        scratch_shapes=[pltpu.VMEM(shape, f32)],
        compiler_params=params(),
        name="project",
    )(vals, w_o)


def expert_in_kernel(
    ctx_ref, own_ref, up_ref, down_ref, far_up_ref, far_down_ref, hidden_ref, gain_ref, pick_ref,
    gate_w_ref, up_w_ref, out_ref, keep_ref, rows_ref, squares_ref,
):
    @pl.when(pl.program_id(0) == 0)
    def _():
        attn = own_ref[...].astype(f32) + up_ref[...].astype(f32) + down_ref[...].astype(f32)
        attn = attn + far_up_ref[...].astype(f32) + far_down_ref[...].astype(f32)
        resid = (hidden_ref[...].astype(f32) + attn).astype(bf16)
        resid32 = resid.astype(f32)
        scaled = (resid32 * gain_ref[...]).astype(bf16)
        rows_ref[...] = dot(pick_ref[...], scaled).astype(bf16)
        picked = dot(pick_ref[...], resid)
        squares = dot(jnp.ones((8, picked.shape[1]), f32), picked * picked, ((1,), (1,)), HIGH)
        hi, mid, low = split3(squares)
        line = iota(squares.shape, 0)
        parts = jnp.where(line == 0, hi, jnp.where(line == 1, mid, jnp.where(line == 2, low, 0.0)))
        squares_ref[...] = jnp.concatenate([parts, jnp.zeros((8, 256 - CAP), f32)], axis=1)
        n = resid.shape[0]
        own_row = jnp.where(iota((8, n), 1) == ctx_ref[0] * 6 + iota((8, n), 0), 1.0, 0.0)
        keep_ref[...] = dot(own_row.astype(bf16), resid)

    rows = rows_ref[...]
    gate = dot(rows, gate_w_ref[...])
    up = dot(rows, up_w_ref[...])
    squares = squares_ref[...]
    for e in range(out_ref.shape[0]):
        cols = slice(128 * e, 128 * e + 128)
        both = jnp.concatenate([gate[:, cols], up[:, cols]], axis=1)
        out_ref[e] = jnp.concatenate([both, squares], axis=0).astype(bf16)


def expert_in(ctx, sums, hidden, gain, pick, w_in, n_exp):
    rows, width = hidden.shape
    steps = 4
    cols = w_in.shape[1] // 2 // steps
    whole = lambda a: pl.BlockSpec(a.shape, lambda i: (0,) * a.ndim)
    return pl.pallas_call(
        expert_in_kernel,
        grid=(steps,),
        in_specs=[SMEM]
        + [whole(a) for a in (*sums, hidden, gain, pick)]
        + [
            pl.BlockSpec((width, cols), lambda i: (0, i)),
            pl.BlockSpec((width, cols), lambda i: (0, i + steps)),
        ],
        out_specs=[
            pl.BlockSpec((n_exp // steps, CAP + 8, 256), lambda i: (i, 0, 0)),
            pl.BlockSpec((8, width), lambda i: (0, 0)),
        ],
        out_shape=[
            jax.ShapeDtypeStruct((n_exp, CAP + 8, 256), bf16),
            jax.ShapeDtypeStruct((8, width), f32),
        ],
        scratch_shapes=[pltpu.VMEM((CAP, width), bf16), pltpu.VMEM((8, 256), f32)],
        compiler_params=params(),
        name="expert_in",
    )(ctx, *sums, hidden, gain, pick, w_in, w_in)


def act_kernel(parts_ref, out_ref):
    x = jnp.sum(parts_ref[...].astype(f32), axis=0)
    line = x[CAP : CAP + 1, :CAP] + x[CAP + 1 : CAP + 2, :CAP] + x[CAP + 2 : CAP + 3, :CAP]
    diagonal = iota((CAP, CAP), 0) == iota((CAP, CAP), 1)
    squares = jnp.sum(jnp.where(diagonal, line, 0.0), axis=1, keepdims=True)
    inv = lax.rsqrt(squares / D + EPS)
    gate, up = x[:CAP, :128] * inv, x[:CAP, 128:] * inv
    act = (jax.nn.silu(gate) * up).astype(bf16)
    for e in range(out_ref.shape[0]):
        out_ref[e] = act


def activation(parts):
    return pl.pallas_call(
        act_kernel,
        in_specs=[VMEM],
        out_specs=VMEM,
        out_shape=jax.ShapeDtypeStruct((parts.shape[0], CAP, 128), bf16),
        compiler_params=params(),
        name="activation",
    )(parts)


def expert_out_kernel(act_ref, w_ref, slot_ref, back_ref, out_ref):
    act = jnp.concatenate([act_ref[e] for e in range(act_ref.shape[0])], axis=1)
    out = (dot(act, w_ref[...]) * slot_ref[:, 0:1]).astype(bf16)
    back = dot(back_ref[...], out)
    n = out_ref.shape[0]
    low = back[:, :256].reshape(n, 8, 256)
    high = jnp.concatenate([back[:, 256:], jnp.zeros((n * 8, 64), f32)], axis=1).reshape(n, 8, 256)
    out_ref[...] = jnp.concatenate([low, high], axis=1).astype(bf16)


def expert_out(act, w_down, slot, back, n_ctx):
    return pl.pallas_call(
        expert_out_kernel,
        in_specs=[VMEM] * 4,
        out_specs=VMEM,
        out_shape=jax.ShapeDtypeStruct((n_ctx, 16, 256), bf16),
        compiler_params=params(),
        name="expert_out",
    )(act, w_down, slot, back)


def last_kernel(parts_ref, keep_ref, out_ref):
    x = jnp.sum(parts_ref[...].astype(f32), axis=0)
    moe = jnp.concatenate([x[:8], x[8:, :192]], axis=1)
    out_ref[...] = (keep_ref[...] + moe)[:6].astype(bf16)


def last(parts, keep):
    return pl.pallas_call(
        last_kernel,
        in_specs=[VMEM] * 2,
        out_specs=VMEM,
        out_shape=jax.ShapeDtypeStruct((6, keep.shape[1]), bf16),
        compiler_params=params(),
        name="last",
    )(parts, keep)


def local(
    cache, idx_keys, lat_query, idx_query, idx_weight, chosen_blocks, w_uv, w_o, hidden_in, norm_gain,
    route, route_weight, w_in, w_down,
):
    n_ctx, n_exp = lax.axis_size("ctx"), lax.axis_size("exp")
    n_z = n_ctx // 2
    ctx = lax.axis_index("ctx").astype(jnp.int32).reshape(1)
    other_core = [(i, i ^ 1) for i in range(n_ctx)]
    z_groups = [[2 * z + k for z in range(n_z)] for k in range(2)]

    def along_z(shift):
        return [(i, (i + 2 * shift) % n_ctx) for i in range(n_ctx)]

    mine, other = attention(ctx, chosen_blocks, lat_query, cache)
    other = lax.ppermute(other, "ctx", other_core)
    index_scores, pick, back, slot = side(
        ctx, route.T, route_weight.T, idx_query, idx_weight, idx_keys
    )
    parts = pair(mine, other)
    parts = lax.all_to_all(parts, "ctx", 0, 0, axis_index_groups=z_groups)
    vals = values(parts, w_uv, n_exp)
    vals = lax.all_to_all(vals, "exp", 0, 0)
    part = project(vals, w_o)

    def add(*terms):
        return sum(t.astype(f32) for t in terms).astype(bf16)

    own = add(part, lax.ppermute(part, "ctx", other_core))
    above = lax.ppermute(own, "ctx", along_z(-1))
    below = lax.ppermute(own, "ctx", along_z(1))
    far_above = lax.ppermute(add(own, above, below), "ctx", along_z(-3))
    far_below = lax.ppermute(add(own, above), "ctx", along_z(3))
    sums = (own, above, below, far_above, far_below)

    terms, keep = expert_in(ctx, sums, hidden_in, norm_gain.reshape(1, -1), pick, w_in[0], n_exp)
    terms = lax.all_to_all(terms, "exp", 0, 0)
    act = lax.all_to_all(activation(terms), "exp", 0, 0)
    outs = expert_out(act, w_down[0], slot, back, n_ctx)
    outs = lax.all_to_all(outs, "ctx", 0, 0)
    return index_scores, last(outs, keep)


def solution(mesh):
    return jax.shard_map(
        local,
        mesh=mesh,
        in_specs=(
            P("exp", "ctx", None),
            P("exp", "ctx", None),
            P("exp", None, None),
            P("exp", None, None),
            P("exp", None),
            P("exp", None),
            P("ctx", None, None),
            P("ctx", "exp"),
            P(None, "exp"),
            P("exp"),
            P(),
            P(),
            P("ctx", "exp", None),
            P("ctx", None, "exp"),
        ),
        out_specs=(P("exp", "ctx"), P("ctx", "exp")),
        check_vma=False,
    )
```

```python
import functools

import jax
import jax.numpy as jnp
from jax import lax
from jax.experimental import pallas as pl
from jax.experimental.pallas import tpu as pltpu
from jax.sharding import PartitionSpec as P

f32 = jnp.float32
bf16 = jnp.bfloat16
D = 7168
BLOCK = 64
LAT = 512
WIDE = 640
CAP = 48
FAR = 6
NEG = -1e30
SCORE_SCALE = 192.0 ** (-0.5)
EPS = 1e-06
HIGH = lax.Precision.HIGHEST
MB = 1 << 20

VMEM = pl.BlockSpec(memory_space=pltpu.VMEM)
SMEM = pl.BlockSpec(memory_space=pltpu.SMEM)
HBM = pl.BlockSpec(memory_space=pltpu.HBM)
ANY = pl.BlockSpec(memory_space=pl.ANY)


def in_hbm(x):
    return pltpu.with_memory_space_constraint(x, pltpu.HBM)


def params(mb=8):
    return pltpu.CompilerParams(vmem_limit_bytes=mb * MB)


def iota(shape, dim):
    return lax.broadcasted_iota(jnp.int32, shape, dim)


def dot(a, b, dims=((1,), (0,)), precision=None):
    return lax.dot_general(a, b, (dims, ((), ())), precision=precision, preferred_element_type=f32)


def split3(x):
    hi = x.astype(bf16).astype(f32)
    mid = (x - hi).astype(bf16).astype(f32)
    low = (x - hi - mid).astype(bf16).astype(f32)
    return hi, mid, low


def stats_tile(peak, total):
    lane = iota(peak.shape[:-1] + (128,), len(peak.shape) - 1)
    tile = jnp.zeros(peak.shape[:-1] + (128,), f32)
    for place, part in enumerate(split3(peak) + split3(total)):
        tile = jnp.where(lane == place, part, tile)
    return tile


def read_stats(x):
    tile = x[..., LAT:WIDE]
    lane = iota(tile.shape, len(tile.shape) - 1)
    peak = jnp.sum(jnp.where(lane < 3, tile, 0.0), axis=-1, keepdims=True)
    total = jnp.sum(jnp.where((lane >= 3) & (lane < 6), tile, 0.0), axis=-1, keepdims=True)
    return peak, total


def attention_kernel(ctx_ref, blocks_ref, query_ref, cache_ref, mine_ref, other_ref, mask_ref):
    step = pl.program_id(0)
    ctx = ctx_ref[0]
    core = lax.rem(ctx, 2)
    tokens = cache_ref.shape[2]
    per = tokens // BLOCK

    @pl.when(step == 0)
    def _():
        rows = blocks_ref.shape[0]
        block_of = iota((rows, tokens), 1) // BLOCK
        mask = jnp.zeros((rows, tokens), f32)
        picked = blocks_ref[...]
        for b in range(per):
            hit = jnp.max(jnp.where(picked == ctx * per + b, 1.0, 0.0), axis=1, keepdims=True)
            mask = jnp.where(block_of == b, hit, mask)
        mask_ref[...] = mask

    mine, other = [], []
    for i in range(2):
        chosen = mask_ref[pl.ds(step * 2 + i, 1), :] > 0.0
        keys = cache_ref[i]
        scores = dot(query_ref[i], keys, ((0,), (0,))) * SCORE_SCALE
        masked = jnp.where(chosen, scores, NEG)
        peak = jnp.max(masked, axis=1, keepdims=True)
        expo = jnp.where(chosen, jnp.exp(masked - peak), 0.0)
        total = jnp.sum(expo, axis=1, keepdims=True)
        weighted = dot(expo.astype(bf16), keys[:LAT], ((1,), (1,)))
        wide = jnp.concatenate([weighted, stats_tile(peak, total)], axis=1)
        wide = wide.reshape(8, 2, 8, WIDE)
        mine.append(jnp.where(core == 0, wide[:, 0], wide[:, 1]))
        other.append(jnp.where(core == 0, wide[:, 1], wide[:, 0]))
    mine_ref[...] = jnp.concatenate(mine, axis=1)
    other_ref[...] = jnp.concatenate(other, axis=1).astype(bf16)


def attention(ctx, blocks, query, cache):
    rows, width, heads = query.shape
    tokens = cache.shape[2]
    return pl.pallas_call(
        attention_kernel,
        grid=(rows // 2,),
        in_specs=[
            SMEM,
            pl.BlockSpec((rows, blocks.shape[1]), lambda i: (0, 0)),
            pl.BlockSpec((2, width, heads), lambda i: (i, 0, 0)),
            pl.BlockSpec((2, width, tokens), lambda i: (i, 0, 0)),
        ],
        out_specs=[pl.BlockSpec((8, 16, WIDE), lambda i: (0, i, 0))] * 2,
        out_shape=[
            jax.ShapeDtypeStruct((8, rows * 8, WIDE), f32),
            jax.ShapeDtypeStruct((8, rows * 8, WIDE), bf16),
        ],
        scratch_shapes=[pltpu.VMEM((rows, tokens), f32)],
        compiler_params=params(16),
        name="attention",
    )(ctx, in_hbm(blocks), in_hbm(query), in_hbm(cache))


def side_kernel(
    ctx_ref, route_ref, gate_ref, iq_ref, iw_ref, keys_ref, _,
    score_ref, send_ref, pick_ref, back_ref, slot_ref,
):
    rows = iq_ref.shape[0]
    for r in range(rows):
        raw = dot(iq_ref[r], keys_ref[r], ((1,), (1,))) * (iq_ref.shape[2] ** (-0.5))
        score_ref[r : r + 1, :] = dot(iw_ref[r : r + 1, :], jnp.maximum(raw, 0.0), precision=HIGH)
    n = route_ref.shape[1]
    ctx = ctx_ref[0]
    n_ctx = n // 6
    names = route_ref[...]
    experts = [ctx, lax.rem(ctx + n_ctx - FAR, n_ctx), lax.rem(ctx + FAR, n_ctx)]
    hit = [jnp.max(jnp.where(names == g, 1.0, 0.0), axis=0, keepdims=True) for g in experts]
    upto = jnp.where(iota((n, n), 0) <= iota((n, n), 1), 1.0, 0.0).astype(bf16)
    hits = jnp.concatenate(hit + [jnp.zeros((8 - len(hit), n), f32)], axis=0)
    slots = dot(hits.astype(bf16), upto).astype(jnp.int32) - 1
    line, col = iota((8, n), 0), iota((8, n), 1)
    picks = []
    for j, g in enumerate(experts):
        picks.append(jnp.where((iota((CAP, n), 0) == slots[j : j + 1]) & (hit[j] > 0.0), 1.0, 0.0))
        own = jnp.where((col == 6 * g + line) & (line < 6), 1.0, 0.0)
        both = jnp.concatenate([picks[j], own], axis=0).astype(bf16)
        if j == 0:
            pick_ref[...] = both
        else:
            send_ref[j - 1] = both
    gate = jnp.sum(jnp.where(names == ctx, gate_ref[...], 0.0), axis=0, keepdims=True)
    row, col = iota((128, n), 0), iota((128, n), 1)
    spread = (row // 8 * 6 + row % 8 == col) & (row % 8 < 6)
    spread = jnp.where(spread, 1.0, 0.0).astype(bf16)
    back_ref[...] = dot(spread, picks[0].astype(bf16), ((1,), (1,))).astype(bf16)
    slot_ref[...] = jnp.broadcast_to(jnp.sum(picks[0] * gate, axis=1, keepdims=True), (CAP, 128))


def side(ctx, route, gate, iq, iw, keys, after):
    n = route.shape[1]
    return pl.pallas_call(
        side_kernel,
        in_specs=[SMEM] + [VMEM] * 5 + [ANY],
        out_specs=[VMEM] * 5,
        out_shape=[
            jax.ShapeDtypeStruct((iq.shape[0], keys.shape[1]), f32),
            jax.ShapeDtypeStruct((2, CAP + 8, n), bf16),
            jax.ShapeDtypeStruct((CAP + 8, n), bf16),
            jax.ShapeDtypeStruct((128, CAP), bf16),
            jax.ShapeDtypeStruct((CAP, 128), f32),
        ],
        compiler_params=params(),
        name="side",
    )(ctx, route, gate, iq, iw, keys, after)


def pair_kernel(mine_ref, other_ref, out_ref):
    one = mine_ref[...]
    two = other_ref[...].astype(f32)
    peak_one, total_one = read_stats(one)
    peak_two, total_two = read_stats(two)
    peak = jnp.maximum(peak_one, peak_two)
    f_one, f_two = jnp.exp(peak_one - peak), jnp.exp(peak_two - peak)
    out_ref[..., :LAT] = (one[..., :LAT] * f_one + two[..., :LAT] * f_two).astype(bf16)
    out_ref[..., LAT:] = stats_tile(peak, total_one * f_one + total_two * f_two).astype(bf16)


def pair(mine, other):
    spec = pl.BlockSpec((2,) + mine.shape[1:], lambda i: (i, 0, 0))
    return pl.pallas_call(
        pair_kernel,
        grid=(mine.shape[0] // 2,),
        in_specs=[spec, spec],
        out_specs=spec,
        out_shape=jax.ShapeDtypeStruct(mine.shape, bf16),
        compiler_params=params(),
        name="pair",
    )(mine, other)


def values_kernel(parts_ref, w_ref, out_ref):
    n, rows, _ = parts_ref.shape
    peaks, totals = [], []
    for i in range(n):
        p, t = read_stats(parts_ref[i].astype(f32))
        peaks.append(p)
        totals.append(t)
    peak = functools.reduce(jnp.maximum, peaks)
    summed = jnp.zeros((rows, LAT), f32)
    total = jnp.zeros((rows, 1), f32)
    for i in range(n):
        factor = jnp.exp(peaks[i] - peak)
        summed = summed + parts_ref[i, :, :LAT].astype(f32) * factor
        total = total + totals[i] * factor
    lat = (summed / total).astype(bf16)
    row, col = iota((64, rows), 0), iota((64, rows), 1)
    by_head = jnp.where((row % 8) * 8 + row // 8 == col, 1.0, 0.0).astype(bf16)
    lat = dot(by_head, lat)
    out = [dot(lat[8 * h : 8 * h + 8].astype(bf16), w_ref[h]) for h in range(8)]
    half = jnp.concatenate([jnp.concatenate(out[:4], axis=1), jnp.concatenate(out[4:], axis=1)], axis=0)
    half = half.astype(bf16)
    for e in range(out_ref.shape[0]):
        out_ref[e] = half


def values(parts, w_uv, n_exp):
    return pl.pallas_call(
        values_kernel,
        in_specs=[VMEM] * 2,
        out_specs=VMEM,
        out_shape=jax.ShapeDtypeStruct((n_exp, 16, 512), bf16),
        compiler_params=params(),
        name="values",
    )(parts, w_uv)


def project_kernel(values_ref, w_ref, _, out_ref, acc_ref):
    x = values_ref[...].astype(f32)
    n = x.shape[0]
    low = x[:, :8].reshape(n * 8, 512).astype(bf16)
    high = x[:, 8:].reshape(n * 8, 512).astype(bf16)
    acc = dot(low, w_ref[:, :512], ((1,), (1,))) + dot(high, w_ref[:, 512:], ((1,), (1,)))
    for e in range(n):
        acc_ref[6 * e : 6 * e + 6, :] = acc[8 * e : 8 * e + 6, :]
    out_ref[...] = acc_ref[...].astype(bf16)


def project(vals, w_o, after):
    shape = (vals.shape[0] * 6, w_o.shape[0])
    return pl.pallas_call(
        project_kernel,
        in_specs=[VMEM] * 2 + [ANY],
        out_specs=VMEM,
        out_shape=jax.ShapeDtypeStruct(shape, bf16),
        scratch_shapes=[pltpu.VMEM(shape, f32)],
        compiler_params=params(),
        name="project",
    )(vals, w_o, after)


def fold_kernel(own_ref, above_ref, below_ref, send_ref, up_ref, down_ref):
    two = own_ref[...].astype(f32) + above_ref[...].astype(f32)
    three = (two + below_ref[...].astype(f32)).astype(bf16)
    up_ref[...] = dot(send_ref[0], three).astype(bf16)
    down_ref[...] = dot(send_ref[1], two.astype(bf16)).astype(bf16)


def fold(own, above, below, send):
    shape = jax.ShapeDtypeStruct((send.shape[1], own.shape[1]), bf16)
    return pl.pallas_call(
        fold_kernel,
        in_specs=[VMEM] * 4,
        out_specs=[VMEM] * 2,
        out_shape=[shape, shape],
        compiler_params=params(),
        name="fold",
    )(own, above, below, send)


def base_kernel(own_ref, above_ref, below_ref, hidden_ref, pick_ref, w_hbm, out_ref, w_ref, sem):
    load = pltpu.make_async_copy(w_hbm, w_ref, sem)
    load.start()
    pick = pick_ref[...]
    near = dot(pick, own_ref[...]) + dot(pick, above_ref[...]) + dot(pick, below_ref[...])
    out_ref[...] = dot(pick, hidden_ref[...]) + near
    load.wait()


def base(own, above, below, hidden, pick, w_in):
    return pl.pallas_call(
        base_kernel,
        in_specs=[VMEM] * 5 + [HBM],
        out_specs=[VMEM] * 2,
        out_shape=[
            jax.ShapeDtypeStruct((pick.shape[0], own.shape[1]), f32),
            jax.ShapeDtypeStruct(w_in.shape, bf16),
        ],
        scratch_shapes=[pltpu.SemaphoreType.DMA],
        compiler_params=params(),
        name="base",
    )(own, above, below, hidden, pick, in_hbm(w_in))


def expert_in_kernel(near_ref, far_up_ref, far_down_ref, gain_ref, w_ref, out_ref, keep_ref):
    n = out_ref.shape[0]
    half = w_ref.shape[1] // 2
    attn = near_ref[...] + far_up_ref[...].astype(f32) + far_down_ref[...].astype(f32)
    resid32 = attn.astype(bf16).astype(f32)
    keep_ref[...] = resid32[CAP:]
    picked = resid32[:CAP]
    rows = (picked * gain_ref[...]).astype(bf16)
    squares = dot(jnp.ones((8, picked.shape[1]), f32), picked * picked, ((1,), (1,)), HIGH)
    hi, mid, low = split3(squares)
    line = iota(squares.shape, 0)
    parts = jnp.where(line == 0, hi, jnp.where(line == 1, mid, jnp.where(line == 2, low, 0.0)))
    parts = jnp.concatenate([parts, jnp.zeros((8, 256 - CAP), f32)], axis=1)
    for e in range(0, n, 2):
        gate = dot(rows, w_ref[:, 128 * e : 128 * e + 256])
        up = dot(rows, w_ref[:, half + 128 * e : half + 128 * e + 256])
        for i in range(2):
            here = slice(128 * i, 128 * i + 128)
            both = jnp.concatenate([gate[:, here], up[:, here]], axis=1)
            out_ref[e + i] = jnp.concatenate([both, parts], axis=0).astype(bf16)


def expert_in(near, far_up, far_down, gain, w_in, n_exp):
    width = near.shape[1]
    return pl.pallas_call(
        expert_in_kernel,
        in_specs=[VMEM] * 5,
        out_specs=[VMEM] * 2,
        out_shape=[
            jax.ShapeDtypeStruct((n_exp, CAP + 8, 256), bf16),
            jax.ShapeDtypeStruct((8, width), f32),
        ],
        compiler_params=params(),
        name="expert_in",
    )(near, far_up, far_down, gain, w_in)


def act_kernel(parts_ref, out_ref):
    x = jnp.sum(parts_ref[...].astype(f32), axis=0)
    line = x[CAP : CAP + 1, :CAP] + x[CAP + 1 : CAP + 2, :CAP] + x[CAP + 2 : CAP + 3, :CAP]
    diagonal = iota((CAP, CAP), 0) == iota((CAP, CAP), 1)
    squares = jnp.sum(jnp.where(diagonal, line, 0.0), axis=1, keepdims=True)
    inv = lax.rsqrt(squares / D + EPS)
    gate, up = x[:CAP, :128] * inv, x[:CAP, 128:] * inv
    act = (jax.nn.silu(gate) * up).astype(bf16)
    for e in range(out_ref.shape[0]):
        out_ref[e] = act


def activation(parts):
    return pl.pallas_call(
        act_kernel,
        in_specs=[VMEM],
        out_specs=VMEM,
        out_shape=jax.ShapeDtypeStruct((parts.shape[0], CAP, 128), bf16),
        compiler_params=params(),
        name="activation",
    )(parts)


def expert_out_kernel(act_ref, w_ref, slot_ref, back_ref, out_ref):
    act = jnp.concatenate([act_ref[e] for e in range(act_ref.shape[0])], axis=1)
    out = (dot(act, w_ref[...], ((1,), (1,))) * slot_ref[:, 0:1]).astype(bf16)
    back = dot(back_ref[...], out)
    n = out_ref.shape[0]
    low = back[:, :256].reshape(n, 8, 256)
    high = jnp.concatenate([back[:, 256:], jnp.zeros((n * 8, 64), f32)], axis=1).reshape(n, 8, 256)
    out_ref[...] = jnp.concatenate([low, high], axis=1).astype(bf16)


def expert_out(act, w_down, slot, back, n_ctx):
    return pl.pallas_call(
        expert_out_kernel,
        in_specs=[VMEM] * 4,
        out_specs=VMEM,
        out_shape=jax.ShapeDtypeStruct((n_ctx, 16, 256), bf16),
        compiler_params=params(),
        name="expert_out",
    )(act, w_down, slot, back)


def last_kernel(parts_ref, keep_ref, out_ref):
    x = jnp.sum(parts_ref[...].astype(f32), axis=0)
    moe = jnp.concatenate([x[:8], x[8:, :192]], axis=1)
    out_ref[...] = (keep_ref[...] + moe)[:6].astype(bf16)


def last(parts, keep):
    return pl.pallas_call(
        last_kernel,
        in_specs=[VMEM] * 2,
        out_specs=VMEM,
        out_shape=jax.ShapeDtypeStruct((6, keep.shape[1]), bf16),
        compiler_params=params(),
        name="last",
    )(parts, keep)


def local(
    cache, idx_keys, lat_query, idx_query, idx_weight, chosen_blocks, w_uv, w_o, hidden_in, norm_gain,
    route, route_weight, w_in, w_down,
):
    n_ctx, n_exp = lax.axis_size("ctx"), lax.axis_size("exp")
    n_z = n_ctx // 2
    ctx = lax.axis_index("ctx").astype(jnp.int32).reshape(1)
    other_core = [(i, i ^ 1) for i in range(n_ctx)]
    def along_z(shift):
        return [(i, (i + shift) % n_ctx) for i in range(n_ctx)]

    z_groups = [[2 * z + k for z in range(n_z)] for k in range(2)]

    mine, other = attention(
        ctx, chosen_blocks, jnp.swapaxes(lat_query, 1, 2), jnp.swapaxes(cache, 1, 2)
    )
    other = lax.ppermute(other, "ctx", other_core)
    parts = pair(mine, other)
    parts = lax.all_to_all(parts, "ctx", 0, 0, axis_index_groups=z_groups)
    vals = values(parts, w_uv, n_exp)
    index_scores, send, pick, back, slot = side(
        ctx, route.T, route_weight.T, idx_query, idx_weight, idx_keys, vals
    )
    vals = lax.all_to_all(vals, "exp", 0, 0)
    part = project(vals, w_o.T, send)
    own = part.astype(f32) + lax.ppermute(part, "ctx", other_core).astype(f32)
    own = own.astype(bf16)
    above = lax.ppermute(own, "ctx", along_z(-2))
    below = lax.ppermute(own, "ctx", along_z(2))
    up, down = fold(own, above, below, send)
    far_up = lax.ppermute(up, "ctx", along_z(-FAR))
    far_down = lax.ppermute(down, "ctx", along_z(FAR))
    near, w_gate_up = base(own, above, below, hidden_in, pick, w_in[0])
    terms, keep = expert_in(near, far_up, far_down, norm_gain.reshape(1, -1), w_gate_up, n_exp)
    terms = lax.all_to_all(terms, "exp", 0, 0)
    act = lax.all_to_all(activation(terms), "exp", 0, 0)
    outs = expert_out(act, w_down[0].T, slot, back, n_ctx)
    outs = lax.all_to_all(outs, "ctx", 0, 0)
    return index_scores, last(outs, keep)


def solution(mesh):
    return jax.shard_map(
        local,
        mesh=mesh,
        in_specs=(
            P("exp", "ctx", None),
            P("exp", "ctx", None),
            P("exp", None, None),
            P("exp", None, None),
            P("exp", None),
            P("exp", None),
            P("ctx", None, None),
            P("ctx", "exp"),
            P(None, "exp"),
            P("exp"),
            P(),
            P(),
            P("ctx", "exp", None),
            P("ctx", None, "exp"),
        ),
        out_specs=(P("exp", "ctx"), P("ctx", "exp")),
        check_vma=False,
    )
```

```python
import functools

import jax
import jax.numpy as jnp
from jax import lax
from jax.experimental import pallas as pl
from jax.experimental.pallas import tpu as pltpu
from jax.sharding import PartitionSpec as P

f32 = jnp.float32
bf16 = jnp.bfloat16
D = 7168
BLOCK = 64
LAT = 512
WIDE = 640
CAP = 48
UP, DOWN = 6, 4
NEG = -1e30
SCORE_SCALE = 192.0 ** (-0.5)
EPS = 1e-06
HIGH = lax.Precision.HIGHEST
MB = 1 << 20

VMEM = pl.BlockSpec(memory_space=pltpu.VMEM)
SMEM = pl.BlockSpec(memory_space=pltpu.SMEM)
HBM = pl.BlockSpec(memory_space=pltpu.HBM)
ANY = pl.BlockSpec(memory_space=pl.ANY)


def in_hbm(x):
    return pltpu.with_memory_space_constraint(x, pltpu.HBM)


def params(mb=8):
    return pltpu.CompilerParams(vmem_limit_bytes=mb * MB)


def iota(shape, dim):
    return lax.broadcasted_iota(jnp.int32, shape, dim)


def dot(a, b, dims=((1,), (0,)), precision=None):
    return lax.dot_general(a, b, (dims, ((), ())), precision=precision, preferred_element_type=f32)


def split3(x):
    hi = x.astype(bf16).astype(f32)
    mid = (x - hi).astype(bf16).astype(f32)
    low = (x - hi - mid).astype(bf16).astype(f32)
    return hi, mid, low


def stats_tile(peak, total):
    lane = iota(peak.shape[:-1] + (128,), len(peak.shape) - 1)
    tile = jnp.zeros(peak.shape[:-1] + (128,), f32)
    for place, part in enumerate(split3(peak) + split3(total)):
        tile = jnp.where(lane == place, part, tile)
    return tile


def read_stats(x):
    tile = x[..., LAT:WIDE]
    lane = iota(tile.shape, len(tile.shape) - 1)
    peak = jnp.sum(jnp.where(lane < 3, tile, 0.0), axis=-1, keepdims=True)
    total = jnp.sum(jnp.where((lane >= 3) & (lane < 6), tile, 0.0), axis=-1, keepdims=True)
    return peak, total


def attention_kernel(ctx_ref, blocks_ref, query_ref, cache_ref, mine_ref, other_ref, mask_ref):
    step = pl.program_id(0)
    ctx = ctx_ref[0]
    core = lax.rem(ctx, 2)
    tokens = cache_ref.shape[2]
    per = tokens // BLOCK

    @pl.when(step == 0)
    def _():
        rows = blocks_ref.shape[0]
        block_of = iota((rows, tokens), 1) // BLOCK
        mask = jnp.zeros((rows, tokens), f32)
        picked = blocks_ref[...]
        for b in range(per):
            hit = jnp.max(jnp.where(picked == ctx * per + b, 1.0, 0.0), axis=1, keepdims=True)
            mask = jnp.where(block_of == b, hit, mask)
        mask_ref[...] = mask

    mine, other = [], []
    for i in range(2):
        chosen = mask_ref[pl.ds(step * 2 + i, 1), :] > 0.0
        keys = cache_ref[i]
        scores = dot(query_ref[i], keys, ((0,), (0,))) * SCORE_SCALE
        masked = jnp.where(chosen, scores, NEG)
        peak = jnp.max(masked, axis=1, keepdims=True)
        expo = jnp.where(chosen, jnp.exp(masked - peak), 0.0)
        total = jnp.sum(expo, axis=1, keepdims=True)
        weighted = dot(expo.astype(bf16), keys[:LAT], ((1,), (1,)))
        wide = jnp.concatenate([weighted, stats_tile(peak, total)], axis=1)
        wide = wide.reshape(8, 2, 8, WIDE)
        mine.append(jnp.where(core == 0, wide[:, 0], wide[:, 1]))
        other.append(jnp.where(core == 0, wide[:, 1], wide[:, 0]))
    mine_ref[...] = jnp.concatenate(mine, axis=1)
    other_ref[...] = jnp.concatenate(other, axis=1).astype(bf16)


def attention(ctx, blocks, query, cache):
    rows, width, heads = query.shape
    tokens = cache.shape[2]
    return pl.pallas_call(
        attention_kernel,
        grid=(rows // 2,),
        in_specs=[
            SMEM,
            pl.BlockSpec((rows, blocks.shape[1]), lambda i: (0, 0)),
            pl.BlockSpec((2, width, heads), lambda i: (i, 0, 0)),
            pl.BlockSpec((2, width, tokens), lambda i: (i, 0, 0)),
        ],
        out_specs=[pl.BlockSpec((8, 16, WIDE), lambda i: (0, i, 0))] * 2,
        out_shape=[
            jax.ShapeDtypeStruct((8, rows * 8, WIDE), f32),
            jax.ShapeDtypeStruct((8, rows * 8, WIDE), bf16),
        ],
        scratch_shapes=[pltpu.VMEM((rows, tokens), f32)],
        compiler_params=params(16),
        name="attention",
    )(ctx, in_hbm(blocks), in_hbm(query), in_hbm(cache))


def side_kernel(
    ctx_ref, route_ref, gate_ref, iq_ref, iw_ref, keys_ref, _,
    score_ref, send_ref, pick_ref, back_ref, slot_ref,
):
    rows = iq_ref.shape[0]
    for r in range(rows):
        raw = dot(iq_ref[r], keys_ref[r], ((1,), (1,))) * (iq_ref.shape[2] ** (-0.5))
        score_ref[r : r + 1, :] = dot(iw_ref[r : r + 1, :], jnp.maximum(raw, 0.0), precision=HIGH)
    n = route_ref.shape[1]
    ctx = ctx_ref[0]
    n_ctx = n // 6
    names = route_ref[...]
    experts = [ctx, lax.rem(ctx + n_ctx - UP, n_ctx), lax.rem(ctx + DOWN, n_ctx)]
    hit = [jnp.max(jnp.where(names == g, 1.0, 0.0), axis=0, keepdims=True) for g in experts]
    upto = jnp.where(iota((n, n), 0) <= iota((n, n), 1), 1.0, 0.0).astype(bf16)
    hits = jnp.concatenate(hit + [jnp.zeros((8 - len(hit), n), f32)], axis=0)
    slots = dot(hits.astype(bf16), upto).astype(jnp.int32) - 1
    line, col = iota((8, n), 0), iota((8, n), 1)
    picks = []
    for j, g in enumerate(experts):
        picks.append(jnp.where((iota((CAP, n), 0) == slots[j : j + 1]) & (hit[j] > 0.0), 1.0, 0.0))
        own = jnp.where((col == 6 * g + line) & (line < 6), 1.0, 0.0)
        both = jnp.concatenate([picks[j], own], axis=0).astype(bf16)
        if j == 0:
            pick_ref[...] = both
        else:
            send_ref[j - 1] = both
    gate = jnp.sum(jnp.where(names == ctx, gate_ref[...], 0.0), axis=0, keepdims=True)
    row, col = iota((128, n), 0), iota((128, n), 1)
    spread = (row // 8 * 6 + row % 8 == col) & (row % 8 < 6)
    spread = jnp.where(spread, 1.0, 0.0).astype(bf16)
    back_ref[...] = dot(spread, picks[0].astype(bf16), ((1,), (1,))).astype(bf16)
    slot_ref[...] = jnp.broadcast_to(jnp.sum(picks[0] * gate, axis=1, keepdims=True), (CAP, 128))


def side(ctx, route, gate, iq, iw, keys, after):
    n = route.shape[1]
    return pl.pallas_call(
        side_kernel,
        in_specs=[SMEM] + [VMEM] * 5 + [ANY],
        out_specs=[VMEM] * 5,
        out_shape=[
            jax.ShapeDtypeStruct((iq.shape[0], keys.shape[1]), f32),
            jax.ShapeDtypeStruct((2, CAP + 8, n), bf16),
            jax.ShapeDtypeStruct((CAP + 8, n), bf16),
            jax.ShapeDtypeStruct((128, CAP), bf16),
            jax.ShapeDtypeStruct((CAP, 128), f32),
        ],
        compiler_params=params(),
        name="side",
    )(ctx, route, gate, iq, iw, keys, after)


def merge(parts):
    stats = [read_stats(x) for x in parts]
    peak = functools.reduce(jnp.maximum, [p for p, _ in stats])
    factors = [jnp.exp(p - peak) for p, _ in stats]
    total = sum(t * f for (_, t), f in zip(stats, factors))
    return peak, total, sum(x[:, :LAT] * f for x, f in zip(parts, factors))


def widen(peak, total, summed):
    return jnp.concatenate([summed, stats_tile(peak, total)], axis=1)


def pair_kernel(ctx_ref, mine_ref, other_ref, keep_ref, up_ref, down_ref):
    n = mine_ref.shape[0]
    z = ctx_ref[0] // 2
    for ref, offsets in ((up_ref, (1, 6, 3)), (down_ref, (7, 4)), (keep_ref, (0, 5, 2))):
        for i, offset in enumerate(offsets):
            there = lax.rem(z + offset, n)
            both = merge([mine_ref[there], other_ref[there].astype(f32)])
            ref[i] = widen(*both).astype(ref.dtype)


def pair(ctx, mine, other):
    rest = mine.shape[1:]
    return pl.pallas_call(
        pair_kernel,
        in_specs=[SMEM, VMEM, VMEM],
        out_specs=[VMEM] * 3,
        out_shape=[
            jax.ShapeDtypeStruct((3,) + rest, f32),
            jax.ShapeDtypeStruct((3,) + rest, bf16),
            jax.ShapeDtypeStruct((2,) + rest, bf16),
        ],
        compiler_params=params(),
        name="pair",
    )(ctx, mine, other)


def relay_kernel(keep_ref, below_ref, above_ref, up_ref, down_ref):
    down = merge([keep_ref[1], below_ref[1].astype(f32), above_ref[1].astype(f32)])
    down_ref[...] = widen(*down).astype(bf16)
    up_ref[...] = widen(*merge([keep_ref[2], below_ref[2].astype(f32)])).astype(bf16)


def relay(keep, below, above):
    return pl.pallas_call(
        relay_kernel,
        in_specs=[VMEM] * 3,
        out_specs=[VMEM] * 2,
        out_shape=[jax.ShapeDtypeStruct(keep.shape[1:], bf16)] * 2,
        compiler_params=params(),
        name="relay",
    )(keep, below, above)


def values_kernel(keep_ref, below_ref, above_ref, far_below_ref, far_above_ref, w_ref, _, out_ref):
    parts = [keep_ref[0], below_ref[0], above_ref[0], far_below_ref[...], far_above_ref[...]]
    _, total, summed = merge([x.astype(f32) for x in parts])
    lat = (summed / total).astype(bf16)
    rows = lat.shape[0]
    row, col = iota((64, rows), 0), iota((64, rows), 1)
    by_head = jnp.where((row % 8) * 8 + row // 8 == col, 1.0, 0.0).astype(bf16)
    lat = dot(by_head, lat)
    out = [dot(lat[8 * h : 8 * h + 8].astype(bf16), w_ref[h]) for h in range(8)]
    half = jnp.concatenate([jnp.concatenate(out[:4], axis=1), jnp.concatenate(out[4:], axis=1)], axis=0)
    half = half.astype(bf16)
    for e in range(out_ref.shape[0]):
        out_ref[e] = half


def values(parts, w_uv, after, n_exp):
    return pl.pallas_call(
        values_kernel,
        in_specs=[VMEM] * (len(parts) + 1) + [ANY],
        out_specs=VMEM,
        out_shape=jax.ShapeDtypeStruct((n_exp, 16, 512), bf16),
        compiler_params=params(),
        name="values",
    )(*parts, w_uv, after)


def project_kernel(values_ref, w_ref, out_ref, acc_ref):
    x = values_ref[...].astype(f32)
    n = x.shape[0]
    low = x[:, :8].reshape(n * 8, 512).astype(bf16)
    high = x[:, 8:].reshape(n * 8, 512).astype(bf16)
    acc = dot(low, w_ref[:, :512], ((1,), (1,))) + dot(high, w_ref[:, 512:], ((1,), (1,)))
    for e in range(n):
        acc_ref[6 * e : 6 * e + 6, :] = acc[8 * e : 8 * e + 6, :]
    out_ref[...] = acc_ref[...].astype(bf16)


def project(vals, w_o):
    shape = (vals.shape[0] * 6, w_o.shape[0])
    return pl.pallas_call(
        project_kernel,
        in_specs=[VMEM] * 2,
        out_specs=VMEM,
        out_shape=jax.ShapeDtypeStruct(shape, bf16),
        scratch_shapes=[pltpu.VMEM(shape, f32)],
        compiler_params=params(),
        name="project",
    )(vals, w_o)


def fold_kernel(own_ref, above_ref, below_ref, send_ref, up_ref, down_ref):
    two = own_ref[...].astype(f32) + below_ref[...].astype(f32)
    three = (two + above_ref[...].astype(f32)).astype(bf16)
    up_ref[...] = dot(send_ref[0], three).astype(bf16)
    down_ref[...] = dot(send_ref[1], two.astype(bf16)).astype(bf16)


def fold(own, above, below, send):
    shape = jax.ShapeDtypeStruct((send.shape[1], own.shape[1]), bf16)
    return pl.pallas_call(
        fold_kernel,
        in_specs=[VMEM] * 4,
        out_specs=[VMEM] * 2,
        out_shape=[shape, shape],
        compiler_params=params(),
        name="fold",
    )(own, above, below, send)


def base_kernel(own_ref, above_ref, below_ref, hidden_ref, pick_ref, w_hbm, out_ref, w_ref, sem):
    load = pltpu.make_async_copy(w_hbm, w_ref, sem)
    load.start()
    pick = pick_ref[...]
    near = dot(pick, own_ref[...]) + dot(pick, above_ref[...]) + dot(pick, below_ref[...])
    out_ref[...] = dot(pick, hidden_ref[...]) + near
    load.wait()


def base(own, above, below, hidden, pick, w_in):
    return pl.pallas_call(
        base_kernel,
        in_specs=[VMEM] * 5 + [HBM],
        out_specs=[VMEM] * 2,
        out_shape=[
            jax.ShapeDtypeStruct((pick.shape[0], own.shape[1]), f32),
            jax.ShapeDtypeStruct(w_in.shape, bf16),
        ],
        scratch_shapes=[pltpu.SemaphoreType.DMA],
        compiler_params=params(),
        name="base",
    )(own, above, below, hidden, pick, in_hbm(w_in))


def expert_in_kernel(near_ref, far_up_ref, far_down_ref, gain_ref, w_ref, out_ref, keep_ref):
    n = out_ref.shape[0]
    half = w_ref.shape[1] // 2
    attn = near_ref[...] + far_up_ref[...].astype(f32) + far_down_ref[...].astype(f32)
    resid32 = attn.astype(bf16).astype(f32)
    keep_ref[...] = resid32[CAP:]
    picked = resid32[:CAP]
    rows = (picked * gain_ref[...]).astype(bf16)
    squares = dot(jnp.ones((8, picked.shape[1]), f32), picked * picked, ((1,), (1,)), HIGH)
    hi, mid, low = split3(squares)
    line = iota(squares.shape, 0)
    parts = jnp.where(line == 0, hi, jnp.where(line == 1, mid, jnp.where(line == 2, low, 0.0)))
    parts = jnp.concatenate([parts, jnp.zeros((8, 256 - CAP), f32)], axis=1)
    for e in range(0, n, 2):
        gate = dot(rows, w_ref[:, 128 * e : 128 * e + 256])
        up = dot(rows, w_ref[:, half + 128 * e : half + 128 * e + 256])
        for i in range(2):
            here = slice(128 * i, 128 * i + 128)
            both = jnp.concatenate([gate[:, here], up[:, here]], axis=1)
            out_ref[e + i] = jnp.concatenate([both, parts], axis=0).astype(bf16)


def expert_in(near, far_up, far_down, gain, w_in, n_exp):
    width = near.shape[1]
    return pl.pallas_call(
        expert_in_kernel,
        in_specs=[VMEM] * 5,
        out_specs=[VMEM] * 2,
        out_shape=[
            jax.ShapeDtypeStruct((n_exp, CAP + 8, 256), bf16),
            jax.ShapeDtypeStruct((8, width), f32),
        ],
        compiler_params=params(),
        name="expert_in",
    )(near, far_up, far_down, gain, w_in)


def act_kernel(parts_ref, out_ref):
    x = jnp.sum(parts_ref[...].astype(f32), axis=0)
    line = x[CAP : CAP + 1, :CAP] + x[CAP + 1 : CAP + 2, :CAP] + x[CAP + 2 : CAP + 3, :CAP]
    diagonal = iota((CAP, CAP), 0) == iota((CAP, CAP), 1)
    squares = jnp.sum(jnp.where(diagonal, line, 0.0), axis=1, keepdims=True)
    inv = lax.rsqrt(squares / D + EPS)
    gate, up = x[:CAP, :128] * inv, x[:CAP, 128:] * inv
    act = (jax.nn.silu(gate) * up).astype(bf16)
    for e in range(out_ref.shape[0]):
        out_ref[e] = act


def activation(parts):
    return pl.pallas_call(
        act_kernel,
        in_specs=[VMEM],
        out_specs=VMEM,
        out_shape=jax.ShapeDtypeStruct((parts.shape[0], CAP, 128), bf16),
        compiler_params=params(),
        name="activation",
    )(parts)


def expert_out_kernel(act_ref, w_ref, slot_ref, back_ref, out_ref):
    act = jnp.concatenate([act_ref[e] for e in range(act_ref.shape[0])], axis=1)
    out = (dot(act, w_ref[...], ((1,), (1,))) * slot_ref[:, 0:1]).astype(bf16)
    back = dot(back_ref[...], out)
    n = out_ref.shape[0]
    low = back[:, :256].reshape(n, 8, 256)
    high = jnp.concatenate([back[:, 256:], jnp.zeros((n * 8, 64), f32)], axis=1).reshape(n, 8, 256)
    out_ref[...] = jnp.concatenate([low, high], axis=1).astype(bf16)


def expert_out(act, w_down, slot, back, n_ctx):
    return pl.pallas_call(
        expert_out_kernel,
        in_specs=[VMEM] * 4,
        out_specs=VMEM,
        out_shape=jax.ShapeDtypeStruct((n_ctx, 16, 256), bf16),
        compiler_params=params(),
        name="expert_out",
    )(act, w_down, slot, back)


def last_kernel(parts_ref, keep_ref, out_ref):
    x = jnp.sum(parts_ref[...].astype(f32), axis=0)
    moe = jnp.concatenate([x[:8], x[8:, :192]], axis=1)
    out_ref[...] = (keep_ref[...] + moe)[:6].astype(bf16)


def last(parts, keep):
    return pl.pallas_call(
        last_kernel,
        in_specs=[VMEM] * 2,
        out_specs=VMEM,
        out_shape=jax.ShapeDtypeStruct((6, keep.shape[1]), bf16),
        compiler_params=params(),
        name="last",
    )(parts, keep)


def local(
    cache, idx_keys, lat_query, idx_query, idx_weight, chosen_blocks, w_uv, w_o, hidden_in, norm_gain,
    route, route_weight, w_in, w_down,
):
    n_ctx, n_exp = lax.axis_size("ctx"), lax.axis_size("exp")
    ctx = lax.axis_index("ctx").astype(jnp.int32).reshape(1)
    other_core = [(i, i ^ 1) for i in range(n_ctx)]
    def along_z(shift):
        return [(i, (i + shift) % n_ctx) for i in range(n_ctx)]

    mine, other = attention(
        ctx, chosen_blocks, jnp.swapaxes(lat_query, 1, 2), jnp.swapaxes(cache, 1, 2)
    )
    other = lax.ppermute(other, "ctx", other_core)
    keep, up, down = pair(ctx, mine, other)
    below = lax.ppermute(up, "ctx", along_z(2))
    above = lax.ppermute(down, "ctx", along_z(-2))
    up, down = relay(keep, below, above)
    far_below = lax.ppermute(up, "ctx", along_z(DOWN))
    far_above = lax.ppermute(down, "ctx", along_z(-UP))
    index_scores, send, pick, back, slot = side(
        ctx, route.T, route_weight.T, idx_query, idx_weight, idx_keys, up
    )
    vals = values((keep, below, above, far_below, far_above), w_uv, send, n_exp)
    vals = lax.all_to_all(vals, "exp", 0, 0)
    part = project(vals, w_o.T)
    own = part.astype(f32) + lax.ppermute(part, "ctx", other_core).astype(f32)
    own = own.astype(bf16)
    above = lax.ppermute(own, "ctx", along_z(-2))
    below = lax.ppermute(own, "ctx", along_z(2))
    up, down = fold(own, above, below, send)
    far_up = lax.ppermute(up, "ctx", along_z(-UP))
    far_down = lax.ppermute(down, "ctx", along_z(DOWN))
    near, w_gate_up = base(own, above, below, hidden_in, pick, w_in[0])
    terms, keep = expert_in(near, far_up, far_down, norm_gain.reshape(1, -1), w_gate_up, n_exp)
    terms = lax.all_to_all(terms, "exp", 0, 0)
    act = lax.all_to_all(activation(terms), "exp", 0, 0)
    outs = expert_out(act, w_down[0].T, slot, back, n_ctx)
    outs = lax.all_to_all(outs, "ctx", 0, 0)
    return index_scores, last(outs, keep)


def solution(mesh):
    return jax.shard_map(
        local,
        mesh=mesh,
        in_specs=(
            P("exp", "ctx", None),
            P("exp", "ctx", None),
            P("exp", None, None),
            P("exp", None, None),
            P("exp", None),
            P("exp", None),
            P("ctx", None, None),
            P("ctx", "exp"),
            P(None, "exp"),
            P("exp"),
            P(),
            P(),
            P("ctx", "exp", None),
            P("ctx", None, "exp"),
        ),
        out_specs=(P("exp", "ctx"), P("ctx", "exp")),
        check_vma=False,
    )
```

```python
import functools

import jax
import jax.numpy as jnp
from jax import lax
from jax.experimental import pallas as pl
from jax.experimental.pallas import tpu as pltpu
from jax.sharding import PartitionSpec as P

f32 = jnp.float32
bf16 = jnp.bfloat16
D = 7168
BLOCK = 64
LAT = 512
WIDE = 640
CAP = 48
UP, DOWN = 6, 4
NEG = -1e30
SCORE_SCALE = 192.0 ** (-0.5)
EPS = 1e-06
HIGH = lax.Precision.HIGHEST
MB = 1 << 20

VMEM = pl.BlockSpec(memory_space=pltpu.VMEM)
SMEM = pl.BlockSpec(memory_space=pltpu.SMEM)
HBM = pl.BlockSpec(memory_space=pltpu.HBM)
ANY = pl.BlockSpec(memory_space=pl.ANY)


def in_hbm(x):
    return pltpu.with_memory_space_constraint(x, pltpu.HBM)


def params(mb=8):
    return pltpu.CompilerParams(vmem_limit_bytes=mb * MB)


def iota(shape, dim):
    return lax.broadcasted_iota(jnp.int32, shape, dim)


def dot(a, b, dims=((1,), (0,)), precision=None):
    return lax.dot_general(a, b, (dims, ((), ())), precision=precision, preferred_element_type=f32)


def split3(x):
    hi = x.astype(bf16).astype(f32)
    mid = (x - hi).astype(bf16).astype(f32)
    low = (x - hi - mid).astype(bf16).astype(f32)
    return hi, mid, low


def stats_tile(peak, total):
    lane = iota(peak.shape[:-1] + (128,), len(peak.shape) - 1)
    tile = jnp.zeros(peak.shape[:-1] + (128,), f32)
    for place, part in enumerate(split3(peak) + split3(total)):
        tile = jnp.where(lane == place, part, tile)
    return tile


def read_stats(x):
    tile = x[..., LAT:WIDE]
    lane = iota(tile.shape, len(tile.shape) - 1)
    peak = jnp.sum(jnp.where(lane < 3, tile, 0.0), axis=-1, keepdims=True)
    total = jnp.sum(jnp.where((lane >= 3) & (lane < 6), tile, 0.0), axis=-1, keepdims=True)
    return peak, total


def pack(x):
    n = x.shape[0]
    half = (n // 2 + 7) // 8 * 8
    ends = jnp.concatenate([x[:half, 384:], x[n - half :, 384:]], axis=1)
    return jnp.concatenate([x[:, :128], x[:, 128:256], x[:, 256:384], ends], axis=0)


def unpack(x, n):
    half = x.shape[0] - 3 * n
    ends = jnp.concatenate([x[3 * n :, :64], x[3 * n + 2 * half - n :, 64:]], axis=0)
    return jnp.concatenate([x[:n], x[n : 2 * n], x[2 * n : 3 * n], ends], axis=1)


def packed_lines(n):
    return 3 * n + (n // 2 + 7) // 8 * 8


def attention_kernel(
    ctx_ref, blocks_hbm, query_hbm, cache_hbm, mine_ref, other_ref, blocks_ref, query_ref, cache_ref, sems, sem
):
    rows, _, tokens = cache_ref.shape
    load_blocks = pltpu.make_async_copy(blocks_hbm, blocks_ref, sem)
    copies = [
        (
            pltpu.make_async_copy(query_hbm.at[r], query_ref.at[r], sems.at[0, r]),
            pltpu.make_async_copy(cache_hbm.at[r], cache_ref.at[r], sems.at[1, r]),
        )
        for r in range(rows)
    ]

    def start(r):
        for copy in copies[r]:
            copy.start()

    start(0)
    load_blocks.start()
    for r in range(1, 4):
        start(r)
    ctx = ctx_ref[0]
    core = lax.rem(ctx, 2)
    per = tokens // BLOCK
    mask = None
    for r in range(0, rows, 2):
        for i in range(r, r + 2):
            for copy in copies[i]:
                copy.wait()
            if i + 4 < rows:
                start(i + 4)
        if mask is None:
            load_blocks.wait()
            block_of = iota((rows, tokens), 1) // BLOCK
            mask = jnp.zeros((rows, tokens), f32)
            picked = blocks_ref[...]
            for b in range(per):
                hit = jnp.max(jnp.where(picked == ctx * per + b, 1.0, 0.0), axis=1, keepdims=True)
                mask = jnp.where(block_of == b, hit, mask)
        mine, other = [], []
        for i in range(r, r + 2):
            chosen = mask[i : i + 1, :] > 0.0
            keys = cache_ref[i]
            scores = dot(query_ref[i], keys, ((0,), (0,))) * SCORE_SCALE
            masked = jnp.where(chosen, scores, NEG)
            peak = jnp.max(masked, axis=1, keepdims=True)
            expo = jnp.where(chosen, jnp.exp(masked - peak), 0.0)
            total = jnp.sum(expo, axis=1, keepdims=True)
            weighted = dot(expo.astype(bf16), keys[:LAT], ((1,), (1,)))
            wide = jnp.concatenate([weighted, stats_tile(peak, total)], axis=1)
            wide = wide.reshape(8, 2, 8, WIDE)
            mine.append(jnp.where(core == 0, wide[:, 0], wide[:, 1]))
            other.append(jnp.where(core == 0, wide[:, 1], wide[:, 0]))
        mine_ref[:, 8 * r : 8 * r + 16, :] = jnp.concatenate(mine, axis=1)
        other_ref[:, 8 * r : 8 * r + 16, :] = jnp.concatenate(other, axis=1).astype(bf16)


def attention(ctx, blocks, query, cache):
    rows = query.shape[0]
    return pl.pallas_call(
        attention_kernel,
        in_specs=[SMEM, HBM, HBM, HBM],
        out_specs=[VMEM] * 2,
        out_shape=[
            jax.ShapeDtypeStruct((8, rows * 8, WIDE), f32),
            jax.ShapeDtypeStruct((8, rows * 8, WIDE), bf16),
        ],
        scratch_shapes=[
            pltpu.VMEM(blocks.shape, jnp.int32),
            pltpu.VMEM(query.shape, bf16),
            pltpu.VMEM(cache.shape, bf16),
            pltpu.SemaphoreType.DMA((2, rows)),
            pltpu.SemaphoreType.DMA,
        ],
        compiler_params=params(16),
        name="attention",
    )(ctx, in_hbm(blocks), in_hbm(query), in_hbm(cache))


def side_kernel(
    ctx_ref, route_ref, gate_ref, iq_ref, iw_ref, keys_ref, _,
    score_ref, send_ref, pick_ref, back_ref, slot_ref,
):
    rows = iq_ref.shape[0]
    for r in range(rows):
        raw = dot(iq_ref[r], keys_ref[r], ((1,), (1,))) * (iq_ref.shape[2] ** (-0.5))
        score_ref[r : r + 1, :] = dot(iw_ref[r : r + 1, :], jnp.maximum(raw, 0.0), precision=HIGH)
    n = route_ref.shape[1]
    ctx = ctx_ref[0]
    n_ctx = n // 6
    names = route_ref[...]
    experts = [ctx, lax.rem(ctx + n_ctx - UP, n_ctx), lax.rem(ctx + DOWN, n_ctx)]
    hit = [jnp.max(jnp.where(names == g, 1.0, 0.0), axis=0, keepdims=True) for g in experts]
    upto = jnp.where(iota((n, n), 0) <= iota((n, n), 1), 1.0, 0.0).astype(bf16)
    hits = jnp.concatenate(hit + [jnp.zeros((8 - len(hit), n), f32)], axis=0)
    slots = dot(hits.astype(bf16), upto).astype(jnp.int32) - 1
    line, col = iota((8, n), 0), iota((8, n), 1)
    picks = []
    for j, g in enumerate(experts):
        picks.append(jnp.where((iota((CAP, n), 0) == slots[j : j + 1]) & (hit[j] > 0.0), 1.0, 0.0))
        own = jnp.where((col == 6 * g + line) & (line < 6), 1.0, 0.0)
        both = jnp.concatenate([picks[j], own], axis=0).astype(bf16)
        if j == 0:
            pick_ref[...] = both
        else:
            send_ref[j - 1] = both
    gate = jnp.sum(jnp.where(names == ctx, gate_ref[...], 0.0), axis=0, keepdims=True)
    row, col = iota((128, n), 0), iota((128, n), 1)
    spread = (row // 8 * 6 + row % 8 == col) & (row % 8 < 6)
    spread = jnp.where(spread, 1.0, 0.0).astype(bf16)
    back_ref[...] = dot(spread, picks[0].astype(bf16), ((1,), (1,))).astype(bf16)
    slot_ref[...] = jnp.broadcast_to(jnp.sum(picks[0] * gate, axis=1, keepdims=True), (CAP, 128))


def side(ctx, route, gate, iq, iw, keys, after):
    n = route.shape[1]
    return pl.pallas_call(
        side_kernel,
        in_specs=[SMEM] + [VMEM] * 5 + [ANY],
        out_specs=[VMEM] * 5,
        out_shape=[
            jax.ShapeDtypeStruct((iq.shape[0], keys.shape[1]), f32),
            jax.ShapeDtypeStruct((2, CAP + 8, n), bf16),
            jax.ShapeDtypeStruct((CAP + 8, n), bf16),
            jax.ShapeDtypeStruct((128, CAP), bf16),
            jax.ShapeDtypeStruct((CAP, 128), f32),
        ],
        compiler_params=params(),
        name="side",
    )(ctx, route, gate, iq, iw, keys, after)


def merge(parts):
    stats = [read_stats(x) for x in parts]
    peak = functools.reduce(jnp.maximum, [p for p, _ in stats])
    factors = [jnp.exp(p - peak) for p, _ in stats]
    total = sum(t * f for (_, t), f in zip(stats, factors))
    return peak, total, sum(x[:, :LAT] * f for x, f in zip(parts, factors))


def widen(peak, total, summed):
    return jnp.concatenate([summed, stats_tile(peak, total)], axis=1)


def pair_kernel(ctx_ref, mine_ref, other_ref, keep_ref, up_ref, down_ref):
    n = mine_ref.shape[0]
    z = ctx_ref[0] // 2
    for ref, offsets in ((up_ref, (1, 6, 3)), (down_ref, (7, 4)), (keep_ref, (0, 5, 2))):
        for i, offset in enumerate(offsets):
            there = lax.rem(z + offset, n)
            both = merge([mine_ref[there], other_ref[there].astype(f32)])
            ref[i] = widen(*both).astype(ref.dtype)


def pair(ctx, mine, other):
    rest = mine.shape[1:]
    return pl.pallas_call(
        pair_kernel,
        in_specs=[SMEM, VMEM, VMEM],
        out_specs=[VMEM] * 3,
        out_shape=[
            jax.ShapeDtypeStruct((3,) + rest, f32),
            jax.ShapeDtypeStruct((3,) + rest, bf16),
            jax.ShapeDtypeStruct((2,) + rest, bf16),
        ],
        compiler_params=params(),
        name="pair",
    )(ctx, mine, other)


def relay_kernel(keep_ref, below_ref, above_ref, up_ref, down_ref):
    down = merge([keep_ref[1], below_ref[1].astype(f32), above_ref[1].astype(f32)])
    down_ref[...] = widen(*down).astype(bf16)
    up_ref[...] = widen(*merge([keep_ref[2], below_ref[2].astype(f32)])).astype(bf16)


def relay(keep, below, above):
    return pl.pallas_call(
        relay_kernel,
        in_specs=[VMEM] * 3,
        out_specs=[VMEM] * 2,
        out_shape=[jax.ShapeDtypeStruct(keep.shape[1:], bf16)] * 2,
        compiler_params=params(),
        name="relay",
    )(keep, below, above)


def values_kernel(keep_ref, below_ref, above_ref, far_below_ref, far_above_ref, w_ref, _, out_ref):
    parts = [keep_ref[0], below_ref[0], above_ref[0], far_below_ref[...], far_above_ref[...]]
    _, total, summed = merge([x.astype(f32) for x in parts])
    lat = (summed / total).astype(bf16)
    rows = lat.shape[0]
    row, col = iota((64, rows), 0), iota((64, rows), 1)
    by_head = jnp.where((row % 8) * 8 + row // 8 == col, 1.0, 0.0).astype(bf16)
    lat = dot(by_head, lat)
    out = [dot(lat[8 * h : 8 * h + 8].astype(bf16), w_ref[h]) for h in range(8)]
    half = jnp.concatenate([jnp.concatenate(out[:4], axis=1), jnp.concatenate(out[4:], axis=1)], axis=0)
    half = half.astype(bf16)
    for e in range(out_ref.shape[0]):
        out_ref[e] = half


def values(parts, w_uv, after, n_exp):
    return pl.pallas_call(
        values_kernel,
        in_specs=[VMEM] * (len(parts) + 1) + [ANY],
        out_specs=VMEM,
        out_shape=jax.ShapeDtypeStruct((n_exp, 16, 512), bf16),
        compiler_params=params(),
        name="values",
    )(*parts, w_uv, after)


def project_kernel(values_ref, w_ref, out_ref, acc_ref):
    x = values_ref[...].astype(f32)
    n = x.shape[0]
    low = x[:, :8].reshape(n * 8, 512).astype(bf16)
    high = x[:, 8:].reshape(n * 8, 512).astype(bf16)
    acc = dot(low, w_ref[:, :512], ((1,), (1,))) + dot(high, w_ref[:, 512:], ((1,), (1,)))
    for e in range(n):
        acc_ref[6 * e : 6 * e + 6, :] = acc[8 * e : 8 * e + 6, :]
    out_ref[...] = pack(acc_ref[...]).astype(bf16)


def project(vals, w_o):
    shape = (vals.shape[0] * 6, w_o.shape[0])
    return pl.pallas_call(
        project_kernel,
        in_specs=[VMEM] * 2,
        out_specs=VMEM,
        out_shape=jax.ShapeDtypeStruct((packed_lines(shape[0]), 128), bf16),
        scratch_shapes=[pltpu.VMEM(shape, f32)],
        compiler_params=params(),
        name="project",
    )(vals, w_o)


def fold_kernel(own_ref, above_ref, below_ref, send_ref, up_ref, down_ref):
    n = send_ref.shape[2]
    two = own_ref[...].astype(f32) + below_ref[...].astype(f32)
    three = two + above_ref[...].astype(f32)
    up_ref[...] = pack(dot(send_ref[0], unpack(three, n).astype(bf16))).astype(bf16)
    down_ref[...] = pack(dot(send_ref[1], unpack(two, n).astype(bf16))).astype(bf16)


def fold(own, above, below, send):
    shape = jax.ShapeDtypeStruct((packed_lines(send.shape[1]), 128), bf16)
    return pl.pallas_call(
        fold_kernel,
        in_specs=[VMEM] * 4,
        out_specs=[VMEM] * 2,
        out_shape=[shape, shape],
        compiler_params=params(),
        name="fold",
    )(own, above, below, send)


def base_kernel(own_ref, above_ref, below_ref, hidden_ref, pick_ref, w_hbm, out_ref, w_ref, sem):
    load = pltpu.make_async_copy(w_hbm, w_ref, sem)
    load.start()
    pick = pick_ref[...]
    n = pick.shape[1]
    near = sum(
        dot(pick, unpack(ref[...].astype(f32), n).astype(bf16)) for ref in (own_ref, above_ref, below_ref)
    )
    out_ref[...] = dot(pick, hidden_ref[...]) + near
    load.wait()


def base(own, above, below, hidden, pick, w_in):
    return pl.pallas_call(
        base_kernel,
        in_specs=[VMEM] * 5 + [HBM],
        out_specs=[VMEM] * 2,
        out_shape=[
            jax.ShapeDtypeStruct((pick.shape[0], hidden.shape[1]), f32),
            jax.ShapeDtypeStruct(w_in.shape, bf16),
        ],
        scratch_shapes=[pltpu.SemaphoreType.DMA],
        compiler_params=params(),
        name="base",
    )(own, above, below, hidden, pick, in_hbm(w_in))


def expert_in_kernel(near_ref, far_up_ref, far_down_ref, gain_ref, w_ref, out_ref, keep_ref):
    n = out_ref.shape[0]
    half = w_ref.shape[1] // 2
    far = far_up_ref[...].astype(f32) + far_down_ref[...].astype(f32)
    attn = near_ref[...] + unpack(far, near_ref.shape[0])
    resid32 = attn.astype(bf16).astype(f32)
    keep_ref[...] = resid32[CAP:]
    picked = resid32[:CAP]
    rows = (picked * gain_ref[...]).astype(bf16)
    squares = dot(jnp.ones((8, picked.shape[1]), f32), picked * picked, ((1,), (1,)), HIGH)
    hi, mid, low = split3(squares)
    line = iota(squares.shape, 0)
    parts = jnp.where(line == 0, hi, jnp.where(line == 1, mid, jnp.where(line == 2, low, 0.0)))
    parts = jnp.concatenate([parts, jnp.zeros((8, 256 - CAP), f32)], axis=1)
    for e in range(0, n, 2):
        gate = dot(rows, w_ref[:, 128 * e : 128 * e + 256])
        up = dot(rows, w_ref[:, half + 128 * e : half + 128 * e + 256])
        for i in range(2):
            here = slice(128 * i, 128 * i + 128)
            both = jnp.concatenate([gate[:, here], up[:, here]], axis=1)
            out_ref[e + i] = jnp.concatenate([both, parts], axis=0).astype(bf16)


def expert_in(near, far_up, far_down, gain, w_in, n_exp):
    width = near.shape[1]
    return pl.pallas_call(
        expert_in_kernel,
        in_specs=[VMEM] * 5,
        out_specs=[VMEM] * 2,
        out_shape=[
            jax.ShapeDtypeStruct((n_exp, CAP + 8, 256), bf16),
            jax.ShapeDtypeStruct((8, width), f32),
        ],
        compiler_params=params(),
        name="expert_in",
    )(near, far_up, far_down, gain, w_in)


def act_kernel(parts_ref, out_ref):
    x = jnp.sum(parts_ref[...].astype(f32), axis=0)
    line = x[CAP : CAP + 1, :CAP] + x[CAP + 1 : CAP + 2, :CAP] + x[CAP + 2 : CAP + 3, :CAP]
    diagonal = iota((CAP, CAP), 0) == iota((CAP, CAP), 1)
    squares = jnp.sum(jnp.where(diagonal, line, 0.0), axis=1, keepdims=True)
    inv = lax.rsqrt(squares / D + EPS)
    gate, up = x[:CAP, :128] * inv, x[:CAP, 128:] * inv
    act = (jax.nn.silu(gate) * up).astype(bf16)
    for e in range(out_ref.shape[0]):
        out_ref[e] = act


def activation(parts):
    return pl.pallas_call(
        act_kernel,
        in_specs=[VMEM],
        out_specs=VMEM,
        out_shape=jax.ShapeDtypeStruct((parts.shape[0], CAP, 128), bf16),
        compiler_params=params(),
        name="activation",
    )(parts)


def expert_out_kernel(act_ref, w_ref, slot_ref, back_ref, out_ref):
    act = jnp.concatenate([act_ref[e] for e in range(act_ref.shape[0])], axis=1)
    out = (dot(act, w_ref[...], ((1,), (1,))) * slot_ref[:, 0:1]).astype(bf16)
    back = dot(back_ref[...], out)
    n = out_ref.shape[0]
    low = back[:, :256].reshape(n, 8, 256)
    high = jnp.concatenate([back[:, 256:], jnp.zeros((n * 8, 64), f32)], axis=1).reshape(n, 8, 256)
    out_ref[...] = jnp.concatenate([low, high], axis=1).astype(bf16)


def expert_out(act, w_down, slot, back, n_ctx):
    return pl.pallas_call(
        expert_out_kernel,
        in_specs=[VMEM] * 4,
        out_specs=VMEM,
        out_shape=jax.ShapeDtypeStruct((n_ctx, 16, 256), bf16),
        compiler_params=params(),
        name="expert_out",
    )(act, w_down, slot, back)


def last_kernel(parts_ref, keep_ref, out_ref):
    x = jnp.sum(parts_ref[...].astype(f32), axis=0)
    moe = jnp.concatenate([x[:8], x[8:, :192]], axis=1)
    out_ref[...] = (keep_ref[...] + moe)[:6].astype(bf16)


def last(parts, keep):
    return pl.pallas_call(
        last_kernel,
        in_specs=[VMEM] * 2,
        out_specs=VMEM,
        out_shape=jax.ShapeDtypeStruct((6, keep.shape[1]), bf16),
        compiler_params=params(),
        name="last",
    )(parts, keep)


def local(
    cache, idx_keys, lat_query, idx_query, idx_weight, chosen_blocks, w_uv, w_o, hidden_in, norm_gain,
    route, route_weight, w_in, w_down,
):
    n_ctx, n_exp = lax.axis_size("ctx"), lax.axis_size("exp")
    ctx = lax.axis_index("ctx").astype(jnp.int32).reshape(1)
    other_core = [(i, i ^ 1) for i in range(n_ctx)]
    def along_z(shift):
        return [(i, (i + shift) % n_ctx) for i in range(n_ctx)]

    mine, other = attention(
        ctx, chosen_blocks, jnp.swapaxes(lat_query, 1, 2), jnp.swapaxes(cache, 1, 2)
    )
    other = lax.ppermute(other, "ctx", other_core)
    keep, up, down = pair(ctx, mine, other)
    below = lax.ppermute(up, "ctx", along_z(2))
    above = lax.ppermute(down, "ctx", along_z(-2))
    up, down = relay(keep, below, above)
    far_below = lax.ppermute(up, "ctx", along_z(DOWN))
    far_above = lax.ppermute(down, "ctx", along_z(-UP))
    index_scores, send, pick, back, slot = side(
        ctx, route.T, route_weight.T, idx_query, idx_weight, idx_keys, up
    )
    vals = values((keep, below, above, far_below, far_above), w_uv, send, n_exp)
    vals = lax.all_to_all(vals, "exp", 0, 0)
    part = project(vals, w_o.T)
    own = part.astype(f32) + lax.ppermute(part, "ctx", other_core).astype(f32)
    own = own.astype(bf16)
    above = lax.ppermute(own, "ctx", along_z(-2))
    below = lax.ppermute(own, "ctx", along_z(2))
    up, down = fold(own, above, below, send)
    far_up = lax.ppermute(up, "ctx", along_z(-UP))
    far_down = lax.ppermute(down, "ctx", along_z(DOWN))
    near, w_gate_up = base(own, above, below, hidden_in, pick, w_in[0])
    terms, keep = expert_in(near, far_up, far_down, norm_gain.reshape(1, -1), w_gate_up, n_exp)
    terms = lax.all_to_all(terms, "exp", 0, 0)
    act = lax.all_to_all(activation(terms), "exp", 0, 0)
    outs = expert_out(act, w_down[0].T, slot, back, n_ctx)
    outs = lax.all_to_all(outs, "ctx", 0, 0)
    return index_scores, last(outs, keep)


def solution(mesh):
    return jax.shard_map(
        local,
        mesh=mesh,
        in_specs=(
            P("exp", "ctx", None),
            P("exp", "ctx", None),
            P("exp", None, None),
            P("exp", None, None),
            P("exp", None),
            P("exp", None),
            P("ctx", None, None),
            P("ctx", "exp"),
            P(None, "exp"),
            P("exp"),
            P(),
            P(),
            P("ctx", "exp", None),
            P("ctx", None, "exp"),
        ),
        out_specs=(P("exp", "ctx"), P("ctx", "exp")),
        check_vma=False,
    )
```

```python
import functools

import jax
import jax.numpy as jnp
from jax import lax
from jax.experimental import pallas as pl
from jax.experimental.pallas import tpu as pltpu
from jax.sharding import PartitionSpec as P

f32 = jnp.float32
bf16 = jnp.bfloat16
D = 7168
BLOCK = 64
LAT = 512
WIDE = 640
CAP = 48
UP, DOWN = 6, 4
NEG = -1e30
SCORE_SCALE = 192.0 ** (-0.5)
EPS = 1e-06
HIGH = lax.Precision.HIGHEST
MB = 1 << 20

VMEM = pl.BlockSpec(memory_space=pltpu.VMEM)
SMEM = pl.BlockSpec(memory_space=pltpu.SMEM)
HBM = pl.BlockSpec(memory_space=pltpu.HBM)
ANY = pl.BlockSpec(memory_space=pl.ANY)


def in_hbm(x):
    return pltpu.with_memory_space_constraint(x, pltpu.HBM)


def params(mb=8):
    return pltpu.CompilerParams(vmem_limit_bytes=mb * MB)


def iota(shape, dim):
    return lax.broadcasted_iota(jnp.int32, shape, dim)


def dot(a, b, dims=((1,), (0,)), precision=None):
    return lax.dot_general(a, b, (dims, ((), ())), precision=precision, preferred_element_type=f32)


def split3(x):
    hi = x.astype(bf16).astype(f32)
    mid = (x - hi).astype(bf16).astype(f32)
    low = (x - hi - mid).astype(bf16).astype(f32)
    return hi, mid, low


def stats_tile(peak, total):
    lane = iota(peak.shape[:-1] + (128,), len(peak.shape) - 1)
    tile = jnp.zeros(peak.shape[:-1] + (128,), f32)
    for place, part in enumerate(split3(peak) + split3(total)):
        tile = jnp.where(lane == place, part, tile)
    return tile


def read_stats(x):
    tile = x[..., LAT:WIDE]
    lane = iota(tile.shape, len(tile.shape) - 1)
    peak = jnp.sum(jnp.where(lane < 3, tile, 0.0), axis=-1, keepdims=True)
    total = jnp.sum(jnp.where((lane >= 3) & (lane < 6), tile, 0.0), axis=-1, keepdims=True)
    return peak, total


def pack(x):
    n = x.shape[0]
    half = (n // 2 + 7) // 8 * 8
    ends = jnp.concatenate([x[:half, 384:], x[n - half :, 384:]], axis=1)
    return jnp.concatenate([x[:, :128], x[:, 128:256], x[:, 256:384], ends], axis=0)


def unpack(x, n):
    half = x.shape[0] - 3 * n
    ends = jnp.concatenate([x[3 * n :, :64], x[3 * n + 2 * half - n :, 64:]], axis=0)
    return jnp.concatenate([x[:n], x[n : 2 * n], x[2 * n : 3 * n], ends], axis=1)


def packed_lines(n):
    return 3 * n + (n // 2 + 7) // 8 * 8


def attention_kernel(
    ctx_ref, blocks_hbm, query_hbm, cache_hbm, mine_ref, other_ref, blocks_ref, query_ref, cache_ref, sems, sem
):
    rows, _, tokens = cache_ref.shape
    load_blocks = pltpu.make_async_copy(blocks_hbm, blocks_ref, sem)
    copies = [
        (
            pltpu.make_async_copy(query_hbm.at[r], query_ref.at[r], sems.at[0, r]),
            pltpu.make_async_copy(cache_hbm.at[r], cache_ref.at[r], sems.at[1, r]),
        )
        for r in range(rows)
    ]

    def start(r):
        for copy in copies[r]:
            copy.start()

    start(0)
    load_blocks.start()
    for r in range(1, 3):
        start(r)
    ctx = ctx_ref[0]
    core = lax.rem(ctx, 2)
    per = tokens // BLOCK

    def scores_of(i):
        for copy in copies[i]:
            copy.wait()
        if i + 3 < rows:
            start(i + 3)
        return dot(query_ref[i], cache_ref[i], ((0,), (0,))) * SCORE_SCALE

    def partial(i, scores, mask):
        chosen = mask[i : i + 1, :] > 0.0
        masked = jnp.where(chosen, scores, NEG)
        peak = jnp.max(masked, axis=1, keepdims=True)
        expo = jnp.where(chosen, jnp.exp(masked - peak), 0.0)
        total = jnp.sum(expo, axis=1, keepdims=True)
        weighted = dot(expo.astype(bf16), cache_ref[i, :LAT], ((1,), (1,)))
        wide = jnp.concatenate([weighted, stats_tile(peak, total)], axis=1).reshape(8, 2, 8, WIDE)
        return jnp.where(core == 0, wide[:, 0], wide[:, 1]), jnp.where(core == 0, wide[:, 1], wide[:, 0])

    scores = scores_of(0)
    load_blocks.wait()
    block_of = iota((rows, tokens), 1) // BLOCK
    mask = jnp.zeros((rows, tokens), f32)
    picked = blocks_ref[...]
    for b in range(per):
        hit = jnp.max(jnp.where(picked == ctx * per + b, 1.0, 0.0), axis=1, keepdims=True)
        mask = jnp.where(block_of == b, hit, mask)
    for i in range(rows):
        later = scores_of(i + 1) if i + 1 < rows else None
        mine, other = partial(i, scores, mask)
        if i % 2 == 0:
            mine_even, other_even = mine, other
        else:
            lines = slice(8 * i - 8, 8 * i + 8)
            mine_ref[:, lines, :] = jnp.concatenate([mine_even, mine], axis=1)
            other_ref[:, lines, :] = jnp.concatenate([other_even, other], axis=1).astype(bf16)
        scores = later


def attention(ctx, blocks, query, cache):
    rows = query.shape[0]
    return pl.pallas_call(
        attention_kernel,
        in_specs=[SMEM, HBM, HBM, HBM],
        out_specs=[VMEM] * 2,
        out_shape=[
            jax.ShapeDtypeStruct((8, rows * 8, WIDE), f32),
            jax.ShapeDtypeStruct((8, rows * 8, WIDE), bf16),
        ],
        scratch_shapes=[
            pltpu.VMEM(blocks.shape, jnp.int32),
            pltpu.VMEM(query.shape, bf16),
            pltpu.VMEM(cache.shape, bf16),
            pltpu.SemaphoreType.DMA((2, rows)),
            pltpu.SemaphoreType.DMA,
        ],
        compiler_params=params(16),
        name="attention",
    )(ctx, in_hbm(blocks), in_hbm(query), in_hbm(cache))


def side_kernel(
    ctx_ref, route_ref, gate_ref, iq_ref, iw_ref, keys_ref, _,
    score_ref, send_ref, pick_ref, back_ref, slot_ref,
):
    rows = iq_ref.shape[0]
    for r in range(rows):
        raw = dot(iq_ref[r], keys_ref[r], ((1,), (1,))) * (iq_ref.shape[2] ** (-0.5))
        score_ref[r : r + 1, :] = dot(iw_ref[r : r + 1, :], jnp.maximum(raw, 0.0), precision=HIGH)
    n = route_ref.shape[1]
    ctx = ctx_ref[0]
    n_ctx = n // 6
    names = route_ref[...]
    experts = [ctx, lax.rem(ctx + n_ctx - UP, n_ctx), lax.rem(ctx + DOWN, n_ctx)]
    hit = [jnp.max(jnp.where(names == g, 1.0, 0.0), axis=0, keepdims=True) for g in experts]
    upto = jnp.where(iota((n, n), 0) <= iota((n, n), 1), 1.0, 0.0).astype(bf16)
    hits = jnp.concatenate(hit + [jnp.zeros((8 - len(hit), n), f32)], axis=0)
    slots = dot(hits.astype(bf16), upto).astype(jnp.int32) - 1
    line, col = iota((8, n), 0), iota((8, n), 1)
    picks = []
    for j, g in enumerate(experts):
        picks.append(jnp.where((iota((CAP, n), 0) == slots[j : j + 1]) & (hit[j] > 0.0), 1.0, 0.0))
        own = jnp.where((col == 6 * g + line) & (line < 6), 1.0, 0.0)
        both = jnp.concatenate([picks[j], own], axis=0).astype(bf16)
        if j == 0:
            pick_ref[...] = both
        else:
            send_ref[j - 1] = both
    gate = jnp.sum(jnp.where(names == ctx, gate_ref[...], 0.0), axis=0, keepdims=True)
    row, col = iota((128, n), 0), iota((128, n), 1)
    spread = (row // 8 * 6 + row % 8 == col) & (row % 8 < 6)
    spread = jnp.where(spread, 1.0, 0.0).astype(bf16)
    back_ref[...] = dot(spread, picks[0].astype(bf16), ((1,), (1,))).astype(bf16)
    slot_ref[...] = jnp.broadcast_to(jnp.sum(picks[0] * gate, axis=1, keepdims=True), (CAP, 128))


def side(ctx, route, gate, iq, iw, keys, after):
    n = route.shape[1]
    return pl.pallas_call(
        side_kernel,
        in_specs=[SMEM] + [VMEM] * 5 + [ANY],
        out_specs=[VMEM] * 5,
        out_shape=[
            jax.ShapeDtypeStruct((iq.shape[0], keys.shape[1]), f32),
            jax.ShapeDtypeStruct((2, CAP + 8, n), bf16),
            jax.ShapeDtypeStruct((CAP + 8, n), bf16),
            jax.ShapeDtypeStruct((128, CAP), bf16),
            jax.ShapeDtypeStruct((CAP, 128), f32),
        ],
        compiler_params=params(),
        name="side",
    )(ctx, route, gate, iq, iw, keys, after)


def merge(parts):
    stats = [read_stats(x) for x in parts]
    peak = functools.reduce(jnp.maximum, [p for p, _ in stats])
    factors = [jnp.exp(p - peak) for p, _ in stats]
    total = sum(t * f for (_, t), f in zip(stats, factors))
    return peak, total, sum(x[:, :LAT] * f for x, f in zip(parts, factors))


def widen(peak, total, summed):
    return jnp.concatenate([summed, stats_tile(peak, total)], axis=1)


def pair_kernel(ctx_ref, mine_ref, other_ref, keep_ref, up_ref, down_ref):
    n = mine_ref.shape[0]
    z = ctx_ref[0] // 2
    for ref, offsets in ((up_ref, (1, 6, 3)), (down_ref, (7, 4)), (keep_ref, (0, 5, 2))):
        for i, offset in enumerate(offsets):
            there = lax.rem(z + offset, n)
            both = merge([mine_ref[there], other_ref[there].astype(f32)])
            ref[i] = widen(*both).astype(ref.dtype)


def pair(ctx, mine, other):
    rest = mine.shape[1:]
    return pl.pallas_call(
        pair_kernel,
        in_specs=[SMEM, VMEM, VMEM],
        out_specs=[VMEM] * 3,
        out_shape=[
            jax.ShapeDtypeStruct((3,) + rest, f32),
            jax.ShapeDtypeStruct((3,) + rest, bf16),
            jax.ShapeDtypeStruct((2,) + rest, bf16),
        ],
        compiler_params=params(),
        name="pair",
    )(ctx, mine, other)


def relay_kernel(keep_ref, below_ref, above_ref, up_ref, down_ref):
    down = merge([keep_ref[1], below_ref[1].astype(f32), above_ref[1].astype(f32)])
    down_ref[...] = widen(*down).astype(bf16)
    up_ref[...] = widen(*merge([keep_ref[2], below_ref[2].astype(f32)])).astype(bf16)


def relay(keep, below, above):
    return pl.pallas_call(
        relay_kernel,
        in_specs=[VMEM] * 3,
        out_specs=[VMEM] * 2,
        out_shape=[jax.ShapeDtypeStruct(keep.shape[1:], bf16)] * 2,
        compiler_params=params(),
        name="relay",
    )(keep, below, above)


def values_kernel(keep_ref, below_ref, above_ref, far_below_ref, far_above_ref, w_ref, _, out_ref):
    parts = [keep_ref[0], below_ref[0], above_ref[0], far_below_ref[...], far_above_ref[...]]
    _, total, summed = merge([x.astype(f32) for x in parts])
    lat = (summed / total).astype(bf16)
    rows = lat.shape[0]
    row, col = iota((64, rows), 0), iota((64, rows), 1)
    by_head = jnp.where((row % 8) * 8 + row // 8 == col, 1.0, 0.0).astype(bf16)
    lat = dot(by_head, lat)
    out = [dot(lat[8 * h : 8 * h + 8].astype(bf16), w_ref[h]) for h in range(8)]
    half = jnp.concatenate([jnp.concatenate(out[:4], axis=1), jnp.concatenate(out[4:], axis=1)], axis=0)
    half = half.astype(bf16)
    for e in range(out_ref.shape[0]):
        out_ref[e] = half


def values(parts, w_uv, after, n_exp):
    return pl.pallas_call(
        values_kernel,
        in_specs=[VMEM] * (len(parts) + 1) + [ANY],
        out_specs=VMEM,
        out_shape=jax.ShapeDtypeStruct((n_exp, 16, 512), bf16),
        compiler_params=params(),
        name="values",
    )(*parts, w_uv, after)


def project_kernel(values_ref, w_ref, out_ref, acc_ref):
    x = values_ref[...].astype(f32)
    n = x.shape[0]
    low = x[:, :8].reshape(n * 8, 512).astype(bf16)
    high = x[:, 8:].reshape(n * 8, 512).astype(bf16)
    acc = dot(low, w_ref[:, :512], ((1,), (1,))) + dot(high, w_ref[:, 512:], ((1,), (1,)))
    for e in range(n):
        acc_ref[6 * e : 6 * e + 6, :] = acc[8 * e : 8 * e + 6, :]
    out_ref[...] = pack(acc_ref[...]).astype(bf16)


def project(vals, w_o):
    shape = (vals.shape[0] * 6, w_o.shape[0])
    return pl.pallas_call(
        project_kernel,
        in_specs=[VMEM] * 2,
        out_specs=VMEM,
        out_shape=jax.ShapeDtypeStruct((packed_lines(shape[0]), 128), bf16),
        scratch_shapes=[pltpu.VMEM(shape, f32)],
        compiler_params=params(),
        name="project",
    )(vals, w_o)


def fold_kernel(own_ref, above_ref, below_ref, send_ref, up_ref, down_ref):
    n = send_ref.shape[2]
    two = own_ref[...].astype(f32) + below_ref[...].astype(f32)
    three = two + above_ref[...].astype(f32)
    up_ref[...] = pack(dot(send_ref[0], unpack(three, n).astype(bf16))).astype(bf16)
    down_ref[...] = pack(dot(send_ref[1], unpack(two, n).astype(bf16))).astype(bf16)


def fold(own, above, below, send):
    shape = jax.ShapeDtypeStruct((packed_lines(send.shape[1]), 128), bf16)
    return pl.pallas_call(
        fold_kernel,
        in_specs=[VMEM] * 4,
        out_specs=[VMEM] * 2,
        out_shape=[shape, shape],
        compiler_params=params(),
        name="fold",
    )(own, above, below, send)


def base_kernel(own_ref, above_ref, below_ref, hidden_ref, pick_ref, w_hbm, out_ref, w_ref, sem):
    load = pltpu.make_async_copy(w_hbm, w_ref, sem)
    load.start()
    pick = pick_ref[...]
    n = pick.shape[1]
    near = sum(
        dot(pick, unpack(ref[...].astype(f32), n).astype(bf16)) for ref in (own_ref, above_ref, below_ref)
    )
    out_ref[...] = dot(pick, hidden_ref[...]) + near
    load.wait()


def base(own, above, below, hidden, pick, w_in):
    return pl.pallas_call(
        base_kernel,
        in_specs=[VMEM] * 5 + [HBM],
        out_specs=[VMEM] * 2,
        out_shape=[
            jax.ShapeDtypeStruct((pick.shape[0], hidden.shape[1]), f32),
            jax.ShapeDtypeStruct(w_in.shape, bf16),
        ],
        scratch_shapes=[pltpu.SemaphoreType.DMA],
        compiler_params=params(),
        name="base",
    )(own, above, below, hidden, pick, in_hbm(w_in))


def expert_in_kernel(near_ref, far_up_ref, far_down_ref, gain_ref, w_ref, out_ref, keep_ref):
    n = out_ref.shape[0]
    half = w_ref.shape[1] // 2
    far = far_up_ref[...].astype(f32) + far_down_ref[...].astype(f32)
    attn = near_ref[...] + unpack(far, near_ref.shape[0])
    resid32 = attn.astype(bf16).astype(f32)
    keep_ref[...] = resid32[CAP:]
    picked = resid32[:CAP]
    rows = (picked * gain_ref[...]).astype(bf16)
    squares = dot(jnp.ones((8, picked.shape[1]), f32), picked * picked, ((1,), (1,)), HIGH)
    hi, mid, low = split3(squares)
    line = iota(squares.shape, 0)
    parts = jnp.where(line == 0, hi, jnp.where(line == 1, mid, jnp.where(line == 2, low, 0.0)))
    parts = jnp.concatenate([parts, jnp.zeros((8, 256 - CAP), f32)], axis=1)
    for e in range(0, n, 2):
        gate = dot(rows, w_ref[:, 128 * e : 128 * e + 256])
        up = dot(rows, w_ref[:, half + 128 * e : half + 128 * e + 256])
        for i in range(2):
            here = slice(128 * i, 128 * i + 128)
            both = jnp.concatenate([gate[:, here], up[:, here]], axis=1)
            out_ref[e + i] = jnp.concatenate([both, parts], axis=0).astype(bf16)


def expert_in(near, far_up, far_down, gain, w_in, n_exp):
    width = near.shape[1]
    return pl.pallas_call(
        expert_in_kernel,
        in_specs=[VMEM] * 5,
        out_specs=[VMEM] * 2,
        out_shape=[
            jax.ShapeDtypeStruct((n_exp, CAP + 8, 256), bf16),
            jax.ShapeDtypeStruct((8, width), f32),
        ],
        compiler_params=params(),
        name="expert_in",
    )(near, far_up, far_down, gain, w_in)


def act_kernel(parts_ref, out_ref):
    x = jnp.sum(parts_ref[...].astype(f32), axis=0)
    line = x[CAP : CAP + 1, :CAP] + x[CAP + 1 : CAP + 2, :CAP] + x[CAP + 2 : CAP + 3, :CAP]
    diagonal = iota((CAP, CAP), 0) == iota((CAP, CAP), 1)
    squares = jnp.sum(jnp.where(diagonal, line, 0.0), axis=1, keepdims=True)
    inv = lax.rsqrt(squares / D + EPS)
    gate, up = x[:CAP, :128] * inv, x[:CAP, 128:] * inv
    act = (jax.nn.silu(gate) * up).astype(bf16)
    for e in range(out_ref.shape[0]):
        out_ref[e] = act


def activation(parts):
    return pl.pallas_call(
        act_kernel,
        in_specs=[VMEM],
        out_specs=VMEM,
        out_shape=jax.ShapeDtypeStruct((parts.shape[0], CAP, 128), bf16),
        compiler_params=params(),
        name="activation",
    )(parts)


def expert_out_kernel(act_ref, w_ref, slot_ref, back_ref, out_ref):
    act = jnp.concatenate([act_ref[e] for e in range(act_ref.shape[0])], axis=1)
    out = (dot(act, w_ref[...], ((1,), (1,))) * slot_ref[:, 0:1]).astype(bf16)
    back = dot(back_ref[...], out)
    n = out_ref.shape[0]
    low = back[:, :256].reshape(n, 8, 256)
    high = jnp.concatenate([back[:, 256:], jnp.zeros((n * 8, 64), f32)], axis=1).reshape(n, 8, 256)
    out_ref[...] = jnp.concatenate([low, high], axis=1).astype(bf16)


def expert_out(act, w_down, slot, back, n_ctx):
    return pl.pallas_call(
        expert_out_kernel,
        in_specs=[VMEM] * 4,
        out_specs=VMEM,
        out_shape=jax.ShapeDtypeStruct((n_ctx, 16, 256), bf16),
        compiler_params=params(),
        name="expert_out",
    )(act, w_down, slot, back)


def last_kernel(parts_ref, keep_ref, out_ref):
    x = jnp.sum(parts_ref[...].astype(f32), axis=0)
    moe = jnp.concatenate([x[:8], x[8:, :192]], axis=1)
    out_ref[...] = (keep_ref[...] + moe)[:6].astype(bf16)


def last(parts, keep):
    return pl.pallas_call(
        last_kernel,
        in_specs=[VMEM] * 2,
        out_specs=VMEM,
        out_shape=jax.ShapeDtypeStruct((6, keep.shape[1]), bf16),
        compiler_params=params(),
        name="last",
    )(parts, keep)


def local(
    cache, idx_keys, lat_query, idx_query, idx_weight, chosen_blocks, w_uv, w_o, hidden_in, norm_gain,
    route, route_weight, w_in, w_down,
):
    n_ctx, n_exp = lax.axis_size("ctx"), lax.axis_size("exp")
    ctx = lax.axis_index("ctx").astype(jnp.int32).reshape(1)
    other_core = [(i, i ^ 1) for i in range(n_ctx)]
    def along_z(shift):
        return [(i, (i + shift) % n_ctx) for i in range(n_ctx)]

    mine, other = attention(
        ctx, chosen_blocks, jnp.swapaxes(lat_query, 1, 2), jnp.swapaxes(cache, 1, 2)
    )
    other = lax.ppermute(other, "ctx", other_core)
    keep, up, down = pair(ctx, mine, other)
    below = lax.ppermute(up, "ctx", along_z(2))
    above = lax.ppermute(down, "ctx", along_z(-2))
    up, down = relay(keep, below, above)
    far_below = lax.ppermute(up, "ctx", along_z(DOWN))
    far_above = lax.ppermute(down, "ctx", along_z(-UP))
    index_scores, send, pick, back, slot = side(
        ctx, route.T, route_weight.T, idx_query, idx_weight, idx_keys, up
    )
    vals = values((keep, below, above, far_below, far_above), w_uv, send, n_exp)
    vals = lax.all_to_all(vals, "exp", 0, 0)
    part = project(vals, w_o.T)
    own = part.astype(f32) + lax.ppermute(part, "ctx", other_core).astype(f32)
    own = own.astype(bf16)
    above = lax.ppermute(own, "ctx", along_z(-2))
    below = lax.ppermute(own, "ctx", along_z(2))
    up, down = fold(own, above, below, send)
    far_up = lax.ppermute(up, "ctx", along_z(-UP))
    far_down = lax.ppermute(down, "ctx", along_z(DOWN))
    near, w_gate_up = base(own, above, below, hidden_in, pick, w_in[0])
    terms, keep = expert_in(near, far_up, far_down, norm_gain.reshape(1, -1), w_gate_up, n_exp)
    terms = lax.all_to_all(terms, "exp", 0, 0)
    act = lax.all_to_all(activation(terms), "exp", 0, 0)
    outs = expert_out(act, w_down[0].T, slot, back, n_ctx)
    outs = lax.all_to_all(outs, "ctx", 0, 0)
    return index_scores, last(outs, keep)


def solution(mesh):
    return jax.shard_map(
        local,
        mesh=mesh,
        in_specs=(
            P("exp", "ctx", None),
            P("exp", "ctx", None),
            P("exp", None, None),
            P("exp", None, None),
            P("exp", None),
            P("exp", None),
            P("ctx", None, None),
            P("ctx", "exp"),
            P(None, "exp"),
            P("exp"),
            P(),
            P(),
            P("ctx", "exp", None),
            P("ctx", None, "exp"),
        ),
        out_specs=(P("exp", "ctx"), P("ctx", "exp")),
        check_vma=False,
    )
```

```python
import functools

import jax
import jax.numpy as jnp
from jax import lax
from jax.experimental import pallas as pl
from jax.experimental.pallas import tpu as pltpu
from jax.sharding import PartitionSpec as P

f32 = jnp.float32
bf16 = jnp.bfloat16
D = 7168
BLOCK = 64
LAT = 512
WIDE = 640
CAP = 48
UP, DOWN = 6, 4
NEG = -1e30
SCORE_SCALE = 192.0 ** (-0.5)
EPS = 1e-06
HIGH = lax.Precision.HIGHEST
MB = 1 << 20

VMEM = pl.BlockSpec(memory_space=pltpu.VMEM)
SMEM = pl.BlockSpec(memory_space=pltpu.SMEM)
HBM = pl.BlockSpec(memory_space=pltpu.HBM)
ANY = pl.BlockSpec(memory_space=pl.ANY)


def in_hbm(x):
    return pltpu.with_memory_space_constraint(x, pltpu.HBM)


def params(mb=8):
    return pltpu.CompilerParams(vmem_limit_bytes=mb * MB)


def iota(shape, dim):
    return lax.broadcasted_iota(jnp.int32, shape, dim)


def dot(a, b, dims=((1,), (0,)), precision=None):
    return lax.dot_general(a, b, (dims, ((), ())), precision=precision, preferred_element_type=f32)


def split3(x):
    hi = x.astype(bf16).astype(f32)
    mid = (x - hi).astype(bf16).astype(f32)
    low = (x - hi - mid).astype(bf16).astype(f32)
    return hi, mid, low


def stats_tile(peak, total):
    lane = iota(peak.shape[:-1] + (128,), len(peak.shape) - 1)
    tile = jnp.zeros(peak.shape[:-1] + (128,), f32)
    for place, part in enumerate(split3(peak) + split3(total)):
        tile = jnp.where(lane == place, part, tile)
    return tile


def read_stats(x):
    tile = x[..., LAT:WIDE]
    lane = iota(tile.shape, len(tile.shape) - 1)
    peak = jnp.sum(jnp.where(lane < 3, tile, 0.0), axis=-1, keepdims=True)
    total = jnp.sum(jnp.where((lane >= 3) & (lane < 6), tile, 0.0), axis=-1, keepdims=True)
    return peak, total


def pack(x):
    n = x.shape[0]
    half = (n // 2 + 7) // 8 * 8
    ends = jnp.concatenate([x[:half, 384:], x[n - half :, 384:]], axis=1)
    return jnp.concatenate([x[:, :128], x[:, 128:256], x[:, 256:384], ends], axis=0)


def unpack(x, n):
    half = x.shape[0] - 3 * n
    ends = jnp.concatenate([x[3 * n :, :64], x[3 * n + 2 * half - n :, 64:]], axis=0)
    return jnp.concatenate([x[:n], x[n : 2 * n], x[2 * n : 3 * n], ends], axis=1)


def packed_lines(n):
    return 3 * n + (n // 2 + 7) // 8 * 8


def attention_kernel(
    ctx_ref, blocks_hbm, query_hbm, cache_hbm, mine_ref, other_ref, blocks_ref, query_ref, cache_ref, sems, sem
):
    rows, _, tokens = cache_ref.shape
    load_blocks = pltpu.make_async_copy(blocks_hbm, blocks_ref, sem)
    copies = [
        (
            pltpu.make_async_copy(query_hbm.at[r], query_ref.at[r], sems.at[0, r]),
            pltpu.make_async_copy(cache_hbm.at[r], cache_ref.at[r], sems.at[1, r]),
        )
        for r in range(rows)
    ]

    def start(r):
        for copy in copies[r]:
            copy.start()

    start(0)
    load_blocks.start()
    for r in range(1, 3):
        start(r)
    ctx = ctx_ref[0]
    core = lax.rem(ctx, 2)
    per = tokens // BLOCK

    def scores_of(i):
        for copy in copies[i]:
            copy.wait()
        if i + 3 < rows:
            start(i + 3)
        return dot(query_ref[i], cache_ref[i], ((0,), (0,))) * SCORE_SCALE

    def partial(i, scores, mask):
        chosen = mask[i : i + 1, :] > 0.0
        masked = jnp.where(chosen, scores, NEG)
        peak = jnp.max(masked, axis=1, keepdims=True)
        expo = jnp.where(chosen, jnp.exp(masked - peak), 0.0)
        total = jnp.sum(expo, axis=1, keepdims=True)
        weighted = dot(expo.astype(bf16), cache_ref[i, :LAT], ((1,), (1,)))
        wide = jnp.concatenate([weighted, stats_tile(peak, total)], axis=1).reshape(8, 2, 8, WIDE)
        return jnp.where(core == 0, wide[:, 0], wide[:, 1]), jnp.where(core == 0, wide[:, 1], wide[:, 0])

    scores = scores_of(0)
    load_blocks.wait()
    block_of = iota((rows, tokens), 1) // BLOCK
    mask = jnp.zeros((rows, tokens), f32)
    picked = blocks_ref[...]
    for b in range(per):
        hit = jnp.max(jnp.where(picked == ctx * per + b, 1.0, 0.0), axis=1, keepdims=True)
        mask = jnp.where(block_of == b, hit, mask)
    for i in range(rows):
        later = scores_of(i + 1) if i + 1 < rows else None
        mine, other = partial(i, scores, mask)
        if i % 2 == 0:
            mine_even, other_even = mine, other
        else:
            lines = slice(8 * i - 8, 8 * i + 8)
            mine_ref[:, lines, :] = jnp.concatenate([mine_even, mine], axis=1)
            other_ref[:, lines, :] = jnp.concatenate([other_even, other], axis=1).astype(bf16)
        scores = later


def attention(ctx, blocks, query, cache):
    rows = query.shape[0]
    return pl.pallas_call(
        attention_kernel,
        in_specs=[SMEM, HBM, HBM, HBM],
        out_specs=[VMEM] * 2,
        out_shape=[
            jax.ShapeDtypeStruct((8, rows * 8, WIDE), f32),
            jax.ShapeDtypeStruct((8, rows * 8, WIDE), bf16),
        ],
        scratch_shapes=[
            pltpu.VMEM(blocks.shape, jnp.int32),
            pltpu.VMEM(query.shape, bf16),
            pltpu.VMEM(cache.shape, bf16),
            pltpu.SemaphoreType.DMA((2, rows)),
            pltpu.SemaphoreType.DMA,
        ],
        compiler_params=params(16),
        name="attention",
    )(ctx, in_hbm(blocks), in_hbm(query), in_hbm(cache))


def side_kernel(
    ctx_ref, route_ref, gate_ref, iq_ref, iw_ref, keys_ref, _,
    score_ref, send_ref, pick_ref, back_ref, slot_ref,
):
    scores = []
    for r in range(iq_ref.shape[0]):
        raw = dot(iq_ref[r], keys_ref[r], ((1,), (1,))) * (iq_ref.shape[2] ** (-0.5))
        scores.append(dot(iw_ref[r : r + 1, :], jnp.maximum(raw, 0.0), precision=HIGH))
    score_ref[...] = jnp.concatenate(scores, axis=0)
    n = route_ref.shape[1]
    ctx = ctx_ref[0]
    n_ctx = n // 6
    names = route_ref[...]
    experts = [ctx, lax.rem(ctx + n_ctx - UP, n_ctx), lax.rem(ctx + DOWN, n_ctx)]
    hit = [jnp.max(jnp.where(names == g, 1.0, 0.0), axis=0, keepdims=True) for g in experts]
    upto = jnp.where(iota((n, n), 0) <= iota((n, n), 1), 1.0, 0.0).astype(bf16)
    hits = jnp.concatenate(hit + [jnp.zeros((8 - len(hit), n), f32)], axis=0)
    slots = dot(hits.astype(bf16), upto).astype(jnp.int32) - 1
    line, col = iota((8, n), 0), iota((8, n), 1)
    picks = []
    for j, g in enumerate(experts):
        picks.append(jnp.where((iota((CAP, n), 0) == slots[j : j + 1]) & (hit[j] > 0.0), 1.0, 0.0))
        own = jnp.where((col == 6 * g + line) & (line < 6), 1.0, 0.0)
        both = jnp.concatenate([picks[j], own], axis=0).astype(bf16)
        if j == 0:
            pick_ref[...] = both
        else:
            send_ref[j - 1] = both
    gate = jnp.sum(jnp.where(names == ctx, gate_ref[...], 0.0), axis=0, keepdims=True)
    row, col = iota((128, n), 0), iota((128, n), 1)
    spread = (row // 8 * 6 + row % 8 == col) & (row % 8 < 6)
    spread = jnp.where(spread, 1.0, 0.0).astype(bf16)
    back_ref[...] = dot(spread, picks[0].astype(bf16), ((1,), (1,))).astype(bf16)
    slot_ref[...] = jnp.broadcast_to(jnp.sum(picks[0] * gate, axis=1, keepdims=True), (CAP, 128))


def side(ctx, route, gate, iq, iw, keys, after):
    n = route.shape[1]
    return pl.pallas_call(
        side_kernel,
        in_specs=[SMEM] + [VMEM] * 5 + [ANY],
        out_specs=[VMEM] * 5,
        out_shape=[
            jax.ShapeDtypeStruct((iq.shape[0], keys.shape[1]), f32),
            jax.ShapeDtypeStruct((2, CAP + 8, n), bf16),
            jax.ShapeDtypeStruct((CAP + 8, n), bf16),
            jax.ShapeDtypeStruct((128, CAP), bf16),
            jax.ShapeDtypeStruct((CAP, 128), f32),
        ],
        compiler_params=params(),
        name="side",
    )(ctx, route, gate, iq, iw, keys, after)


def merge(parts):
    stats = [read_stats(x) for x in parts]
    peak = functools.reduce(jnp.maximum, [p for p, _ in stats])
    factors = [jnp.exp(p - peak) for p, _ in stats]
    total = sum(t * f for (_, t), f in zip(stats, factors))
    return peak, total, sum(x[:, :LAT] * f for x, f in zip(parts, factors))


def widen(peak, total, summed):
    return jnp.concatenate([summed, stats_tile(peak, total)], axis=1)


def pair_kernel(ctx_ref, mine_ref, other_ref, keep_ref, up_ref, down_ref):
    n = mine_ref.shape[0]
    z = ctx_ref[0] // 2
    for ref, offsets in ((up_ref, (1, 6, 3)), (down_ref, (7, 4)), (keep_ref, (0, 5, 2))):
        for i, offset in enumerate(offsets):
            there = lax.rem(z + offset, n)
            both = merge([mine_ref[there], other_ref[there].astype(f32)])
            ref[i] = widen(*both).astype(ref.dtype)


def pair(ctx, mine, other):
    rest = mine.shape[1:]
    return pl.pallas_call(
        pair_kernel,
        in_specs=[SMEM, VMEM, VMEM],
        out_specs=[VMEM] * 3,
        out_shape=[
            jax.ShapeDtypeStruct((3,) + rest, f32),
            jax.ShapeDtypeStruct((3,) + rest, bf16),
            jax.ShapeDtypeStruct((2,) + rest, bf16),
        ],
        compiler_params=params(),
        name="pair",
    )(ctx, mine, other)


def relay_kernel(keep_ref, below_ref, above_ref, up_ref, down_ref):
    down = merge([keep_ref[1], below_ref[1].astype(f32), above_ref[1].astype(f32)])
    down_ref[...] = widen(*down).astype(bf16)
    up_ref[...] = widen(*merge([keep_ref[2], below_ref[2].astype(f32)])).astype(bf16)


def relay(keep, below, above):
    return pl.pallas_call(
        relay_kernel,
        in_specs=[VMEM] * 3,
        out_specs=[VMEM] * 2,
        out_shape=[jax.ShapeDtypeStruct(keep.shape[1:], bf16)] * 2,
        compiler_params=params(),
        name="relay",
    )(keep, below, above)


def values_kernel(keep_ref, below_ref, above_ref, far_below_ref, far_above_ref, w_ref, _, out_ref):
    parts = [keep_ref[0], below_ref[0], above_ref[0], far_below_ref[...], far_above_ref[...]]
    _, total, summed = merge([x.astype(f32) for x in parts])
    lat = (summed / total).astype(bf16)
    rows = lat.shape[0]
    row, col = iota((64, rows), 0), iota((64, rows), 1)
    by_head = jnp.where((row % 8) * 8 + row // 8 == col, 1.0, 0.0).astype(bf16)
    lat = dot(by_head, lat)
    out = [dot(lat[8 * h : 8 * h + 8].astype(bf16), w_ref[h]) for h in range(8)]
    half = jnp.concatenate([jnp.concatenate(out[:4], axis=1), jnp.concatenate(out[4:], axis=1)], axis=0)
    half = half.astype(bf16)
    for e in range(out_ref.shape[0]):
        out_ref[e] = half


def values(parts, w_uv, after, n_exp):
    return pl.pallas_call(
        values_kernel,
        in_specs=[VMEM] * (len(parts) + 1) + [ANY],
        out_specs=VMEM,
        out_shape=jax.ShapeDtypeStruct((n_exp, 16, 512), bf16),
        compiler_params=params(),
        name="values",
    )(*parts, w_uv, after)


def project_kernel(values_ref, w_ref, out_ref, acc_ref):
    x = values_ref[...].astype(f32)
    n = x.shape[0]
    low = x[:, :8].reshape(n * 8, 512).astype(bf16)
    high = x[:, 8:].reshape(n * 8, 512).astype(bf16)
    acc = dot(low, w_ref[:, :512], ((1,), (1,))) + dot(high, w_ref[:, 512:], ((1,), (1,)))
    for e in range(n):
        acc_ref[6 * e : 6 * e + 6, :] = acc[8 * e : 8 * e + 6, :]
    out_ref[...] = pack(acc_ref[: 6 * n, :]).astype(bf16)


def project(vals, w_o):
    shape = (vals.shape[0] * 6, w_o.shape[0])
    return pl.pallas_call(
        project_kernel,
        in_specs=[VMEM] * 2,
        out_specs=VMEM,
        out_shape=jax.ShapeDtypeStruct((packed_lines(shape[0]), 128), bf16),
        scratch_shapes=[pltpu.VMEM((shape[0] + 8, shape[1]), f32)],
        compiler_params=params(),
        name="project",
    )(vals, w_o)


def fold_kernel(own_ref, above_ref, below_ref, send_ref, up_ref, down_ref):
    n = send_ref.shape[2]
    two = own_ref[...].astype(f32) + below_ref[...].astype(f32)
    three = two + above_ref[...].astype(f32)
    up_ref[...] = pack(dot(send_ref[0], unpack(three, n).astype(bf16))).astype(bf16)
    down_ref[...] = pack(dot(send_ref[1], unpack(two, n).astype(bf16))).astype(bf16)


def fold(own, above, below, send):
    shape = jax.ShapeDtypeStruct((packed_lines(send.shape[1]), 128), bf16)
    return pl.pallas_call(
        fold_kernel,
        in_specs=[VMEM] * 4,
        out_specs=[VMEM] * 2,
        out_shape=[shape, shape],
        compiler_params=params(),
        name="fold",
    )(own, above, below, send)


def base_kernel(own_ref, above_ref, below_ref, hidden_ref, pick_ref, w_hbm, out_ref, w_ref, sem):
    load = pltpu.make_async_copy(w_hbm, w_ref, sem)
    load.start()
    pick = pick_ref[...]
    n = pick.shape[1]
    near = sum(
        dot(pick, unpack(ref[...].astype(f32), n).astype(bf16)) for ref in (own_ref, above_ref, below_ref)
    )
    out_ref[...] = dot(pick, hidden_ref[...]) + near
    load.wait()


def base(own, above, below, hidden, pick, w_in):
    return pl.pallas_call(
        base_kernel,
        in_specs=[VMEM] * 5 + [HBM],
        out_specs=[VMEM] * 2,
        out_shape=[
            jax.ShapeDtypeStruct((pick.shape[0], hidden.shape[1]), f32),
            jax.ShapeDtypeStruct(w_in.shape, bf16),
        ],
        scratch_shapes=[pltpu.SemaphoreType.DMA],
        compiler_params=params(),
        name="base",
    )(own, above, below, hidden, pick, in_hbm(w_in))


def expert_in_kernel(near_ref, far_up_ref, far_down_ref, gain_ref, w_ref, out_ref, keep_ref):
    n = out_ref.shape[0]
    half = w_ref.shape[1] // 2
    far = far_up_ref[...].astype(f32) + far_down_ref[...].astype(f32)
    attn = near_ref[...] + unpack(far, near_ref.shape[0])
    resid32 = attn.astype(bf16).astype(f32)
    keep_ref[...] = resid32[CAP:]
    picked = resid32[:CAP]
    rows = (picked * gain_ref[...]).astype(bf16)
    squares = dot(jnp.ones((8, picked.shape[1]), f32), picked * picked, ((1,), (1,)), HIGH)
    hi, mid, low = split3(squares)
    line = iota(squares.shape, 0)
    parts = jnp.where(line == 0, hi, jnp.where(line == 1, mid, jnp.where(line == 2, low, 0.0)))
    parts = jnp.concatenate([parts, jnp.zeros((8, 256 - CAP), f32)], axis=1)
    for e in range(0, n, 2):
        gate = dot(rows, w_ref[:, 128 * e : 128 * e + 256])
        up = dot(rows, w_ref[:, half + 128 * e : half + 128 * e + 256])
        for i in range(2):
            here = slice(128 * i, 128 * i + 128)
            both = jnp.concatenate([gate[:, here], up[:, here]], axis=1)
            out_ref[e + i] = jnp.concatenate([both, parts], axis=0).astype(bf16)


def expert_in(near, far_up, far_down, gain, w_in, n_exp):
    width = near.shape[1]
    return pl.pallas_call(
        expert_in_kernel,
        in_specs=[VMEM] * 5,
        out_specs=[VMEM] * 2,
        out_shape=[
            jax.ShapeDtypeStruct((n_exp, CAP + 8, 256), bf16),
            jax.ShapeDtypeStruct((8, width), f32),
        ],
        compiler_params=params(),
        name="expert_in",
    )(near, far_up, far_down, gain, w_in)


def act_kernel(parts_ref, out_ref):
    x = jnp.sum(parts_ref[...].astype(f32), axis=0)
    line = x[CAP : CAP + 1, :CAP] + x[CAP + 1 : CAP + 2, :CAP] + x[CAP + 2 : CAP + 3, :CAP]
    diagonal = iota((CAP, CAP), 0) == iota((CAP, CAP), 1)
    squares = jnp.sum(jnp.where(diagonal, line, 0.0), axis=1, keepdims=True)
    inv = lax.rsqrt(squares / D + EPS)
    gate, up = x[:CAP, :128] * inv, x[:CAP, 128:] * inv
    act = (jax.nn.silu(gate) * up).astype(bf16)
    for e in range(out_ref.shape[0]):
        out_ref[e] = act


def activation(parts):
    return pl.pallas_call(
        act_kernel,
        in_specs=[VMEM],
        out_specs=VMEM,
        out_shape=jax.ShapeDtypeStruct((parts.shape[0], CAP, 128), bf16),
        compiler_params=params(),
        name="activation",
    )(parts)


def expert_out_kernel(act_ref, w_ref, slot_ref, back_ref, out_ref):
    act = jnp.concatenate([act_ref[e] for e in range(act_ref.shape[0])], axis=1)
    out = (dot(act, w_ref[...], ((1,), (1,))) * slot_ref[:, 0:1]).astype(bf16)
    back = dot(back_ref[...], out)
    n = out_ref.shape[0]
    low = back[:, :256].reshape(n, 8, 256)
    high = jnp.concatenate([back[:, 256:], jnp.zeros((n * 8, 64), f32)], axis=1).reshape(n, 8, 256)
    out_ref[...] = jnp.concatenate([low, high], axis=1).astype(bf16)


def expert_out(act, w_down, slot, back, n_ctx):
    return pl.pallas_call(
        expert_out_kernel,
        in_specs=[VMEM] * 4,
        out_specs=VMEM,
        out_shape=jax.ShapeDtypeStruct((n_ctx, 16, 256), bf16),
        compiler_params=params(),
        name="expert_out",
    )(act, w_down, slot, back)


def last_kernel(parts_ref, keep_ref, out_ref):
    x = jnp.sum(parts_ref[...].astype(f32), axis=0)
    moe = jnp.concatenate([x[:8], x[8:, :192]], axis=1)
    out_ref[...] = (keep_ref[...] + moe)[:6].astype(bf16)


def last(parts, keep):
    return pl.pallas_call(
        last_kernel,
        in_specs=[VMEM] * 2,
        out_specs=VMEM,
        out_shape=jax.ShapeDtypeStruct((6, keep.shape[1]), bf16),
        compiler_params=params(),
        name="last",
    )(parts, keep)


def local(
    cache, idx_keys, lat_query, idx_query, idx_weight, chosen_blocks, w_uv, w_o, hidden_in, norm_gain,
    route, route_weight, w_in, w_down,
):
    n_ctx, n_exp = lax.axis_size("ctx"), lax.axis_size("exp")
    ctx = lax.axis_index("ctx").astype(jnp.int32).reshape(1)
    other_core = [(i, i ^ 1) for i in range(n_ctx)]
    def along_z(shift):
        return [(i, (i + shift) % n_ctx) for i in range(n_ctx)]

    mine, other = attention(
        ctx, chosen_blocks, jnp.swapaxes(lat_query, 1, 2), jnp.swapaxes(cache, 1, 2)
    )
    other = lax.ppermute(other, "ctx", other_core)
    keep, up, down = pair(ctx, mine, other)
    below = lax.ppermute(up, "ctx", along_z(2))
    above = lax.ppermute(down, "ctx", along_z(-2))
    up, down = relay(keep, below, above)
    far_below = lax.ppermute(up, "ctx", along_z(DOWN))
    far_above = lax.ppermute(down, "ctx", along_z(-UP))
    index_scores, send, pick, back, slot = side(
        ctx, route.T, route_weight.T, idx_query, idx_weight, idx_keys, up
    )
    vals = values((keep, below, above, far_below, far_above), w_uv, send, n_exp)
    vals = lax.all_to_all(vals, "exp", 0, 0)
    part = project(vals, w_o.T)
    own = part.astype(f32) + lax.ppermute(part, "ctx", other_core).astype(f32)
    own = own.astype(bf16)
    above = lax.ppermute(own, "ctx", along_z(-2))
    below = lax.ppermute(own, "ctx", along_z(2))
    up, down = fold(own, above, below, send)
    far_up = lax.ppermute(up, "ctx", along_z(-UP))
    far_down = lax.ppermute(down, "ctx", along_z(DOWN))
    near, w_gate_up = base(own, above, below, hidden_in, pick, w_in[0])
    terms, keep = expert_in(near, far_up, far_down, norm_gain.reshape(1, -1), w_gate_up, n_exp)
    terms = lax.all_to_all(terms, "exp", 0, 0)
    act = lax.all_to_all(activation(terms), "exp", 0, 0)
    outs = expert_out(act, w_down[0].T, slot, back, n_ctx)
    outs = lax.all_to_all(outs, "ctx", 0, 0)
    return index_scores, last(outs, keep)


def solution(mesh):
    return jax.shard_map(
        local,
        mesh=mesh,
        in_specs=(
            P("exp", "ctx", None),
            P("exp", "ctx", None),
            P("exp", None, None),
            P("exp", None, None),
            P("exp", None),
            P("exp", None),
            P("ctx", None, None),
            P("ctx", "exp"),
            P(None, "exp"),
            P("exp"),
            P(),
            P(),
            P("ctx", "exp", None),
            P("ctx", None, "exp"),
        ),
        out_specs=(P("exp", "ctx"), P("ctx", "exp")),
        check_vma=False,
    )
```

```python
import functools

import jax
import jax.numpy as jnp
from jax import lax
from jax.experimental import pallas as pl
from jax.experimental.pallas import tpu as pltpu
from jax.sharding import PartitionSpec as P

f32 = jnp.float32
bf16 = jnp.bfloat16
D = 7168
BLOCK = 64
LAT = 512
WIDE = 640
CAP = 48
UP, DOWN = 6, 4
NEG = -1e30
SCORE_SCALE = 192.0 ** (-0.5)
EPS = 1e-06
HIGH = lax.Precision.HIGHEST
MB = 1 << 20

VMEM = pl.BlockSpec(memory_space=pltpu.VMEM)
SMEM = pl.BlockSpec(memory_space=pltpu.SMEM)
HBM = pl.BlockSpec(memory_space=pltpu.HBM)
ANY = pl.BlockSpec(memory_space=pl.ANY)


def in_hbm(x):
    return pltpu.with_memory_space_constraint(x, pltpu.HBM)


def params(mb=8):
    return pltpu.CompilerParams(vmem_limit_bytes=mb * MB)


def iota(shape, dim):
    return lax.broadcasted_iota(jnp.int32, shape, dim)


def dot(a, b, dims=((1,), (0,)), precision=None):
    return lax.dot_general(a, b, (dims, ((), ())), precision=precision, preferred_element_type=f32)


def split3(x):
    hi = x.astype(bf16).astype(f32)
    mid = (x - hi).astype(bf16).astype(f32)
    low = (x - hi - mid).astype(bf16).astype(f32)
    return hi, mid, low


def stats_tile(peak, total):
    lane = iota(peak.shape[:-1] + (128,), len(peak.shape) - 1)
    tile = jnp.zeros(peak.shape[:-1] + (128,), f32)
    for place, part in enumerate(split3(peak) + split3(total)):
        tile = jnp.where(lane == place, part, tile)
    return tile


def read_stats(x):
    tile = x[..., LAT:WIDE]
    lane = iota(tile.shape, len(tile.shape) - 1)
    peak = jnp.sum(jnp.where(lane < 3, tile, 0.0), axis=-1, keepdims=True)
    total = jnp.sum(jnp.where((lane >= 3) & (lane < 6), tile, 0.0), axis=-1, keepdims=True)
    return peak, total


def pack(x):
    n = x.shape[0]
    half = (n // 2 + 7) // 8 * 8
    ends = jnp.concatenate([x[:half, 384:], x[n - half :, 384:]], axis=1)
    return jnp.concatenate([x[:, :128], x[:, 128:256], x[:, 256:384], ends], axis=0)


def unpack(x, n):
    half = x.shape[0] - 3 * n
    ends = jnp.concatenate([x[3 * n :, :64], x[3 * n + 2 * half - n :, 64:]], axis=0)
    return jnp.concatenate([x[:n], x[n : 2 * n], x[2 * n : 3 * n], ends], axis=1)


def packed_lines(n):
    return 3 * n + (n // 2 + 7) // 8 * 8


def chosen_mask(ctx, picked, tokens):
    rows = picked.shape[0]
    per = tokens // BLOCK
    block_of = iota((rows, tokens), 1) // BLOCK
    mask = jnp.zeros((rows, tokens), f32)
    for b in range(per):
        hit = jnp.max(jnp.where(picked == ctx * per + b, 1.0, 0.0), axis=1, keepdims=True)
        mask = jnp.where(block_of == b, hit, mask)
    return mask


def scores_of(query, keys):
    return dot(query, keys, ((0,), (0,))) * SCORE_SCALE


def partial_row(core, scores, keys, chosen):
    masked = jnp.where(chosen, scores, NEG)
    peak = jnp.max(masked, axis=1, keepdims=True)
    expo = jnp.where(chosen, jnp.exp(masked - peak), 0.0)
    total = jnp.sum(expo, axis=1, keepdims=True)
    weighted = dot(expo.astype(bf16), keys[:LAT], ((1,), (1,)))
    wide = jnp.concatenate([weighted, stats_tile(peak, total)], axis=1).reshape(8, 2, 8, WIDE)
    return jnp.where(core == 0, wide[:, 0], wide[:, 1]), jnp.where(core == 0, wide[:, 1], wide[:, 0])


def store_pair(i, even, odd, mine_ref, other_ref):
    lines = slice(8 * i - 8, 8 * i + 8)
    mine_ref[:, lines, :] = jnp.concatenate([even[0], odd[0]], axis=1)
    other_ref[:, lines, :] = jnp.concatenate([even[1], odd[1]], axis=1).astype(bf16)


def attention_kernel(
    ctx_ref, blocks_hbm, query_hbm, cache_hbm, mine_ref, other_ref, blocks_ref, query_rest, cache_rest,
    query_ref, cache_ref, sems, sem,
):
    here, _, tokens = cache_ref.shape
    rows = cache_hbm.shape[0]
    load_blocks = pltpu.make_async_copy(blocks_hbm, blocks_ref, sem)
    copies = []
    for r in range(rows):
        query_to = query_ref.at[r] if r < here else query_rest.at[r - here]
        cache_to = cache_ref.at[r] if r < here else cache_rest.at[r - here]
        copies.append(
            (
                pltpu.make_async_copy(query_hbm.at[r], query_to, sems.at[0, r]),
                pltpu.make_async_copy(cache_hbm.at[r], cache_to, sems.at[1, r]),
            )
        )

    def start(r):
        for copy in copies[r]:
            copy.start()

    def ready(r):
        for copy in copies[r]:
            copy.wait()
        if r + 3 < rows:
            start(r + 3)

    start(0)
    load_blocks.start()
    start(1)
    start(2)
    ctx = ctx_ref[0]
    core = lax.rem(ctx, 2)
    ready(0)
    scores = scores_of(query_ref[0], cache_ref[0])
    load_blocks.wait()
    mask = chosen_mask(ctx, blocks_ref[...], tokens)
    even = None
    for i in range(here):
        later = None
        if i + 1 < here:
            ready(i + 1)
            later = scores_of(query_ref[i + 1], cache_ref[i + 1])
        row = partial_row(core, scores, cache_ref[i], mask[i : i + 1, :] > 0.0)
        if i % 2 == 0:
            even = row
        else:
            store_pair(i, even, row, mine_ref, other_ref)
        scores = later
    for r in range(here, rows):
        ready(r)


def rest_kernel(ctx_ref, blocks_ref, query_ref, cache_ref, mine_ref, other_ref):
    count, _, tokens = cache_ref.shape
    ctx = ctx_ref[0]
    core = lax.rem(ctx, 2)
    rows = blocks_ref.shape[0]
    mask = chosen_mask(ctx, blocks_ref[...], tokens)
    scores = [scores_of(query_ref[i], cache_ref[i]) for i in range(count)]
    even = None
    for i in range(count):
        at = rows - count + i
        row = partial_row(core, scores[i], cache_ref[i], mask[at : at + 1, :] > 0.0)
        if i % 2 == 0:
            even = row
        else:
            store_pair(i, even, row, mine_ref, other_ref)


def halves_out(rows):
    return [
        jax.ShapeDtypeStruct((8, rows * 8, WIDE), f32),
        jax.ShapeDtypeStruct((8, rows * 8, WIDE), bf16),
    ]


def attention(ctx, blocks, query, cache):
    rows = query.shape[0]
    here, rest = rows - 2, 2
    return pl.pallas_call(
        attention_kernel,
        in_specs=[SMEM, HBM, HBM, HBM],
        out_specs=[VMEM] * 5,
        out_shape=halves_out(here)
        + [
            jax.ShapeDtypeStruct(blocks.shape, jnp.int32),
            jax.ShapeDtypeStruct((rest,) + query.shape[1:], bf16),
            jax.ShapeDtypeStruct((rest,) + cache.shape[1:], bf16),
        ],
        scratch_shapes=[
            pltpu.VMEM((here,) + query.shape[1:], bf16),
            pltpu.VMEM((here,) + cache.shape[1:], bf16),
            pltpu.SemaphoreType.DMA((2, rows)),
            pltpu.SemaphoreType.DMA,
        ],
        compiler_params=params(16),
        name="attention",
    )(ctx, in_hbm(blocks), in_hbm(query), in_hbm(cache))


def attention_rest(ctx, blocks, query, cache):
    return pl.pallas_call(
        rest_kernel,
        in_specs=[SMEM] + [VMEM] * 3,
        out_specs=[VMEM] * 2,
        out_shape=halves_out(query.shape[0]),
        compiler_params=params(),
        name="attention_rest",
    )(ctx, blocks, query, cache)


def side_kernel(
    ctx_ref, route_ref, gate_ref, iq_ref, iw_ref, keys_ref, _,
    score_ref, send_ref, pick_ref, back_ref, slot_ref,
):
    scores = []
    for r in range(iq_ref.shape[0]):
        raw = dot(iq_ref[r], keys_ref[r], ((1,), (1,))) * (iq_ref.shape[2] ** (-0.5))
        scores.append(dot(iw_ref[r : r + 1, :], jnp.maximum(raw, 0.0), precision=HIGH))
    score_ref[...] = jnp.concatenate(scores, axis=0)
    n = route_ref.shape[1]
    ctx = ctx_ref[0]
    n_ctx = n // 6
    names = route_ref[...]
    experts = [ctx, lax.rem(ctx + n_ctx - UP, n_ctx), lax.rem(ctx + DOWN, n_ctx)]
    hit = [jnp.max(jnp.where(names == g, 1.0, 0.0), axis=0, keepdims=True) for g in experts]
    upto = jnp.where(iota((n, n), 0) <= iota((n, n), 1), 1.0, 0.0).astype(bf16)
    hits = jnp.concatenate(hit + [jnp.zeros((8 - len(hit), n), f32)], axis=0)
    slots = dot(hits.astype(bf16), upto).astype(jnp.int32) - 1
    line, col = iota((8, n), 0), iota((8, n), 1)
    picks = []
    for j, g in enumerate(experts):
        picks.append(jnp.where((iota((CAP, n), 0) == slots[j : j + 1]) & (hit[j] > 0.0), 1.0, 0.0))
        own = jnp.where((col == 6 * g + line) & (line < 6), 1.0, 0.0)
        both = jnp.concatenate([picks[j], own], axis=0).astype(bf16)
        if j == 0:
            pick_ref[...] = both
        else:
            send_ref[j - 1] = both
    gate = jnp.sum(jnp.where(names == ctx, gate_ref[...], 0.0), axis=0, keepdims=True)
    row, col = iota((128, n), 0), iota((128, n), 1)
    spread = (row // 8 * 6 + row % 8 == col) & (row % 8 < 6)
    spread = jnp.where(spread, 1.0, 0.0).astype(bf16)
    back_ref[...] = dot(spread, picks[0].astype(bf16), ((1,), (1,))).astype(bf16)
    slot_ref[...] = jnp.broadcast_to(jnp.sum(picks[0] * gate, axis=1, keepdims=True), (CAP, 128))


def side(ctx, route, gate, iq, iw, keys, after):
    n = route.shape[1]
    return pl.pallas_call(
        side_kernel,
        in_specs=[SMEM] + [VMEM] * 5 + [ANY],
        out_specs=[VMEM] * 5,
        out_shape=[
            jax.ShapeDtypeStruct((iq.shape[0], keys.shape[1]), f32),
            jax.ShapeDtypeStruct((2, CAP + 8, n), bf16),
            jax.ShapeDtypeStruct((CAP + 8, n), bf16),
            jax.ShapeDtypeStruct((128, CAP), bf16),
            jax.ShapeDtypeStruct((CAP, 128), f32),
        ],
        compiler_params=params(),
        name="side",
    )(ctx, route, gate, iq, iw, keys, after)


def merge(parts):
    stats = [read_stats(x) for x in parts]
    peak = functools.reduce(jnp.maximum, [p for p, _ in stats])
    factors = [jnp.exp(p - peak) for p, _ in stats]
    total = sum(t * f for (_, t), f in zip(stats, factors))
    return peak, total, sum(x[:, :LAT] * f for x, f in zip(parts, factors))


def widen(peak, total, summed):
    return jnp.concatenate([summed, stats_tile(peak, total)], axis=1)


def pair_kernel(offsets, ctx_ref, mine_ref, other_ref, mine_rest, other_rest, *out_refs):
    n = mine_ref.shape[0]
    z = ctx_ref[0] // 2
    for ref, group in zip(out_refs[-len(offsets) :], offsets):
        for i, offset in enumerate(group):
            there = lax.rem(z + offset, n)
            mine = jnp.concatenate([mine_ref[there], mine_rest[there]], axis=0)
            other = jnp.concatenate([other_ref[there].astype(f32), other_rest[there].astype(f32)], axis=0)
            ref[i] = widen(*merge([mine, other])).astype(ref.dtype)


def pair(ctx, parts, offsets, kind, after=()):
    rows = parts[0].shape[1] + parts[2].shape[1]
    return pl.pallas_call(
        functools.partial(pair_kernel, offsets),
        in_specs=[SMEM] + [VMEM] * 4 + [ANY] * len(after),
        out_specs=[VMEM] * len(offsets),
        out_shape=[jax.ShapeDtypeStruct((len(group), rows, WIDE), kind) for group in offsets],
        compiler_params=params(),
        name="pair",
    )(ctx, *parts, *after)


def relay_kernel(keep_ref, below_ref, above_ref, up_ref, down_ref):
    down = merge([keep_ref[1], below_ref[1].astype(f32), above_ref[1].astype(f32)])
    down_ref[...] = widen(*down).astype(bf16)
    up_ref[...] = widen(*merge([keep_ref[2], below_ref[2].astype(f32)])).astype(bf16)


def relay(keep, below, above):
    return pl.pallas_call(
        relay_kernel,
        in_specs=[VMEM] * 3,
        out_specs=[VMEM] * 2,
        out_shape=[jax.ShapeDtypeStruct(keep.shape[1:], bf16)] * 2,
        compiler_params=params(),
        name="relay",
    )(keep, below, above)


def values_kernel(keep_ref, below_ref, above_ref, far_below_ref, far_above_ref, w_ref, _, out_ref):
    parts = [keep_ref[0], below_ref[0], above_ref[0], far_below_ref[...], far_above_ref[...]]
    _, total, summed = merge([x.astype(f32) for x in parts])
    lat = (summed / total).astype(bf16)
    rows = lat.shape[0]
    row, col = iota((64, rows), 0), iota((64, rows), 1)
    by_head = jnp.where((row % 8) * 8 + row // 8 == col, 1.0, 0.0).astype(bf16)
    lat = dot(by_head, lat)
    out = [dot(lat[8 * h : 8 * h + 8].astype(bf16), w_ref[h]) for h in range(8)]
    half = jnp.concatenate([jnp.concatenate(out[:4], axis=1), jnp.concatenate(out[4:], axis=1)], axis=0)
    half = half.astype(bf16)
    for e in range(out_ref.shape[0]):
        out_ref[e] = half


def values(parts, w_uv, after, n_exp):
    return pl.pallas_call(
        values_kernel,
        in_specs=[VMEM] * (len(parts) + 1) + [ANY],
        out_specs=VMEM,
        out_shape=jax.ShapeDtypeStruct((n_exp, 16, 512), bf16),
        compiler_params=params(),
        name="values",
    )(*parts, w_uv, after)


def project_kernel(values_ref, w_ref, out_ref, acc_ref):
    x = values_ref[...].astype(f32)
    n = x.shape[0]
    low = x[:, :8].reshape(n * 8, 512).astype(bf16)
    high = x[:, 8:].reshape(n * 8, 512).astype(bf16)
    acc = dot(low, w_ref[:, :512], ((1,), (1,))) + dot(high, w_ref[:, 512:], ((1,), (1,)))
    for e in range(n):
        acc_ref[6 * e : 6 * e + 6, :] = acc[8 * e : 8 * e + 6, :]
    out_ref[...] = pack(acc_ref[: 6 * n, :]).astype(bf16)


def project(vals, w_o):
    shape = (vals.shape[0] * 6, w_o.shape[0])
    return pl.pallas_call(
        project_kernel,
        in_specs=[VMEM] * 2,
        out_specs=VMEM,
        out_shape=jax.ShapeDtypeStruct((packed_lines(shape[0]), 128), bf16),
        scratch_shapes=[pltpu.VMEM((shape[0] + 8, shape[1]), f32)],
        compiler_params=params(),
        name="project",
    )(vals, w_o)


def fold_kernel(own_ref, above_ref, below_ref, send_ref, up_ref, down_ref):
    n = send_ref.shape[2]
    two = own_ref[...].astype(f32) + below_ref[...].astype(f32)
    three = two + above_ref[...].astype(f32)
    up_ref[...] = pack(dot(send_ref[0], unpack(three, n).astype(bf16))).astype(bf16)
    down_ref[...] = pack(dot(send_ref[1], unpack(two, n).astype(bf16))).astype(bf16)


def fold(own, above, below, send):
    shape = jax.ShapeDtypeStruct((packed_lines(send.shape[1]), 128), bf16)
    return pl.pallas_call(
        fold_kernel,
        in_specs=[VMEM] * 4,
        out_specs=[VMEM] * 2,
        out_shape=[shape, shape],
        compiler_params=params(),
        name="fold",
    )(own, above, below, send)


def base_kernel(own_ref, above_ref, below_ref, hidden_ref, pick_ref, w_hbm, out_ref, w_ref, sem):
    load = pltpu.make_async_copy(w_hbm, w_ref, sem)
    load.start()
    pick = pick_ref[...]
    n = pick.shape[1]
    near = sum(
        dot(pick, unpack(ref[...].astype(f32), n).astype(bf16)) for ref in (own_ref, above_ref, below_ref)
    )
    out_ref[...] = dot(pick, hidden_ref[...]) + near
    load.wait()


def base(own, above, below, hidden, pick, w_in):
    return pl.pallas_call(
        base_kernel,
        in_specs=[VMEM] * 5 + [HBM],
        out_specs=[VMEM] * 2,
        out_shape=[
            jax.ShapeDtypeStruct((pick.shape[0], hidden.shape[1]), f32),
            jax.ShapeDtypeStruct(w_in.shape, bf16),
        ],
        scratch_shapes=[pltpu.SemaphoreType.DMA],
        compiler_params=params(),
        name="base",
    )(own, above, below, hidden, pick, in_hbm(w_in))


def expert_in_kernel(near_ref, far_up_ref, far_down_ref, gain_ref, w_ref, out_ref, keep_ref):
    n = out_ref.shape[0]
    half = w_ref.shape[1] // 2
    far = far_up_ref[...].astype(f32) + far_down_ref[...].astype(f32)
    attn = near_ref[...] + unpack(far, near_ref.shape[0])
    resid32 = attn.astype(bf16).astype(f32)
    keep_ref[...] = resid32[CAP:]
    picked = resid32[:CAP]
    rows = (picked * gain_ref[...]).astype(bf16)
    squares = dot(jnp.ones((8, picked.shape[1]), f32), picked * picked, ((1,), (1,)), HIGH)
    hi, mid, low = split3(squares)
    line = iota(squares.shape, 0)
    parts = jnp.where(line == 0, hi, jnp.where(line == 1, mid, jnp.where(line == 2, low, 0.0)))
    parts = jnp.concatenate([parts, jnp.zeros((8, 256 - CAP), f32)], axis=1)
    for e in range(0, n, 2):
        gate = dot(rows, w_ref[:, 128 * e : 128 * e + 256])
        up = dot(rows, w_ref[:, half + 128 * e : half + 128 * e + 256])
        for i in range(2):
            here = slice(128 * i, 128 * i + 128)
            both = jnp.concatenate([gate[:, here], up[:, here]], axis=1)
            out_ref[e + i] = jnp.concatenate([both, parts], axis=0).astype(bf16)


def expert_in(near, far_up, far_down, gain, w_in, n_exp):
    width = near.shape[1]
    return pl.pallas_call(
        expert_in_kernel,
        in_specs=[VMEM] * 5,
        out_specs=[VMEM] * 2,
        out_shape=[
            jax.ShapeDtypeStruct((n_exp, CAP + 8, 256), bf16),
            jax.ShapeDtypeStruct((8, width), f32),
        ],
        compiler_params=params(),
        name="expert_in",
    )(near, far_up, far_down, gain, w_in)


def act_kernel(parts_ref, out_ref):
    x = jnp.sum(parts_ref[...].astype(f32), axis=0)
    line = x[CAP : CAP + 1, :CAP] + x[CAP + 1 : CAP + 2, :CAP] + x[CAP + 2 : CAP + 3, :CAP]
    diagonal = iota((CAP, CAP), 0) == iota((CAP, CAP), 1)
    squares = jnp.sum(jnp.where(diagonal, line, 0.0), axis=1, keepdims=True)
    inv = lax.rsqrt(squares / D + EPS)
    gate, up = x[:CAP, :128] * inv, x[:CAP, 128:] * inv
    act = (jax.nn.silu(gate) * up).astype(bf16)
    for e in range(out_ref.shape[0]):
        out_ref[e] = act


def activation(parts):
    return pl.pallas_call(
        act_kernel,
        in_specs=[VMEM],
        out_specs=VMEM,
        out_shape=jax.ShapeDtypeStruct((parts.shape[0], CAP, 128), bf16),
        compiler_params=params(),
        name="activation",
    )(parts)


def expert_out_kernel(act_ref, w_ref, slot_ref, back_ref, out_ref):
    act = jnp.concatenate([act_ref[e] for e in range(act_ref.shape[0])], axis=1)
    out = (dot(act, w_ref[...], ((1,), (1,))) * slot_ref[:, 0:1]).astype(bf16)
    back = dot(back_ref[...], out)
    n = out_ref.shape[0]
    low = back[:, :256].reshape(n, 8, 256)
    high = jnp.concatenate([back[:, 256:], jnp.zeros((n * 8, 64), f32)], axis=1).reshape(n, 8, 256)
    out_ref[...] = jnp.concatenate([low, high], axis=1).astype(bf16)


def expert_out(act, w_down, slot, back, n_ctx):
    return pl.pallas_call(
        expert_out_kernel,
        in_specs=[VMEM] * 4,
        out_specs=VMEM,
        out_shape=jax.ShapeDtypeStruct((n_ctx, 16, 256), bf16),
        compiler_params=params(),
        name="expert_out",
    )(act, w_down, slot, back)


def last_kernel(parts_ref, keep_ref, out_ref):
    x = jnp.sum(parts_ref[...].astype(f32), axis=0)
    moe = jnp.concatenate([x[:8], x[8:, :192]], axis=1)
    out_ref[...] = (keep_ref[...] + moe)[:6].astype(bf16)


def last(parts, keep):
    return pl.pallas_call(
        last_kernel,
        in_specs=[VMEM] * 2,
        out_specs=VMEM,
        out_shape=jax.ShapeDtypeStruct((6, keep.shape[1]), bf16),
        compiler_params=params(),
        name="last",
    )(parts, keep)


def local(
    cache, idx_keys, lat_query, idx_query, idx_weight, chosen_blocks, w_uv, w_o, hidden_in, norm_gain,
    route, route_weight, w_in, w_down,
):
    n_ctx, n_exp = lax.axis_size("ctx"), lax.axis_size("exp")
    ctx = lax.axis_index("ctx").astype(jnp.int32).reshape(1)
    other_core = [(i, i ^ 1) for i in range(n_ctx)]
    def along_z(shift):
        return [(i, (i + shift) % n_ctx) for i in range(n_ctx)]

    mine, other, blocks, query, cache = attention(
        ctx, chosen_blocks, jnp.swapaxes(lat_query, 1, 2), jnp.swapaxes(cache, 1, 2)
    )
    mine_rest, other_rest = attention_rest(ctx, blocks, query, cache)
    other = lax.ppermute(other, "ctx", other_core)
    other_rest = lax.ppermute(other_rest, "ctx", other_core)
    parts = (mine, other, mine_rest, other_rest)
    up, down = pair(ctx, parts, ((1, 6, 3), (7, 4)), bf16)
    (keep,) = pair(ctx, parts, ((0, 5, 2),), f32, (down,))
    below = lax.ppermute(up, "ctx", along_z(2))
    above = lax.ppermute(down, "ctx", along_z(-2))
    up, down = relay(keep, below, above)
    far_below = lax.ppermute(up, "ctx", along_z(DOWN))
    far_above = lax.ppermute(down, "ctx", along_z(-UP))
    index_scores, send, pick, back, slot = side(
        ctx, route.T, route_weight.T, idx_query, idx_weight, idx_keys, up
    )
    vals = values((keep, below, above, far_below, far_above), w_uv, send, n_exp)
    vals = lax.all_to_all(vals, "exp", 0, 0)
    part = project(vals, w_o.T)
    own = part.astype(f32) + lax.ppermute(part, "ctx", other_core).astype(f32)
    own = own.astype(bf16)
    above = lax.ppermute(own, "ctx", along_z(-2))
    below = lax.ppermute(own, "ctx", along_z(2))
    up, down = fold(own, above, below, send)
    far_up = lax.ppermute(up, "ctx", along_z(-UP))
    far_down = lax.ppermute(down, "ctx", along_z(DOWN))
    near, w_gate_up = base(own, above, below, hidden_in, pick, w_in[0])
    terms, keep = expert_in(near, far_up, far_down, norm_gain.reshape(1, -1), w_gate_up, n_exp)
    terms = lax.all_to_all(terms, "exp", 0, 0)
    act = lax.all_to_all(activation(terms), "exp", 0, 0)
    outs = expert_out(act, w_down[0].T, slot, back, n_ctx)
    outs = lax.all_to_all(outs, "ctx", 0, 0)
    return index_scores, last(outs, keep)


def solution(mesh):
    return jax.shard_map(
        local,
        mesh=mesh,
        in_specs=(
            P("exp", "ctx", None),
            P("exp", "ctx", None),
            P("exp", None, None),
            P("exp", None, None),
            P("exp", None),
            P("exp", None),
            P("ctx", None, None),
            P("ctx", "exp"),
            P(None, "exp"),
            P("exp"),
            P(),
            P(),
            P("ctx", "exp", None),
            P("ctx", None, "exp"),
        ),
        out_specs=(P("exp", "ctx"), P("ctx", "exp")),
        check_vma=False,
    )
```

```python
import functools

import jax
import jax.numpy as jnp
from jax import lax
from jax.experimental import pallas as pl
from jax.experimental.pallas import tpu as pltpu
from jax.sharding import PartitionSpec as P

f32 = jnp.float32
bf16 = jnp.bfloat16
D = 7168
BLOCK = 64
LAT = 512
WIDE = 640
CAP = 48
UP, DOWN = 6, 4
NEG = -1e30
SCORE_SCALE = 192.0 ** (-0.5)
EPS = 1e-06
HIGH = lax.Precision.HIGHEST
MB = 1 << 20

VMEM = pl.BlockSpec(memory_space=pltpu.VMEM)
SMEM = pl.BlockSpec(memory_space=pltpu.SMEM)
HBM = pl.BlockSpec(memory_space=pltpu.HBM)
ANY = pl.BlockSpec(memory_space=pl.ANY)


def in_hbm(x):
    return pltpu.with_memory_space_constraint(x, pltpu.HBM)


def params(mb=8):
    return pltpu.CompilerParams(vmem_limit_bytes=mb * MB)


def iota(shape, dim):
    return lax.broadcasted_iota(jnp.int32, shape, dim)


def dot(a, b, dims=((1,), (0,)), precision=None):
    return lax.dot_general(a, b, (dims, ((), ())), precision=precision, preferred_element_type=f32)


def split3(x):
    hi = x.astype(bf16).astype(f32)
    mid = (x - hi).astype(bf16).astype(f32)
    low = (x - hi - mid).astype(bf16).astype(f32)
    return hi, mid, low


def stats_tile(peak, total):
    lane = iota(peak.shape[:-1] + (128,), len(peak.shape) - 1)
    tile = jnp.zeros(peak.shape[:-1] + (128,), f32)
    for place, part in enumerate(split3(peak) + split3(total)):
        tile = jnp.where(lane == place, part, tile)
    return tile


def read_stats(x):
    tile = x[..., LAT:WIDE]
    lane = iota(tile.shape, len(tile.shape) - 1)
    peak = jnp.sum(jnp.where(lane < 3, tile, 0.0), axis=-1, keepdims=True)
    total = jnp.sum(jnp.where((lane >= 3) & (lane < 6), tile, 0.0), axis=-1, keepdims=True)
    return peak, total


def pack(x):
    n = x.shape[0]
    half = (n // 2 + 7) // 8 * 8
    ends = jnp.concatenate([x[:half, 384:], x[n - half :, 384:]], axis=1)
    return jnp.concatenate([x[:, :128], x[:, 128:256], x[:, 256:384], ends], axis=0)


def unpack(x, n):
    half = x.shape[0] - 3 * n
    ends = jnp.concatenate([x[3 * n :, :64], x[3 * n + 2 * half - n :, 64:]], axis=0)
    return jnp.concatenate([x[:n], x[n : 2 * n], x[2 * n : 3 * n], ends], axis=1)


def packed_lines(n):
    return 3 * n + (n // 2 + 7) // 8 * 8


def chosen_mask(ctx, picked, tokens):
    rows = picked.shape[0]
    per = tokens // BLOCK
    block_of = iota((rows, tokens), 1) // BLOCK
    mask = jnp.zeros((rows, tokens), f32)
    for b in range(per):
        hit = jnp.max(jnp.where(picked == ctx * per + b, 1.0, 0.0), axis=1, keepdims=True)
        mask = jnp.where(block_of == b, hit, mask)
    return mask


def scores_of(query, keys):
    return dot(query, keys, ((0,), (0,))) * SCORE_SCALE


def partial_row(core, scores, keys, chosen):
    masked = jnp.where(chosen, scores, NEG)
    peak = jnp.max(masked, axis=1, keepdims=True)
    expo = jnp.where(chosen, jnp.exp(masked - peak), 0.0)
    total = jnp.sum(expo, axis=1, keepdims=True)
    weighted = dot(expo.astype(bf16), keys[:LAT], ((1,), (1,)))
    wide = jnp.concatenate([weighted, stats_tile(peak, total)], axis=1).reshape(8, 2, 8, WIDE)
    return jnp.where(core == 0, wide[:, 0], wide[:, 1]), jnp.where(core == 0, wide[:, 1], wide[:, 0])


def store_pair(i, even, odd, mine_ref, other_ref):
    lines = slice(8 * i - 8, 8 * i + 8)
    mine_ref[:, lines, :] = jnp.concatenate([even[0], odd[0]], axis=1)
    other_ref[:, lines, :] = jnp.concatenate([even[1], odd[1]], axis=1).astype(bf16)


def attention_kernel(
    ctx_ref, blocks_hbm, query_hbm, cache_hbm, mine_ref, other_ref, blocks_ref, query_rest, cache_rest,
    query_ref, cache_ref, sems, sem,
):
    here, _, tokens = cache_ref.shape
    rows = cache_hbm.shape[0]
    load_blocks = pltpu.make_async_copy(blocks_hbm, blocks_ref, sem)
    copies = []
    for r in range(rows):
        query_to = query_ref.at[r] if r < here else query_rest.at[r - here]
        cache_to = cache_ref.at[r] if r < here else cache_rest.at[r - here]
        copies.append(
            (
                pltpu.make_async_copy(query_hbm.at[r], query_to, sems.at[0, r]),
                pltpu.make_async_copy(cache_hbm.at[r], cache_to, sems.at[1, r]),
            )
        )

    def start(r):
        for copy in copies[r]:
            copy.start()

    def ready(r):
        for copy in copies[r]:
            copy.wait()
        if r + 3 < rows:
            start(r + 3)

    start(0)
    load_blocks.start()
    start(1)
    start(2)
    ctx = ctx_ref[0]
    core = lax.rem(ctx, 2)
    ready(0)
    scores = scores_of(query_ref[0], cache_ref[0])
    load_blocks.wait()
    mask = chosen_mask(ctx, blocks_ref[...], tokens)
    even = None
    for i in range(here):
        later = None
        if i + 1 < here:
            ready(i + 1)
            later = scores_of(query_ref[i + 1], cache_ref[i + 1])
        row = partial_row(core, scores, cache_ref[i], mask[i : i + 1, :] > 0.0)
        if i % 2 == 0:
            even = row
        else:
            store_pair(i, even, row, mine_ref, other_ref)
        scores = later
    for r in range(here, rows):
        ready(r)


def rest_kernel(ctx_ref, blocks_ref, query_ref, cache_ref, mine_ref, other_ref):
    count, _, tokens = cache_ref.shape
    ctx = ctx_ref[0]
    core = lax.rem(ctx, 2)
    rows = blocks_ref.shape[0]
    mask = chosen_mask(ctx, blocks_ref[...], tokens)
    scores = [scores_of(query_ref[i], cache_ref[i]) for i in range(count)]
    even = None
    for i in range(count):
        at = rows - count + i
        row = partial_row(core, scores[i], cache_ref[i], mask[at : at + 1, :] > 0.0)
        if i % 2 == 0:
            even = row
        else:
            store_pair(i, even, row, mine_ref, other_ref)


def halves_out(rows):
    return [
        jax.ShapeDtypeStruct((8, rows * 8, WIDE), f32),
        jax.ShapeDtypeStruct((8, rows * 8, WIDE), bf16),
    ]


def attention(ctx, blocks, query, cache):
    rows = query.shape[0]
    here, rest = rows - 2, 2
    return pl.pallas_call(
        attention_kernel,
        in_specs=[SMEM, HBM, HBM, HBM],
        out_specs=[VMEM] * 5,
        out_shape=halves_out(here)
        + [
            jax.ShapeDtypeStruct(blocks.shape, jnp.int32),
            jax.ShapeDtypeStruct((rest,) + query.shape[1:], bf16),
            jax.ShapeDtypeStruct((rest,) + cache.shape[1:], bf16),
        ],
        scratch_shapes=[
            pltpu.VMEM((here,) + query.shape[1:], bf16),
            pltpu.VMEM((here,) + cache.shape[1:], bf16),
            pltpu.SemaphoreType.DMA((2, rows)),
            pltpu.SemaphoreType.DMA,
        ],
        compiler_params=params(16),
        name="attention",
    )(ctx, in_hbm(blocks), in_hbm(query), in_hbm(cache))


def attention_rest(ctx, blocks, query, cache):
    return pl.pallas_call(
        rest_kernel,
        in_specs=[SMEM] + [VMEM] * 3,
        out_specs=[VMEM] * 2,
        out_shape=halves_out(query.shape[0]),
        compiler_params=params(),
        name="attention_rest",
    )(ctx, blocks, query, cache)


def side_kernel(
    ctx_ref, route_ref, gate_ref, iq_ref, iw_ref, keys_ref, _,
    score_ref, send_ref, pick_ref, back_ref, slot_ref,
):
    scores = []
    for r in range(iq_ref.shape[0]):
        raw = dot(iq_ref[r], keys_ref[r], ((1,), (1,))) * (iq_ref.shape[2] ** (-0.5))
        scores.append(dot(iw_ref[r : r + 1, :], jnp.maximum(raw, 0.0), precision=HIGH))
    score_ref[...] = jnp.concatenate(scores, axis=0)
    n = route_ref.shape[1]
    ctx = ctx_ref[0]
    n_ctx = n // 6
    names = route_ref[...]
    experts = [ctx, lax.rem(ctx + n_ctx - UP, n_ctx), lax.rem(ctx + DOWN, n_ctx)]
    hit = [jnp.max(jnp.where(names == g, 1.0, 0.0), axis=0, keepdims=True) for g in experts]
    upto = jnp.where(iota((n, n), 0) <= iota((n, n), 1), 1.0, 0.0).astype(bf16)
    hits = jnp.concatenate(hit + [jnp.zeros((8 - len(hit), n), f32)], axis=0)
    slots = dot(hits.astype(bf16), upto).astype(jnp.int32) - 1
    line, col = iota((8, n), 0), iota((8, n), 1)
    picks = []
    for j, g in enumerate(experts):
        picks.append(jnp.where((iota((CAP, n), 0) == slots[j : j + 1]) & (hit[j] > 0.0), 1.0, 0.0))
        own = jnp.where((col == 6 * g + line) & (line < 6), 1.0, 0.0)
        both = jnp.concatenate([picks[j], own], axis=0).astype(bf16)
        if j == 0:
            pick_ref[...] = both
        else:
            send_ref[j - 1] = both
    gate = jnp.sum(jnp.where(names == ctx, gate_ref[...], 0.0), axis=0, keepdims=True)
    row, col = iota((128, n), 0), iota((128, n), 1)
    spread = (row // 8 * 6 + row % 8 == col) & (row % 8 < 6)
    spread = jnp.where(spread, 1.0, 0.0).astype(bf16)
    back_ref[...] = dot(spread, picks[0].astype(bf16), ((1,), (1,))).astype(bf16)
    slot_ref[...] = jnp.broadcast_to(jnp.sum(picks[0] * gate, axis=1, keepdims=True), (CAP, 128))


def side(ctx, route, gate, iq, iw, keys, after):
    n = route.shape[1]
    return pl.pallas_call(
        side_kernel,
        in_specs=[SMEM] + [VMEM] * 5 + [ANY],
        out_specs=[VMEM] * 5,
        out_shape=[
            jax.ShapeDtypeStruct((iq.shape[0], keys.shape[1]), f32),
            jax.ShapeDtypeStruct((2, CAP + 8, n), bf16),
            jax.ShapeDtypeStruct((CAP + 8, n), bf16),
            jax.ShapeDtypeStruct((128, CAP), bf16),
            jax.ShapeDtypeStruct((CAP, 128), f32),
        ],
        compiler_params=params(),
        name="side",
    )(ctx, route, gate, iq, iw, keys, after)


def merge(parts):
    stats = [read_stats(x) for x in parts]
    peak = functools.reduce(jnp.maximum, [p for p, _ in stats])
    factors = [jnp.exp(p - peak) for p, _ in stats]
    total = sum(t * f for (_, t), f in zip(stats, factors))
    return peak, total, sum(x[:, :LAT] * f for x, f in zip(parts, factors))


def widen(peak, total, summed):
    return jnp.concatenate([summed, stats_tile(peak, total)], axis=1)


def first_eight():
    return jnp.where(iota((8, 128), 0) == iota((8, 128), 1), 1.0, 0.0)


def to_lines(peak, total, summed):
    stats = dot(first_eight(), stats_tile(peak, total), ((1,), (1,)))
    stats = jnp.concatenate([stats, jnp.zeros((8, 128 - stats.shape[1]), f32)], axis=1)
    return jnp.concatenate([summed[:, at : at + 128] for at in range(0, LAT, 128)] + [stats], axis=0)


def from_lines(x):
    x = x.astype(f32)
    rows = (x.shape[0] - 8) // 4
    stats = dot(x[4 * rows :], first_eight(), ((0,), (0,)))[:rows]
    return jnp.concatenate([x[k * rows : (k + 1) * rows] for k in range(4)] + [stats], axis=1)


def pair_kernel(offsets, ctx_ref, mine_ref, other_ref, mine_rest, other_rest, *out_refs):
    n = mine_ref.shape[0]
    z = ctx_ref[0] // 2
    for ref, group in zip(out_refs[-len(offsets) :], offsets):
        for i, offset in enumerate(group):
            there = lax.rem(z + offset, n)
            mine = jnp.concatenate([mine_ref[there], mine_rest[there]], axis=0)
            other = jnp.concatenate([other_ref[there].astype(f32), other_rest[there].astype(f32)], axis=0)
            shape = widen if ref.shape[2] == WIDE else to_lines
            ref[i] = shape(*merge([mine, other])).astype(ref.dtype)


def pair(ctx, parts, offsets, kind, after=()):
    rows = parts[0].shape[1] + parts[2].shape[1]
    shape = (rows, WIDE) if kind == f32 else (4 * rows + 8, 128)
    return pl.pallas_call(
        functools.partial(pair_kernel, offsets),
        in_specs=[SMEM] + [VMEM] * 4 + [ANY] * len(after),
        out_specs=[VMEM] * len(offsets),
        out_shape=[jax.ShapeDtypeStruct((len(group),) + shape, kind) for group in offsets],
        compiler_params=params(),
        name="pair",
    )(ctx, *parts, *after)


def relay_kernel(keep_ref, below_ref, above_ref, up_ref, down_ref):
    down = merge([keep_ref[1], from_lines(below_ref[1]), from_lines(above_ref[1])])
    down_ref[...] = to_lines(*down).astype(bf16)
    up_ref[...] = to_lines(*merge([keep_ref[2], from_lines(below_ref[2])])).astype(bf16)


def relay(keep, below, above):
    return pl.pallas_call(
        relay_kernel,
        in_specs=[VMEM] * 3,
        out_specs=[VMEM] * 2,
        out_shape=[jax.ShapeDtypeStruct(below.shape[1:], bf16)] * 2,
        compiler_params=params(),
        name="relay",
    )(keep, below, above)


def values_kernel(keep_ref, below_ref, above_ref, far_below_ref, far_above_ref, w_ref, _, out_ref):
    parts = [below_ref[0], above_ref[0], far_below_ref[...], far_above_ref[...]]
    _, total, summed = merge([keep_ref[0]] + [from_lines(x) for x in parts])
    lat = (summed / total).astype(bf16)
    rows = lat.shape[0]
    row, col = iota((64, rows), 0), iota((64, rows), 1)
    by_head = jnp.where((row % 8) * 8 + row // 8 == col, 1.0, 0.0).astype(bf16)
    lat = dot(by_head, lat)
    out = [dot(lat[8 * h : 8 * h + 8].astype(bf16), w_ref[h]) for h in range(8)]
    half = jnp.concatenate([jnp.concatenate(out[:4], axis=1), jnp.concatenate(out[4:], axis=1)], axis=0)
    half = half.astype(bf16)
    for e in range(out_ref.shape[0]):
        out_ref[e] = half


def values(parts, w_uv, after, n_exp):
    return pl.pallas_call(
        values_kernel,
        in_specs=[VMEM] * (len(parts) + 1) + [ANY],
        out_specs=VMEM,
        out_shape=jax.ShapeDtypeStruct((n_exp, 16, 512), bf16),
        compiler_params=params(),
        name="values",
    )(*parts, w_uv, after)


def project_kernel(values_ref, w_ref, out_ref, acc_ref):
    x = values_ref[...].astype(f32)
    n = x.shape[0]
    low = x[:, :8].reshape(n * 8, 512).astype(bf16)
    high = x[:, 8:].reshape(n * 8, 512).astype(bf16)
    acc = dot(low, w_ref[:, :512], ((1,), (1,))) + dot(high, w_ref[:, 512:], ((1,), (1,)))
    for e in range(n):
        acc_ref[6 * e : 6 * e + 6, :] = acc[8 * e : 8 * e + 6, :]
    out_ref[...] = pack(acc_ref[: 6 * n, :]).astype(bf16)


def project(vals, w_o):
    shape = (vals.shape[0] * 6, w_o.shape[0])
    return pl.pallas_call(
        project_kernel,
        in_specs=[VMEM] * 2,
        out_specs=VMEM,
        out_shape=jax.ShapeDtypeStruct((packed_lines(shape[0]), 128), bf16),
        scratch_shapes=[pltpu.VMEM((shape[0] + 8, shape[1]), f32)],
        compiler_params=params(),
        name="project",
    )(vals, w_o)


def fold_kernel(own_ref, above_ref, below_ref, send_ref, up_ref, down_ref):
    n = send_ref.shape[2]
    two = own_ref[...].astype(f32) + below_ref[...].astype(f32)
    three = two + above_ref[...].astype(f32)
    up_ref[...] = pack(dot(send_ref[0], unpack(three, n).astype(bf16))).astype(bf16)
    down_ref[...] = pack(dot(send_ref[1], unpack(two, n).astype(bf16))).astype(bf16)


def fold(own, above, below, send):
    shape = jax.ShapeDtypeStruct((packed_lines(send.shape[1]), 128), bf16)
    return pl.pallas_call(
        fold_kernel,
        in_specs=[VMEM] * 4,
        out_specs=[VMEM] * 2,
        out_shape=[shape, shape],
        compiler_params=params(),
        name="fold",
    )(own, above, below, send)


def base_kernel(own_ref, above_ref, below_ref, hidden_ref, pick_ref, w_hbm, out_ref, w_ref, sem):
    load = pltpu.make_async_copy(w_hbm, w_ref, sem)
    load.start()
    pick = pick_ref[...]
    n = pick.shape[1]
    near = sum(
        dot(pick, unpack(ref[...].astype(f32), n).astype(bf16)) for ref in (own_ref, above_ref, below_ref)
    )
    out_ref[...] = dot(pick, hidden_ref[...]) + near
    load.wait()


def base(own, above, below, hidden, pick, w_in):
    return pl.pallas_call(
        base_kernel,
        in_specs=[VMEM] * 5 + [HBM],
        out_specs=[VMEM] * 2,
        out_shape=[
            jax.ShapeDtypeStruct((pick.shape[0], hidden.shape[1]), f32),
            jax.ShapeDtypeStruct(w_in.shape, bf16),
        ],
        scratch_shapes=[pltpu.SemaphoreType.DMA],
        compiler_params=params(),
        name="base",
    )(own, above, below, hidden, pick, in_hbm(w_in))


def expert_in_kernel(near_ref, far_up_ref, far_down_ref, gain_ref, w_ref, out_ref, keep_ref):
    n = out_ref.shape[0]
    half = w_ref.shape[1] // 2
    far = far_up_ref[...].astype(f32) + far_down_ref[...].astype(f32)
    attn = near_ref[...] + unpack(far, near_ref.shape[0])
    resid32 = attn.astype(bf16).astype(f32)
    keep_ref[...] = resid32[CAP:]
    picked = resid32[:CAP]
    rows = (picked * gain_ref[...]).astype(bf16)
    squares = dot(jnp.ones((8, picked.shape[1]), f32), picked * picked, ((1,), (1,)), HIGH)
    hi, mid, low = split3(squares)
    line = iota(squares.shape, 0)
    parts = jnp.where(line == 0, hi, jnp.where(line == 1, mid, jnp.where(line == 2, low, 0.0)))
    parts = jnp.concatenate([parts, jnp.zeros((8, 256 - CAP), f32)], axis=1)
    for e in range(0, n, 2):
        gate = dot(rows, w_ref[:, 128 * e : 128 * e + 256])
        up = dot(rows, w_ref[:, half + 128 * e : half + 128 * e + 256])
        for i in range(2):
            here = slice(128 * i, 128 * i + 128)
            both = jnp.concatenate([gate[:, here], up[:, here]], axis=1)
            out_ref[e + i] = jnp.concatenate([both, parts], axis=0).astype(bf16)


def expert_in(near, far_up, far_down, gain, w_in, n_exp):
    width = near.shape[1]
    return pl.pallas_call(
        expert_in_kernel,
        in_specs=[VMEM] * 5,
        out_specs=[VMEM] * 2,
        out_shape=[
            jax.ShapeDtypeStruct((n_exp, CAP + 8, 256), bf16),
            jax.ShapeDtypeStruct((8, width), f32),
        ],
        compiler_params=params(),
        name="expert_in",
    )(near, far_up, far_down, gain, w_in)


def act_kernel(parts_ref, out_ref):
    x = jnp.sum(parts_ref[...].astype(f32), axis=0)
    line = x[CAP : CAP + 1, :CAP] + x[CAP + 1 : CAP + 2, :CAP] + x[CAP + 2 : CAP + 3, :CAP]
    diagonal = iota((CAP, CAP), 0) == iota((CAP, CAP), 1)
    squares = jnp.sum(jnp.where(diagonal, line, 0.0), axis=1, keepdims=True)
    inv = lax.rsqrt(squares / D + EPS)
    gate, up = x[:CAP, :128] * inv, x[:CAP, 128:] * inv
    act = (jax.nn.silu(gate) * up).astype(bf16)
    for e in range(out_ref.shape[0]):
        out_ref[e] = act


def activation(parts):
    return pl.pallas_call(
        act_kernel,
        in_specs=[VMEM],
        out_specs=VMEM,
        out_shape=jax.ShapeDtypeStruct((parts.shape[0], CAP, 128), bf16),
        compiler_params=params(),
        name="activation",
    )(parts)


def expert_out_kernel(act_ref, w_ref, slot_ref, back_ref, out_ref):
    act = jnp.concatenate([act_ref[e] for e in range(act_ref.shape[0])], axis=1)
    out = (dot(act, w_ref[...], ((1,), (1,))) * slot_ref[:, 0:1]).astype(bf16)
    back = dot(back_ref[...], out)
    n = out_ref.shape[0]
    low = back[:, :256].reshape(n, 8, 256)
    high = jnp.concatenate([back[:, 256:], jnp.zeros((n * 8, 64), f32)], axis=1).reshape(n, 8, 256)
    out_ref[...] = jnp.concatenate([low, high], axis=1).astype(bf16)


def expert_out(act, w_down, slot, back, n_ctx):
    return pl.pallas_call(
        expert_out_kernel,
        in_specs=[VMEM] * 4,
        out_specs=VMEM,
        out_shape=jax.ShapeDtypeStruct((n_ctx, 16, 256), bf16),
        compiler_params=params(),
        name="expert_out",
    )(act, w_down, slot, back)


def last_kernel(parts_ref, keep_ref, out_ref):
    x = jnp.sum(parts_ref[...].astype(f32), axis=0)
    moe = jnp.concatenate([x[:8], x[8:, :192]], axis=1)
    out_ref[...] = (keep_ref[...] + moe)[:6].astype(bf16)


def last(parts, keep):
    return pl.pallas_call(
        last_kernel,
        in_specs=[VMEM] * 2,
        out_specs=VMEM,
        out_shape=jax.ShapeDtypeStruct((6, keep.shape[1]), bf16),
        compiler_params=params(),
        name="last",
    )(parts, keep)


def local(
    cache, idx_keys, lat_query, idx_query, idx_weight, chosen_blocks, w_uv, w_o, hidden_in, norm_gain,
    route, route_weight, w_in, w_down,
):
    n_ctx, n_exp = lax.axis_size("ctx"), lax.axis_size("exp")
    ctx = lax.axis_index("ctx").astype(jnp.int32).reshape(1)
    other_core = [(i, i ^ 1) for i in range(n_ctx)]
    def along_z(shift):
        return [(i, (i + shift) % n_ctx) for i in range(n_ctx)]

    mine, other, blocks, query, cache = attention(
        ctx, chosen_blocks, jnp.swapaxes(lat_query, 1, 2), jnp.swapaxes(cache, 1, 2)
    )
    mine_rest, other_rest = attention_rest(ctx, blocks, query, cache)
    other = lax.ppermute(other, "ctx", other_core)
    other_rest = lax.ppermute(other_rest, "ctx", other_core)
    parts = (mine, other, mine_rest, other_rest)
    up, down = pair(ctx, parts, ((1, 6, 3), (7, 4)), bf16)
    (keep,) = pair(ctx, parts, ((0, 5, 2),), f32, (down,))
    below = lax.ppermute(up, "ctx", along_z(2))
    above = lax.ppermute(down, "ctx", along_z(-2))
    up, down = relay(keep, below, above)
    far_below = lax.ppermute(up, "ctx", along_z(DOWN))
    far_above = lax.ppermute(down, "ctx", along_z(-UP))
    index_scores, send, pick, back, slot = side(
        ctx, route.T, route_weight.T, idx_query, idx_weight, idx_keys, up
    )
    vals = values((keep, below, above, far_below, far_above), w_uv, send, n_exp)
    vals = lax.all_to_all(vals, "exp", 0, 0)
    part = project(vals, w_o.T)
    own = part.astype(f32) + lax.ppermute(part, "ctx", other_core).astype(f32)
    own = own.astype(bf16)
    above = lax.ppermute(own, "ctx", along_z(-2))
    below = lax.ppermute(own, "ctx", along_z(2))
    up, down = fold(own, above, below, send)
    far_up = lax.ppermute(up, "ctx", along_z(-UP))
    far_down = lax.ppermute(down, "ctx", along_z(DOWN))
    near, w_gate_up = base(own, above, below, hidden_in, pick, w_in[0])
    terms, keep = expert_in(near, far_up, far_down, norm_gain.reshape(1, -1), w_gate_up, n_exp)
    terms = lax.all_to_all(terms, "exp", 0, 0)
    act = lax.all_to_all(activation(terms), "exp", 0, 0)
    outs = expert_out(act, w_down[0].T, slot, back, n_ctx)
    outs = lax.all_to_all(outs, "ctx", 0, 0)
    return index_scores, last(outs, keep)


def solution(mesh):
    return jax.shard_map(
        local,
        mesh=mesh,
        in_specs=(
            P("exp", "ctx", None),
            P("exp", "ctx", None),
            P("exp", None, None),
            P("exp", None, None),
            P("exp", None),
            P("exp", None),
            P("ctx", None, None),
            P("ctx", "exp"),
            P(None, "exp"),
            P("exp"),
            P(),
            P(),
            P("ctx", "exp", None),
            P("ctx", None, "exp"),
        ),
        out_specs=(P("exp", "ctx"), P("ctx", "exp")),
        check_vma=False,
    )
```

```python
import functools

import jax
import jax.numpy as jnp
from jax import lax
from jax.experimental import pallas as pl
from jax.experimental.pallas import tpu as pltpu
from jax.sharding import PartitionSpec as P

f32 = jnp.float32
bf16 = jnp.bfloat16
D = 7168
BLOCK = 64
LAT = 512
WIDE = 640
CAP = 48
UP, DOWN = 6, 4
NEG = -1e30
SCORE_SCALE = 192.0 ** (-0.5)
EPS = 1e-06
HIGH = lax.Precision.HIGHEST
MB = 1 << 20

VMEM = pl.BlockSpec(memory_space=pltpu.VMEM)
SMEM = pl.BlockSpec(memory_space=pltpu.SMEM)
HBM = pl.BlockSpec(memory_space=pltpu.HBM)
ANY = pl.BlockSpec(memory_space=pl.ANY)


def in_hbm(x):
    return pltpu.with_memory_space_constraint(x, pltpu.HBM)


def params(mb=8):
    return pltpu.CompilerParams(vmem_limit_bytes=mb * MB)


def iota(shape, dim):
    return lax.broadcasted_iota(jnp.int32, shape, dim)


def dot(a, b, dims=((1,), (0,)), precision=None):
    return lax.dot_general(a, b, (dims, ((), ())), precision=precision, preferred_element_type=f32)


def split3(x):
    hi = x.astype(bf16).astype(f32)
    mid = (x - hi).astype(bf16).astype(f32)
    low = (x - hi - mid).astype(bf16).astype(f32)
    return hi, mid, low


def stats_tile(peak, total):
    lane = iota(peak.shape[:-1] + (128,), len(peak.shape) - 1)
    tile = jnp.zeros(peak.shape[:-1] + (128,), f32)
    for place, part in enumerate(split3(peak) + split3(total)):
        tile = jnp.where(lane == place, part, tile)
    return tile


def read_stats(x):
    tile = x[..., LAT:WIDE]
    lane = iota(tile.shape, len(tile.shape) - 1)
    peak = jnp.sum(jnp.where(lane < 3, tile, 0.0), axis=-1, keepdims=True)
    total = jnp.sum(jnp.where((lane >= 3) & (lane < 6), tile, 0.0), axis=-1, keepdims=True)
    return peak, total


def pack(x):
    n = x.shape[0]
    half = (n // 2 + 7) // 8 * 8
    ends = jnp.concatenate([x[:half, 384:], x[n - half :, 384:]], axis=1)
    return jnp.concatenate([x[:, :128], x[:, 128:256], x[:, 256:384], ends], axis=0)


def unpack(x, n):
    half = x.shape[0] - 3 * n
    ends = jnp.concatenate([x[3 * n :, :64], x[3 * n + 2 * half - n :, 64:]], axis=0)
    return jnp.concatenate([x[:n], x[n : 2 * n], x[2 * n : 3 * n], ends], axis=1)


def packed_lines(n):
    return 3 * n + (n // 2 + 7) // 8 * 8


def chosen_mask(ctx, picked, tokens):
    rows = picked.shape[0]
    per = tokens // BLOCK
    block_of = iota((rows, tokens), 1) // BLOCK
    mask = jnp.zeros((rows, tokens), f32)
    for b in range(per):
        hit = jnp.max(jnp.where(picked == ctx * per + b, 1.0, 0.0), axis=1, keepdims=True)
        mask = jnp.where(block_of == b, hit, mask)
    return mask


def scores_of(query, keys):
    return dot(query, keys, ((0,), (0,))) * SCORE_SCALE


def partial_row(core, scores, keys, chosen):
    masked = jnp.where(chosen, scores, NEG)
    peak = jnp.max(masked, axis=1, keepdims=True)
    expo = jnp.where(chosen, jnp.exp(masked - peak), 0.0)
    total = jnp.sum(expo, axis=1, keepdims=True)
    weighted = dot(expo.astype(bf16), keys[:LAT], ((1,), (1,)))
    wide = jnp.concatenate([weighted, stats_tile(peak, total)], axis=1).reshape(8, 2, 8, WIDE)
    return jnp.where(core == 0, wide[:, 0], wide[:, 1]), jnp.where(core == 0, wide[:, 1], wide[:, 0])


def store_pair(i, even, odd, mine_ref, other_ref):
    lines = slice(8 * i - 8, 8 * i + 8)
    mine_ref[:, lines, :] = jnp.concatenate([even[0], odd[0]], axis=1)
    other_ref[:, lines, :] = jnp.concatenate([even[1], odd[1]], axis=1).astype(bf16)


def attention_kernel(
    ctx_ref, blocks_hbm, query_hbm, cache_hbm, mine_ref, other_ref, blocks_ref, query_rest, cache_rest,
    query_ref, cache_ref, sems, sem,
):
    here, _, tokens = cache_ref.shape
    rows = cache_hbm.shape[0]
    load_blocks = pltpu.make_async_copy(blocks_hbm, blocks_ref, sem)
    copies = []
    for r in range(rows):
        query_to = query_ref.at[r] if r < here else query_rest.at[r - here]
        cache_to = cache_ref.at[r] if r < here else cache_rest.at[r - here]
        copies.append(
            (
                pltpu.make_async_copy(query_hbm.at[r], query_to, sems.at[0, r]),
                pltpu.make_async_copy(cache_hbm.at[r], cache_to, sems.at[1, r]),
            )
        )

    def start(r):
        for copy in copies[r]:
            copy.start()

    def ready(r):
        for copy in copies[r]:
            copy.wait()
        if r + 3 < rows:
            start(r + 3)

    start(0)
    load_blocks.start()
    start(1)
    start(2)
    ctx = ctx_ref[0]
    core = lax.rem(ctx, 2)
    ready(0)
    scores = scores_of(query_ref[0], cache_ref[0])
    load_blocks.wait()
    mask = chosen_mask(ctx, blocks_ref[...], tokens)
    even = None
    for i in range(here):
        later = None
        if i + 1 < here:
            ready(i + 1)
            later = scores_of(query_ref[i + 1], cache_ref[i + 1])
        row = partial_row(core, scores, cache_ref[i], mask[i : i + 1, :] > 0.0)
        if i % 2 == 0:
            even = row
        else:
            store_pair(i, even, row, mine_ref, other_ref)
        scores = later
    for r in range(here, rows):
        ready(r)


def rest_kernel(ctx_ref, blocks_ref, query_ref, cache_ref, mine_ref, other_ref):
    count, _, tokens = cache_ref.shape
    ctx = ctx_ref[0]
    core = lax.rem(ctx, 2)
    rows = blocks_ref.shape[0]
    mask = chosen_mask(ctx, blocks_ref[...], tokens)
    scores = [scores_of(query_ref[i], cache_ref[i]) for i in range(count)]
    even = None
    for i in range(count):
        at = rows - count + i
        row = partial_row(core, scores[i], cache_ref[i], mask[at : at + 1, :] > 0.0)
        if i % 2 == 0:
            even = row
        else:
            store_pair(i, even, row, mine_ref, other_ref)


def halves_out(rows):
    return [
        jax.ShapeDtypeStruct((8, rows * 8, WIDE), f32),
        jax.ShapeDtypeStruct((8, rows * 8, WIDE), bf16),
    ]


def attention(ctx, blocks, query, cache):
    rows = query.shape[0]
    here, rest = rows - 2, 2
    return pl.pallas_call(
        attention_kernel,
        in_specs=[SMEM, HBM, HBM, HBM],
        out_specs=[VMEM] * 5,
        out_shape=halves_out(here)
        + [
            jax.ShapeDtypeStruct(blocks.shape, jnp.int32),
            jax.ShapeDtypeStruct((rest,) + query.shape[1:], bf16),
            jax.ShapeDtypeStruct((rest,) + cache.shape[1:], bf16),
        ],
        scratch_shapes=[
            pltpu.VMEM((here,) + query.shape[1:], bf16),
            pltpu.VMEM((here,) + cache.shape[1:], bf16),
            pltpu.SemaphoreType.DMA((2, rows)),
            pltpu.SemaphoreType.DMA,
        ],
        compiler_params=params(16),
        name="attention",
    )(ctx, in_hbm(blocks), in_hbm(query), in_hbm(cache))


def attention_rest(ctx, blocks, query, cache):
    return pl.pallas_call(
        rest_kernel,
        in_specs=[SMEM] + [VMEM] * 3,
        out_specs=[VMEM] * 2,
        out_shape=halves_out(query.shape[0]),
        compiler_params=params(),
        name="attention_rest",
    )(ctx, blocks, query, cache)


def side_kernel(
    ctx_ref, route_ref, gate_ref, iq_ref, iw_ref, keys_ref, _,
    score_ref, send_ref, pick_ref, back_ref, slot_ref,
):
    scores = []
    for r in range(iq_ref.shape[0]):
        raw = dot(iq_ref[r], keys_ref[r], ((1,), (1,))) * (iq_ref.shape[2] ** (-0.5))
        scores.append(dot(iw_ref[r : r + 1, :], jnp.maximum(raw, 0.0), precision=HIGH))
    score_ref[...] = jnp.concatenate(scores, axis=0)
    n = route_ref.shape[1]
    ctx = ctx_ref[0]
    n_ctx = n // 6
    names = route_ref[...]
    experts = [ctx, lax.rem(ctx + n_ctx - UP, n_ctx), lax.rem(ctx + DOWN, n_ctx)]
    hit = [jnp.max(jnp.where(names == g, 1.0, 0.0), axis=0, keepdims=True) for g in experts]
    upto = jnp.where(iota((n, n), 0) <= iota((n, n), 1), 1.0, 0.0).astype(bf16)
    hits = jnp.concatenate(hit + [jnp.zeros((8 - len(hit), n), f32)], axis=0)
    slots = dot(hits.astype(bf16), upto).astype(jnp.int32) - 1
    line, col = iota((8, n), 0), iota((8, n), 1)
    picks = []
    for j, g in enumerate(experts):
        picks.append(jnp.where((iota((CAP, n), 0) == slots[j : j + 1]) & (hit[j] > 0.0), 1.0, 0.0))
        own = jnp.where((col == 6 * g + line) & (line < 6), 1.0, 0.0)
        both = jnp.concatenate([picks[j], own], axis=0).astype(bf16)
        if j == 0:
            pick_ref[...] = both
        else:
            send_ref[j - 1] = both
    gate = jnp.sum(jnp.where(names == ctx, gate_ref[...], 0.0), axis=0, keepdims=True)
    row, col = iota((128, n), 0), iota((128, n), 1)
    spread = (row // 8 * 6 + row % 8 == col) & (row % 8 < 6)
    spread = jnp.where(spread, 1.0, 0.0).astype(bf16)
    back_ref[...] = dot(spread, picks[0].astype(bf16), ((1,), (1,))).astype(bf16)
    slot_ref[...] = jnp.broadcast_to(jnp.sum(picks[0] * gate, axis=1, keepdims=True), (CAP, 128))


def side(ctx, route, gate, iq, iw, keys, after):
    n = route.shape[1]
    return pl.pallas_call(
        side_kernel,
        in_specs=[SMEM] + [VMEM] * 5 + [ANY],
        out_specs=[VMEM] * 5,
        out_shape=[
            jax.ShapeDtypeStruct((iq.shape[0], keys.shape[1]), f32),
            jax.ShapeDtypeStruct((2, CAP + 8, n), bf16),
            jax.ShapeDtypeStruct((CAP + 8, n), bf16),
            jax.ShapeDtypeStruct((128, CAP), bf16),
            jax.ShapeDtypeStruct((CAP, 128), f32),
        ],
        compiler_params=params(),
        name="side",
    )(ctx, route, gate, iq, iw, keys, after)


def merge(parts):
    stats = [read_stats(x) for x in parts]
    peak = functools.reduce(jnp.maximum, [p for p, _ in stats])
    factors = [jnp.exp(p - peak) for p, _ in stats]
    total = sum(t * f for (_, t), f in zip(stats, factors))
    return peak, total, sum(x[:, :LAT] * f for x, f in zip(parts, factors))


def widen(peak, total, summed):
    return jnp.concatenate([summed, stats_tile(peak, total)], axis=1)


def first_eight():
    return jnp.where(iota((8, 128), 0) == iota((8, 128), 1), 1.0, 0.0)


def to_lines(peak, total, summed):
    stats = dot(first_eight(), stats_tile(peak, total), ((1,), (1,)))
    stats = jnp.concatenate([stats, jnp.zeros((8, 128 - stats.shape[1]), f32)], axis=1)
    return jnp.concatenate([summed[:, at : at + 128] for at in range(0, LAT, 128)] + [stats], axis=0)


def from_lines(x):
    x = x.astype(f32)
    rows = (x.shape[0] - 8) // 4
    stats = dot(x[4 * rows :], first_eight(), ((0,), (0,)))[:rows]
    return jnp.concatenate([x[k * rows : (k + 1) * rows] for k in range(4)] + [stats], axis=1)


def pair_kernel(offsets, ctx_ref, mine_ref, other_ref, mine_rest, other_rest, *out_refs):
    n = mine_ref.shape[0]
    z = ctx_ref[0] // 2
    for ref, group in zip(out_refs[-len(offsets) :], offsets):
        for i, offset in enumerate(group):
            there = lax.rem(z + offset, n)
            mine = jnp.concatenate([mine_ref[there], mine_rest[there]], axis=0)
            other = jnp.concatenate([other_ref[there].astype(f32), other_rest[there].astype(f32)], axis=0)
            shape = widen if ref.shape[2] == WIDE else to_lines
            ref[i] = shape(*merge([mine, other])).astype(ref.dtype)


def pair(ctx, parts, offsets, kind, after=()):
    rows = parts[0].shape[1] + parts[2].shape[1]
    shape = (rows, WIDE) if kind == f32 else (4 * rows + 8, 128)
    return pl.pallas_call(
        functools.partial(pair_kernel, offsets),
        in_specs=[SMEM] + [VMEM] * 4 + [ANY] * len(after),
        out_specs=[VMEM] * len(offsets),
        out_shape=[jax.ShapeDtypeStruct((len(group),) + shape, kind) for group in offsets],
        compiler_params=params(),
        name="pair",
    )(ctx, *parts, *after)


def relay_kernel(keep_ref, below_ref, above_ref, up_ref, down_ref):
    down = merge([keep_ref[1], from_lines(below_ref[1]), from_lines(above_ref[1])])
    down_ref[...] = to_lines(*down).astype(bf16)
    up_ref[...] = to_lines(*merge([keep_ref[2], from_lines(below_ref[2])])).astype(bf16)


def relay(keep, below, above):
    return pl.pallas_call(
        relay_kernel,
        in_specs=[VMEM] * 3,
        out_specs=[VMEM] * 2,
        out_shape=[jax.ShapeDtypeStruct(below.shape[1:], bf16)] * 2,
        compiler_params=params(),
        name="relay",
    )(keep, below, above)


def values_kernel(keep_ref, below_ref, above_ref, far_below_ref, far_above_ref, w_ref, _, out_ref):
    parts = [below_ref[0], above_ref[0], far_below_ref[...], far_above_ref[...]]
    _, total, summed = merge([keep_ref[0]] + [from_lines(x) for x in parts])
    lat = (summed / total).astype(bf16)
    rows = lat.shape[0]
    row, col = iota((64, rows), 0), iota((64, rows), 1)
    by_head = jnp.where((row % 8) * 8 + row // 8 == col, 1.0, 0.0).astype(bf16)
    lat = dot(by_head, lat)
    out = [dot(lat[8 * h : 8 * h + 8].astype(bf16), w_ref[h]) for h in range(8)]
    half = jnp.concatenate([jnp.concatenate(out[:4], axis=1), jnp.concatenate(out[4:], axis=1)], axis=0)
    half = half.astype(bf16)
    for e in range(out_ref.shape[0]):
        out_ref[e] = half


def values(parts, w_uv, after, n_exp):
    return pl.pallas_call(
        values_kernel,
        in_specs=[VMEM] * (len(parts) + 1) + [ANY],
        out_specs=VMEM,
        out_shape=jax.ShapeDtypeStruct((n_exp, 16, 512), bf16),
        compiler_params=params(),
        name="values",
    )(*parts, w_uv, after)


def project_kernel(values_ref, w_ref, out_ref, acc_ref):
    x = values_ref[...].astype(f32)
    n = x.shape[0]
    low = x[:, :8].reshape(n * 8, 512).astype(bf16)
    high = x[:, 8:].reshape(n * 8, 512).astype(bf16)
    acc = dot(low, w_ref[:, :512], ((1,), (1,))) + dot(high, w_ref[:, 512:], ((1,), (1,)))
    for e in range(n):
        acc_ref[6 * e : 6 * e + 6, :] = acc[8 * e : 8 * e + 6, :]
    out_ref[...] = pack(acc_ref[: 6 * n, :]).astype(bf16)


def project(vals, w_o):
    shape = (vals.shape[0] * 6, w_o.shape[0])
    return pl.pallas_call(
        project_kernel,
        in_specs=[VMEM] * 2,
        out_specs=VMEM,
        out_shape=jax.ShapeDtypeStruct((packed_lines(shape[0]), 128), bf16),
        scratch_shapes=[pltpu.VMEM((shape[0] + 8, shape[1]), f32)],
        compiler_params=params(),
        name="project",
    )(vals, w_o)


def fold_kernel(own_ref, above_ref, below_ref, send_ref, up_ref, down_ref):
    n = send_ref.shape[2]
    two = own_ref[...].astype(f32) + below_ref[...].astype(f32)
    three = two + above_ref[...].astype(f32)
    up_ref[...] = pack(dot(send_ref[0], unpack(three, n).astype(bf16))).astype(bf16)
    down_ref[...] = pack(dot(send_ref[1], unpack(two, n).astype(bf16))).astype(bf16)


def fold(own, above, below, send):
    shape = jax.ShapeDtypeStruct((packed_lines(send.shape[1]), 128), bf16)
    return pl.pallas_call(
        fold_kernel,
        in_specs=[VMEM] * 4,
        out_specs=[VMEM] * 2,
        out_shape=[shape, shape],
        compiler_params=params(),
        name="fold",
    )(own, above, below, send)


def base_kernel(own_ref, above_ref, below_ref, hidden_ref, pick_ref, w_hbm, out_ref, w_ref, sem):
    load = pltpu.make_async_copy(w_hbm, w_ref, sem)
    load.start()
    pick = pick_ref[...]
    n = pick.shape[1]
    near = sum(
        dot(pick, unpack(ref[...].astype(f32), n).astype(bf16)) for ref in (own_ref, above_ref, below_ref)
    )
    out_ref[...] = dot(pick, hidden_ref[...]) + near
    load.wait()


def base(own, above, below, hidden, pick, w_in):
    return pl.pallas_call(
        base_kernel,
        in_specs=[VMEM] * 5 + [HBM],
        out_specs=[VMEM] * 2,
        out_shape=[
            jax.ShapeDtypeStruct((pick.shape[0], hidden.shape[1]), f32),
            jax.ShapeDtypeStruct(w_in.shape, bf16),
        ],
        scratch_shapes=[pltpu.SemaphoreType.DMA],
        compiler_params=params(),
        name="base",
    )(own, above, below, hidden, pick, in_hbm(w_in))


def expert_in_kernel(near_ref, far_up_ref, far_down_ref, gain_ref, w_ref, out_ref, keep_ref):
    n = out_ref.shape[0]
    half = w_ref.shape[1] // 2
    far = far_up_ref[...].astype(f32) + far_down_ref[...].astype(f32)
    attn = near_ref[...] + unpack(far, near_ref.shape[0])
    resid32 = attn.astype(bf16).astype(f32)
    keep_ref[...] = resid32[CAP:]
    picked = resid32[:CAP]
    rows = (picked * gain_ref[...]).astype(bf16)
    squares = dot(jnp.ones((8, picked.shape[1]), f32), picked * picked, ((1,), (1,)), HIGH)
    hi, mid, low = split3(squares)
    line = iota(squares.shape, 0)
    parts = jnp.where(line == 0, hi, jnp.where(line == 1, mid, jnp.where(line == 2, low, 0.0)))
    parts = jnp.concatenate([parts, jnp.zeros((8, 128 - CAP), f32)], axis=1)
    for e in range(0, n, 2):
        gate = dot(rows, w_ref[:, 128 * e : 128 * e + 256])
        up = dot(rows, w_ref[:, half + 128 * e : half + 128 * e + 256])
        for i in range(2):
            here = slice(128 * i, 128 * i + 128)
            out_ref[e + i] = jnp.concatenate([gate[:, here], up[:, here], parts], axis=0).astype(bf16)


def expert_in(near, far_up, far_down, gain, w_in, n_exp):
    width = near.shape[1]
    return pl.pallas_call(
        expert_in_kernel,
        in_specs=[VMEM] * 5,
        out_specs=[VMEM] * 2,
        out_shape=[
            jax.ShapeDtypeStruct((n_exp, 2 * CAP + 8, 128), bf16),
            jax.ShapeDtypeStruct((8, width), f32),
        ],
        compiler_params=params(),
        name="expert_in",
    )(near, far_up, far_down, gain, w_in)


def act_kernel(parts_ref, out_ref):
    x = jnp.sum(parts_ref[...].astype(f32), axis=0)
    line = sum(x[2 * CAP + k : 2 * CAP + k + 1, :CAP] for k in range(3))
    diagonal = iota((CAP, CAP), 0) == iota((CAP, CAP), 1)
    squares = jnp.sum(jnp.where(diagonal, line, 0.0), axis=1, keepdims=True)
    inv = lax.rsqrt(squares / D + EPS)
    gate, up = x[:CAP] * inv, x[CAP : 2 * CAP] * inv
    act = (jax.nn.silu(gate) * up).astype(bf16)
    for e in range(out_ref.shape[0]):
        out_ref[e] = act


def activation(parts):
    return pl.pallas_call(
        act_kernel,
        in_specs=[VMEM],
        out_specs=VMEM,
        out_shape=jax.ShapeDtypeStruct((parts.shape[0], CAP, 128), bf16),
        compiler_params=params(),
        name="activation",
    )(parts)


def expert_out_kernel(act_ref, w_ref, slot_ref, back_ref, out_ref):
    act = jnp.concatenate([act_ref[e] for e in range(act_ref.shape[0])], axis=1)
    out = (dot(act, w_ref[...], ((1,), (1,))) * slot_ref[:, 0:1]).astype(bf16)
    back = dot(back_ref[...], out)
    n = out_ref.shape[0]
    low = back[:, :256].reshape(n, 8, 256)
    high = jnp.concatenate([back[:, 256:], jnp.zeros((n * 8, 64), f32)], axis=1).reshape(n, 8, 256)
    out_ref[...] = jnp.concatenate([low, high], axis=1).astype(bf16)


def expert_out(act, w_down, slot, back, n_ctx):
    return pl.pallas_call(
        expert_out_kernel,
        in_specs=[VMEM] * 4,
        out_specs=VMEM,
        out_shape=jax.ShapeDtypeStruct((n_ctx, 16, 256), bf16),
        compiler_params=params(),
        name="expert_out",
    )(act, w_down, slot, back)


def last_kernel(parts_ref, keep_ref, out_ref):
    x = jnp.sum(parts_ref[...].astype(f32), axis=0)
    moe = jnp.concatenate([x[:8], x[8:, :192]], axis=1)
    out_ref[...] = (keep_ref[...] + moe)[:6].astype(bf16)


def last(parts, keep):
    return pl.pallas_call(
        last_kernel,
        in_specs=[VMEM] * 2,
        out_specs=VMEM,
        out_shape=jax.ShapeDtypeStruct((6, keep.shape[1]), bf16),
        compiler_params=params(),
        name="last",
    )(parts, keep)


def local(
    cache, idx_keys, lat_query, idx_query, idx_weight, chosen_blocks, w_uv, w_o, hidden_in, norm_gain,
    route, route_weight, w_in, w_down,
):
    n_ctx, n_exp = lax.axis_size("ctx"), lax.axis_size("exp")
    ctx = lax.axis_index("ctx").astype(jnp.int32).reshape(1)
    other_core = [(i, i ^ 1) for i in range(n_ctx)]
    def along_z(shift):
        return [(i, (i + shift) % n_ctx) for i in range(n_ctx)]

    mine, other, blocks, query, cache = attention(
        ctx, chosen_blocks, jnp.swapaxes(lat_query, 1, 2), jnp.swapaxes(cache, 1, 2)
    )
    mine_rest, other_rest = attention_rest(ctx, blocks, query, cache)
    other = lax.ppermute(other, "ctx", other_core)
    other_rest = lax.ppermute(other_rest, "ctx", other_core)
    parts = (mine, other, mine_rest, other_rest)
    up, down = pair(ctx, parts, ((1, 6, 3), (7, 4)), bf16)
    (keep,) = pair(ctx, parts, ((0, 5, 2),), f32, (down,))
    below = lax.ppermute(up, "ctx", along_z(2))
    above = lax.ppermute(down, "ctx", along_z(-2))
    up, down = relay(keep, below, above)
    far_below = lax.ppermute(up, "ctx", along_z(DOWN))
    far_above = lax.ppermute(down, "ctx", along_z(-UP))
    index_scores, send, pick, back, slot = side(
        ctx, route.T, route_weight.T, idx_query, idx_weight, idx_keys, up
    )
    vals = values((keep, below, above, far_below, far_above), w_uv, send, n_exp)
    vals = lax.all_to_all(vals, "exp", 0, 0)
    part = project(vals, w_o.T)
    own = part.astype(f32) + lax.ppermute(part, "ctx", other_core).astype(f32)
    own = own.astype(bf16)
    above = lax.ppermute(own, "ctx", along_z(-2))
    below = lax.ppermute(own, "ctx", along_z(2))
    up, down = fold(own, above, below, send)
    far_up = lax.ppermute(up, "ctx", along_z(-UP))
    far_down = lax.ppermute(down, "ctx", along_z(DOWN))
    near, w_gate_up = base(own, above, below, hidden_in, pick, w_in[0])
    terms, keep = expert_in(near, far_up, far_down, norm_gain.reshape(1, -1), w_gate_up, n_exp)
    terms = lax.all_to_all(terms, "exp", 0, 0)
    act = lax.all_to_all(activation(terms), "exp", 0, 0)
    outs = expert_out(act, w_down[0].T, slot, back, n_ctx)
    outs = lax.all_to_all(outs, "ctx", 0, 0)
    return index_scores, last(outs, keep)


def solution(mesh):
    return jax.shard_map(
        local,
        mesh=mesh,
        in_specs=(
            P("exp", "ctx", None),
            P("exp", "ctx", None),
            P("exp", None, None),
            P("exp", None, None),
            P("exp", None),
            P("exp", None),
            P("ctx", None, None),
            P("ctx", "exp"),
            P(None, "exp"),
            P("exp"),
            P(),
            P(),
            P("ctx", "exp", None),
            P("ctx", None, "exp"),
        ),
        out_specs=(P("exp", "ctx"), P("ctx", "exp")),
        check_vma=False,
    )
```
